32 devices in a mesh: dp: 4 (over y, core), blk: 2 (over x), sp: 4 (over z).
Axes of the slice: x: 2, y: 2, z: 4, core: 2. Of those that a mesh axis runs over, the one named last changes fastest.
Arguments:
- clip_tokens: bfloat16 [4, 2048, 1536], P('dp', ('blk', 'sp')), may hold values from -6 to 6
- text_tokens: bfloat16 [4, 512, 1536], P('dp', ('blk', 'sp')), may hold values from -6 to 6
- text_lengths: int32 [4], P('dp'), may hold values from 64 to 512, as said below
- positions: int32 [4, 3, 2048], P('dp', None, ('blk', 'sp')), may hold values from 0 to 31
- time_embed: float32 [4, 6, 1536], P('dp'), may hold values from -4 to 4
- modulation: bfloat16 [6, 1536], P(None, ('blk', 'sp')), may hold values from -4 to 4
- gains: bfloat16 [5, 1536], P(None, ('blk', 'sp')), may hold values from 0.5 to 1.5
- biases: bfloat16 [10, 1536], P(None, ('blk', 'sp')), may hold values from -1.1953125 to 1.1953125
- self_qkv: bfloat16 [1536, 4608], P(('blk', 'sp')), may hold values from -0.15625 to 0.15625
- self_out: bfloat16 [1536, 1536], P(('blk', 'sp')), may hold values from -4 to 4
- cross_qkv: bfloat16 [1536, 4608], P(('blk', 'sp')), may hold values from -0.15625 to 0.15625
- cross_out: bfloat16 [1536, 1536], P(('blk', 'sp')), may hold values from -2 to 2
- ffn_in: bfloat16 [8960, 1536], P(('blk', 'sp')), may hold values from -0.15625 to 0.15625
- ffn_out: bfloat16 [8960, 1536], P(('blk', 'sp')), may hold values from -0.0625 to 0.0625
- ffn_bias: bfloat16 [8960], P(('blk', 'sp')), may hold values from -1.1953125 to 1.1953125
- cotangent: bfloat16 [4, 2048, 1536], P('dp', ('blk', 'sp')), may hold values from -6 to 6
Outputs:
- block_out: bfloat16 [4, 2048, 1536], P('dp', ('blk', 'sp'))
- grad_tokens: float32 [4, 2048, 1536], P('dp', ('blk', 'sp'))
- grad_text: float32 [4, 512, 1536], P('dp', ('blk', 'sp'))
- grad_modulation: float32 [6, 1536], P(None, ('blk', 'sp'))
- grad_gains: float32 [5, 1536], P(None, ('blk', 'sp'))
- grad_biases: float32 [10, 1536], P(None, ('blk', 'sp'))
- grad_self_qkv: float32 [1536, 4608], P(('blk', 'sp'))
- grad_self_out: float32 [1536, 1536], P(('blk', 'sp'))
- grad_cross_qkv: float32 [1536, 4608], P(('blk', 'sp'))
- grad_cross_out: float32 [1536, 1536], P(('blk', 'sp'))
- grad_ffn_in: float32 [8960, 1536], P(('blk', 'sp'))
- grad_ffn_out: float32 [8960, 1536], P(('blk', 'sp'))
- grad_ffn_bias: float32 [8960], P(('blk', 'sp'))
The draws below stay inside these ranges and needn't reach their ends.
Inputs may be any that keep to these rules, and one draw needn't show every extreme that they name: `text_lengths`: valid text tokens of each clip; in every draw some clip has all 512 and another has 64.
All inputs are finite; a program needn't handle non-finite values.
Results may differ from the reference program's by a relative error of at most 0.02.
Values may be sent and summed in bfloat16 or wider, within the bound.
A program may use at most 384 MiB of HBM per device.

```python
import jax
import jax.numpy as jnp
import numpy as np
from jax import lax

H = 12
HD = 128
FF = 8960
D = 1536
L = 2048
TEXT = 512
CLIPS = 4


def draw_text_lengths(key, part):
    key_len, key_full, key_short = jax.random.split(key, 3)
    lengths = jax.random.randint(key_len, (CLIPS,), TEXT // 8, TEXT + 1)
    full_at = jax.random.randint(key_full, (), 0, CLIPS)
    short_at = (full_at + jax.random.randint(key_short, (), 1, CLIPS)) % CLIPS
    places = jnp.arange(CLIPS)
    lengths = jnp.where(places == full_at, TEXT, lengths)
    lengths = jnp.where(places == short_at, TEXT // 8, lengths)
    return lengths.astype(jnp.int32)


def with_ends(entries, own_key, least, high):
    longest = entries.shape.index(max(entries.shape))
    spots = []
    for shift in (0, 1):
        where = [jax.random.randint(jax.random.fold_in(own_key, axis), (), 0, length) for axis, length in enumerate(entries.shape)]
        where[longest] = (where[longest] + shift) % entries.shape[longest]
        spots.append(tuple(where))
    return entries.at[spots[0]].set(least).at[spots[1]].set(high)


def levels(key, dims, pieces, low, high):
    loudness = 1.0
    for position, parts in pieces:
        draws = jax.random.uniform(jax.random.fold_in(jax.random.fold_in(key, 6), position), (parts,), jnp.float32, low / len(pieces), high / len(pieces))
        loudness = loudness * jnp.repeat(jnp.exp(draws), dims[position] // parts).reshape((-1,) + (1,) * (len(dims) - 1 - position))
    return loudness


def noise(stream_key, extent, spread, limit, shards=(), kind=jnp.bfloat16):
    values = jax.random.normal(stream_key, extent, jnp.float32) * spread
    if len(shards) > 0:
        values = levels(stream_key, extent, shards, -0.22, 0.18) * values
    return jnp.clip(values, min=-limit, max=limit).astype(kind)


def setup_inputs(seed: int = 0) -> dict:
    splits = jax.random.split(jax.random.key(seed), 17)
    return {
        "clip_tokens": noise(splits[0], (CLIPS, L, D), 1.0, 6.0, ((0, 4), (1, 8))),
        "text_tokens": noise(splits[1], (CLIPS, TEXT, D), 1.0, 6.0, ((0, 4), (1, 8))),
        "text_lengths": draw_text_lengths(jax.random.fold_in(splits[16], 71), 0),
        "positions": with_ends(jax.random.randint(splits[3], (CLIPS, 3, L), 0, 32), jax.random.fold_in(splits[3], 1), 0, 31).astype(jnp.int32),
        "time_embed": noise(splits[4], (CLIPS, 6, D), 0.5, 4.0, ((0, 4),), jnp.float32),
        "modulation": noise(splits[5], (6, D), 0.5, 4.0, ((1, 8),)),
        "gains": jnp.clip(1.0 + 0.1 * jax.random.normal(splits[6], (5, D), jnp.float32), 0.5, 1.5).astype(jnp.bfloat16),
        "biases": noise(splits[7], (10, D), 0.2, 1.1953125, ((1, 8),)),
        "self_qkv": noise(splits[8], (D, 3 * D), D ** -0.5, 0.15625, ((0, 8),)),
        "self_out": noise(splits[9], (D, D), (max(1, 3 * D // L)) ** -0.5, 4.0, ((0, 8),)),
        "cross_qkv": noise(splits[10], (D, 3 * D), D ** -0.5, 0.15625, ((0, 8),)),
        "cross_out": noise(splits[11], (D, D), (max(1, 3 * D // TEXT)) ** -0.5, 2.0, ((0, 8),)),
        "ffn_in": noise(splits[12], (FF, D), D ** -0.5, 0.15625, ((0, 8),)),
        "ffn_out": noise(splits[13], (FF, D), FF ** -0.5, 0.0625, ((0, 8),)),
        "ffn_bias": noise(splits[14], (FF,), 0.2, 1.1953125, ((0, 8),)),
        "cotangent": noise(splits[15], (CLIPS, L, D), 1.0, 6.0, ((0, 4), (1, 8))),
    }


EPS = 1e-06
NEG = -1e+30
HIGH = lax.Precision.HIGHEST

@jax.custom_vjp
def low(v):
    return lax.optimization_barrier(v.astype(jnp.bfloat16)).astype(jnp.float32)

@jax.custom_vjp
def low_back(v):
    return v

def low_keep(v):
    return (low(v), None)

def low_pass(kept, grad):
    return (grad,)

def back_keep(v):
    return (v, None)

def back_low(kept, grad):
    return (low(grad),)
low.defvjp(low_keep, low_pass)
low_back.defvjp(back_keep, back_low)

def layer_norm(values):
    centre = values - lax.optimization_barrier(jnp.mean(values, axis=-1, keepdims=True))
    return centre * lax.rsqrt(lax.optimization_barrier(jnp.mean(centre * centre, axis=-1, keepdims=True)) + EPS)

def rms_norm(values, gain_row):
    return values * lax.rsqrt(lax.optimization_barrier(jnp.mean(values * values, axis=-1, keepdims=True)) + EPS) * gain_row

def rope_tables(head_dim):
    pair_count = head_dim // 2
    side_count = head_dim // 6
    first_count = pair_count - 2 * side_count
    tables = np.zeros((3, pair_count))
    for column in range(pair_count):
        if column < first_count:
            tables[0, column] = 10000.0 ** (-column / first_count)
        elif column < first_count + side_count:
            tables[1, column] = 10000.0 ** (-(column - first_count) / side_count)
        else:
            tables[2, column] = 10000.0 ** (-(column - first_count - side_count) / side_count)
    return tables

def rope_angles(positions, head_dim):
    tables = jnp.asarray(rope_tables(head_dim), dtype=jnp.float32)
    places = positions.astype(jnp.float32)
    angles = places[0][:, None] * tables[0] + places[1][:, None] * tables[1] + places[2][:, None] * tables[2]
    cosine = jnp.cos(angles)
    sine_part = jnp.sin(angles)
    return (jnp.concatenate([cosine, cosine], -1), jnp.concatenate([sine_part, sine_part], -1))

def rotate(values, cosine, sine_part):
    half_dim = values.shape[-1] // 2
    turned = jnp.concatenate([-values[..., half_dim:], values[..., :half_dim]], -1)
    return values * cosine[:, None, :] + turned * sine_part[:, None, :]

def softmax_rows(scores):
    top_score = lax.optimization_barrier(jnp.max(scores, -1, keepdims=True))
    raised = jnp.exp(scores - top_score)
    return raised / lax.optimization_barrier(jnp.sum(raised, -1, keepdims=True))

def clip_forward(x_in, text_in, params, time_row, length, positions):
    mod_p, gain_p, bias_p, qkv_s, out_s, qkv_c, out_c, w_in, w_out, b_in = params
    seq_len = x_in.shape[0]
    text_len = text_in.shape[0]
    width = H * HD
    scale = HD ** (-0.5)
    block_rows = 512 if seq_len % 512 == 0 else seq_len
    mods = time_row + mod_p
    shifted = low(layer_norm(x_in) * (1.0 + mods[1]) + mods[0])
    proj = low_back(jnp.dot(shifted, qkv_s, precision=HIGH) + jnp.concatenate([bias_p[0], bias_p[1], bias_p[2]]))
    cosine, sine_part = rope_angles(positions, HD)
    q_rot = low(low_back(rotate(rms_norm(proj[:, :width], gain_p[0]).reshape(seq_len, H, HD), cosine, sine_part)))
    k_rot = low(low_back(rotate(rms_norm(proj[:, width:2 * width], gain_p[1]).reshape(seq_len, H, HD), cosine, sine_part)))
    v_heads = low(proj[:, 2 * width:].reshape(seq_len, H, HD))

    def self_block(q_block):
        scores = low_back(jnp.einsum('rhe,khe->hrk', q_block, k_rot, precision=HIGH) * scale)
        probs = low(softmax_rows(scores))
        return jnp.einsum('hrk,khe->rhe', probs, v_heads, precision=HIGH)
    attended = lax.map(jax.checkpoint(self_block), q_rot.reshape(seq_len // block_rows, block_rows, H, HD))
    attended = low(low_back(attended.reshape(seq_len, width)))
    a_lin = low_back(jnp.dot(attended, out_s, precision=HIGH) + bias_p[3])
    x_one = x_in + mods[2] * a_lin
    cross_in = low(layer_norm(x_one) * gain_p[2] + bias_p[8])
    qc_lin = low_back(jnp.dot(cross_in, qkv_c[:, :width], precision=HIGH) + bias_p[4])
    q_cross = low(rms_norm(qc_lin, gain_p[3])).reshape(seq_len, H, HD)
    kv_lin = low_back(jnp.dot(text_in, qkv_c[:, width:], precision=HIGH) + jnp.concatenate([bias_p[5], bias_p[6]]))
    k_cross = low(rms_norm(kv_lin[:, :width], gain_p[4])).reshape(text_len, H, HD)
    v_cross = low(kv_lin[:, width:]).reshape(text_len, H, HD)
    valid = jnp.arange(text_len, dtype=jnp.int32) < length

    def cross_block(q_block):
        scores = low_back(jnp.einsum('rhe,khe->hrk', q_block, k_cross, precision=HIGH) * scale)
        scores = jnp.where(valid[None, None, :], scores, NEG)
        probs = low(softmax_rows(scores))
        return jnp.einsum('hrk,khe->rhe', probs, v_cross, precision=HIGH)
    crossed = lax.map(jax.checkpoint(cross_block), q_cross.reshape(seq_len // block_rows, block_rows, H, HD))
    crossed = low(low_back(crossed.reshape(seq_len, width)))
    c_lin = low_back(jnp.dot(crossed, out_c, precision=HIGH) + bias_p[7])
    x_two = x_one + c_lin
    ffn_rows = low(layer_norm(x_two) * (1.0 + mods[4]) + mods[3])
    u_lin = low_back(jnp.dot(ffn_rows, w_in.T, precision=HIGH) + b_in)
    g_act = low(jax.nn.gelu(u_lin, approximate=True))
    z_lin = low_back(jnp.dot(g_act, w_out, precision=HIGH) + bias_p[9])
    return x_two + mods[5] * z_lin

def reference(clip_tokens, text_tokens, text_lengths, positions, time_embed, modulation, gains, biases, self_qkv, self_out, cross_qkv, cross_out, ffn_in, ffn_out, ffn_bias, cotangent):
    params = tuple((param.astype(jnp.float32) for param in (modulation, gains, biases, self_qkv, self_out, cross_qkv, cross_out, ffn_in, ffn_out, ffn_bias)))

    def per_clip(totals, inputs_now):
        x_clip, text_clip, length, place_rows, time_row, cot_clip = inputs_now

        def forward(x_f, text_f, *weights):
            return clip_forward(x_f, text_f, weights, time_row, length, place_rows)
        result, back_fn = jax.vjp(forward, x_clip.astype(jnp.float32), text_clip.astype(jnp.float32), *params)
        grads = back_fn(cot_clip.astype(jnp.float32))
        totals = tuple((total + grad for total, grad in zip(totals, grads[2:])))
        return (totals, (result.astype(jnp.bfloat16), grads[0], grads[1]))
    zeros = tuple((jnp.zeros_like(param) for param in params))
    totals, (outputs, grad_x, grad_txt) = lax.scan(per_clip, zeros, (clip_tokens, text_tokens, text_lengths, positions, time_embed, cotangent))
    return (outputs, grad_x, grad_txt) + totals
```

```python
import functools

import jax
import jax.numpy as jnp
import numpy as np
from jax import lax
from jax.experimental import pallas as pl
from jax.experimental.pallas import tpu as pltpu
from jax.sharding import PartitionSpec as P

H = 12
HD = 128


EPS = 1e-06
NEG = -1e30


def layer_norm(values):
    centre = values - jnp.mean(values, axis=-1, keepdims=True)
    return centre * lax.rsqrt(jnp.mean(centre * centre, axis=-1, keepdims=True) + EPS)


def rms_norm(values, gain_row):
    return values * lax.rsqrt(jnp.mean(values * values, axis=-1, keepdims=True) + EPS) * gain_row


def layer_back(values, grad_out):
    return jax.vjp(layer_norm, values)[1](grad_out)[0]


def rope_tables(head_dim):
    pair_count = head_dim // 2
    side_count = head_dim // 6
    first_count = pair_count - 2 * side_count
    tables = np.zeros((3, pair_count))
    for column in range(pair_count):
        if column < first_count:
            tables[0, column] = 10000.0 ** (-column / first_count)
        elif column < first_count + side_count:
            tables[1, column] = 10000.0 ** (-(column - first_count) / side_count)
        else:
            tables[2, column] = 10000.0 ** (-(column - first_count - side_count) / side_count)
    return tables


def rotate(values, cosine, sine_part):
    half_dim = values.shape[-1] // 2
    turned = jnp.concatenate([-values[..., half_dim:], values[..., :half_dim]], -1)
    return values * cosine[:, None, :] + turned * sine_part[:, None, :]


def softmax_rows(scores):
    top_score = jnp.max(scores, -1, keepdims=True)
    raised = jnp.exp(scores - top_score)
    return raised / jnp.sum(raised, -1, keepdims=True)


def col_sum(values):
    return jnp.sum(values.astype(jnp.float32), 0)


def gelu_tanh(inner):
    return jax.nn.gelu(inner, approximate=True)


BF = jnp.bfloat16
F32 = jnp.float32


MESH = pl.DeviceIdType.MESH
PARAM_ROWS = 32
SMALL_ROWS = 16 + PARAM_ROWS
SMALL_LANES = 256


def remote_copy(src, dst, send, recv, target):
    return pltpu.make_async_remote_copy(
        src_ref=src,
        dst_ref=dst,
        send_sem=send,
        recv_sem=recv,
        device_id=target,
        device_id_type=MESH,
    )


def meet(targets):
    barrier = pltpu.get_barrier_semaphore()
    for target in targets:
        pl.semaphore_signal(barrier, inc=1, device_id=target, device_id_type=MESH)
    pl.semaphore_wait(barrier, len(targets))


def rows_at(start, size):
    return pl.ds(pl.multiple_of(start, 16), size)


def lanes_at(start, size):
    return pl.ds(pl.multiple_of(start, 128), size)


def mm(a, b):
    return lax.dot_general(a, b, (((1,), (0,)), ((), ())), preferred_element_type=F32)


def mm_t(a, b):
    return lax.dot_general(a, b, (((1,), (1,)), ((), ())), preferred_element_type=F32)


def mm_first(a, b):
    return lax.dot_general(a, b, (((0,), (0,)), ((), ())), preferred_element_type=F32)


def exact_first(a, b):
    return lax.dot_general(
        a,
        b,
        (((0,), (0,)), ((), ())),
        precision=lax.Precision.HIGHEST,
        preferred_element_type=F32,
    )


def exact_sums(values):
    ones = jnp.ones((8, values.shape[1]), F32)
    return lax.dot_general(
        ones,
        values,
        (((1,), (1,)), ((), ())),
        precision=lax.Precision.HIGHEST,
        preferred_element_type=F32,
    )


def row_pick(which):
    return (lax.broadcasted_iota(jnp.int32, (8, 128), 0) == which).astype(F32)


def turn_sign():
    lane = lax.broadcasted_iota(jnp.int32, (1, HD), 1)
    return jnp.where(lane < HD // 2, -1.0, 1.0).astype(F32)


def turned(value, cosine, sine):
    return value * cosine + pltpu.roll(value, HD // 2, 1) * (sine * turn_sign())


def front_kernel(
    n_sp,
    x_ref,
    small_ref,
    qkv_ref,
    rest_ref,
    in_ref,
    out_ref,
    text_ref,
    cot_ref,
    time_ref,
    table_ref,
    par_ref,
    h1_out,
    w_out_ref,
    lin_out,
    rho_out,
    trig_out,
    q_out,
    kv_out,
    lse_out,
    att_out,
    tok_out,
    rest_out,
    in_out,
    out_out,
    text_out,
    cot_out,
    xall_ref,
    sall_ref,
    w_ref,
    lin_ref,
    sums_ref,
    rho_ref,
    trig_ref,
    q_ref,
    kv_ref,
    acc_ref,
    stat_ref,
    att_ref,
    h1_ref,
    *sems,
):
    lo, zs, zr, ss, sr, ws, wr, xs, xr, cs, cr, ps, pr, vs, vr, qs, qr, ts, tr, out = sems[:20]
    (ls, lr, lxs, lxr, lys, lyr, lcs, lcr, fs, fr, es, er, exs, exr, os, osr) = sems[20:]
    spot_d = lax.axis_index("dp")
    spot_b = lax.axis_index("blk")
    spot_s = lax.axis_index("sp")
    core = lax.rem(spot_d, 2)
    pair = lax.rem(spot_d // 2, 2)
    core_id = {"dp": spot_d + 1 - 2 * core}
    pair_id = {"dp": spot_d + 2 - 4 * pair}
    blk_id = {"blk": 1 - spot_b}
    line = [{"sp": lax.rem(spot_s + step, n_sp)} for step in range(1, n_sp)]
    rows = x_ref.shape[0]
    shard = qkv_ref.shape[0]
    half = shard // 2
    cols = w_ref.shape[1] // 3
    wide = qkv_ref.shape[1] // 3
    heads_here = cols // HD
    total_rows = n_sp * rows
    sums_ref[spot_s] = jnp.zeros((8, total_rows), F32)
    meet(line + [core_id, blk_id, pair_id])

    def w_rows(blk, spot, part):
        return rows_at((blk * n_sp + spot) * shard + part * half, half)

    here = spot_b * n_sp + spot_s
    keep = [
        pltpu.make_async_copy(
            qkv_ref.at[:, lanes_at(j * wide + spot_s * cols, cols)],
            w_ref.at[rows_at(here * shard, shard), pl.ds(j * cols, cols)],
            lo.at[j],
        )
        for j in range(3)
    ]
    keep.append(pltpu.make_async_copy(x_ref, xall_ref.at[rows_at(spot_s * rows, rows)], lo.at[3]))
    keep.append(pltpu.make_async_copy(small_ref, sall_ref.at[here], lo.at[4]))
    for copy in keep:
        copy.start()
    small_away = [
        remote_copy(small_ref, sall_ref.at[here], ss.at[k], sr.at[k], line[k])
        for k in range(n_sp - 1)
    ]
    for copy in small_away:
        copy.start()
    w_away = []
    for k in range(n_sp - 1):
        spot = lax.rem(spot_s + k + 1, n_sp)
        for j in range(3):
            copy = remote_copy(
                qkv_ref.at[rows_at(core * half, half), lanes_at(j * wide + spot * cols, cols)],
                w_ref.at[w_rows(spot_b, spot_s, core), pl.ds(j * cols, cols)],
                ws.at[3 * k + j],
                wr.at[3 * k + j],
                line[k],
            )
            copy.start()
            w_away.append(copy)

    def sends(way, k):
        if way == 0:
            return jnp.logical_and(spot_s < n_sp - 1, spot_s >= k)
        return jnp.logical_and(spot_s > 0, spot_s + k < n_sp)

    def gets(way, k):
        return spot_s > k if way == 0 else spot_s + k + 1 < n_sp

    def line_gather(first, place, pieces, send, recv, then=None):
        def copy(way, k, part):
            block = spot_s - k if way == 0 else spot_s + k
            at = place(block, part)
            src = first(part) if k == 0 else at
            target = {"sp": spot_s + 1 if way == 0 else spot_s - 1}
            index = (way * (n_sp - 1) + k) * pieces + part
            return remote_copy(src, at, send.at[index], recv.at[index], target)

        def step(k):
            for part in range(pieces):
                for way in range(2):
                    if k > 0:

                        @pl.when(gets(way, k - 1))
                        def _():
                            copy(way, k - 1, part).wait_recv()

                    if k < n_sp - 1:

                        @pl.when(sends(way, k))
                        def _():
                            copy(way, k, part).start()

                    if k > 0 and then is not None:

                        @pl.when(gets(way, k - 1))
                        def _():
                            then(spot_s - k if way == 0 else spot_s + k)

        def sent():
            for k in range(n_sp - 1):
                for part in range(pieces):
                    for way in range(2):

                        @pl.when(sends(way, k))
                        def _():
                            copy(way, k, part).wait_send()

        return step, sent

    pieces = 2
    piece = rows // pieces
    token_step, token_sent = line_gather(
        lambda part: x_ref.at[pl.ds(part * piece, piece)],
        lambda block, part: xall_ref.at[rows_at(block * rows + part * piece, piece)],
        pieces,
        zs,
        zr,
    )

    fourth = shard // 4
    quarter = core * 2 + pair

    def rest_rows(blk, spot, which):
        return rest_out.at[rows_at((blk * n_sp + spot) * shard + which * fourth, fourth)]

    def rest_copy(sems, blk, spot, which, slot, target):
        at = rest_rows(blk, spot, which)
        index = (slot * 2 + blk) * n_sp + spot
        return remote_copy(at, at, sems[0].at[index], sems[1].at[index], target)

    def rest_core(blk, spot, slot):
        which = core * 2 + (pair if slot == 0 else 1 - pair)
        return rest_copy((lcs, lcr), blk, spot, which, slot, core_id)

    def rest_pair(blk, spot):
        return rest_copy((lys, lyr), blk, spot, quarter, 0, pair_id)

    def rest_blk(spot):
        at = rest_rows(spot_b, spot, quarter)
        return remote_copy(at, at, lxs.at[spot], lxr.at[spot], blk_id)

    def rest_arrived(spot):
        rest_blk(spot).start()
        rest_pair(spot_b, spot).start()
        rest_core(spot_b, spot, 0).start()

    rest_step, rest_sent = line_gather(
        lambda part: rest_ref.at[rows_at(quarter * fourth, fourth)],
        lambda block, part: rest_rows(spot_b, block, quarter),
        1,
        ls,
        lr,
        rest_arrived,
    )
    rest_own = remote_copy(
        rest_ref.at[rows_at(quarter * fourth, fourth)],
        rest_rows(spot_b, spot_s, quarter),
        lxs.at[spot_s],
        lxr.at[spot_s],
        blk_id,
    )
    rest_keep = pltpu.make_async_copy(
        rest_ref, rest_out.at[rows_at((spot_b * n_sp + spot_s) * shard, shard)], out.at[9]
    )

    def at_distance(k, call):
        if k == 0:
            call(spot_s)
        else:
            for way in range(2):

                @pl.when(gets(way, k - 1))
                def _():
                    call(spot_s - k if way == 0 else spot_s + k)

    def rest_from_blk(k):
        def one(spot):
            rest_blk(spot).wait_recv()
            rest_pair(1 - spot_b, spot).start()
            rest_core(1 - spot_b, spot, 0).start()

        at_distance(k, one)

    def rest_from_pair(k):
        def one(spot):
            if k > 0:
                rest_pair(spot_b, spot).wait_recv()
                rest_core(spot_b, spot, 1).start()
            rest_pair(1 - spot_b, spot).wait_recv()
            rest_core(1 - spot_b, spot, 1).start()

        at_distance(k, one)

    def rest_last(k):
        def one(spot):
            for slot in range(2):
                if k > 0:
                    rest_core(spot_b, spot, slot).wait_recv()
                rest_core(1 - spot_b, spot, slot).wait_recv()

        at_distance(k, one)

    def rest_done(k):
        def one(spot):
            rest_blk(spot).wait_send()
            for slot in range(2):
                if k > 0:
                    rest_core(spot_b, spot, slot).wait_send()
                rest_core(1 - spot_b, spot, slot).wait_send()
            if k > 0:
                rest_pair(spot_b, spot).wait_send()
            rest_pair(1 - spot_b, spot).wait_send()

        at_distance(k, one)

    hidden = in_ref.shape[0]
    hidden_half = hidden // 2
    hidden_at = rows_at(core * hidden_half, hidden_half)

    def hidden_blk(which):
        src = in_ref if which == 0 else out_ref
        dst = in_out if which == 0 else out_out
        return remote_copy(
            src.at[hidden_at], dst.at[hidden_at], fs.at[which], fr.at[which], blk_id
        )

    def hidden_core(which):
        at = (in_out if which == 0 else out_out).at[hidden_at]
        return remote_copy(at, at, fs.at[2 + which], fr.at[2 + which], core_id)

    text_rows = text_ref.shape[0]

    def text_at(blk, spot):
        return text_out.at[rows_at((blk * n_sp + spot) * text_rows, text_rows)]

    def text_blk(spot, own):
        at = text_at(spot_b, spot)
        src = text_ref if own else at
        return remote_copy(src, at, exs.at[spot], exr.at[spot], blk_id)

    text_step, text_sent = line_gather(
        lambda part: text_ref,
        lambda block, part: text_at(spot_b, block),
        1,
        es,
        er,
        lambda spot: text_blk(spot, False).start(),
    )
    text_keep = pltpu.make_async_copy(text_ref, text_at(spot_b, spot_s), out.at[10])
    cot_step, cot_sent = line_gather(
        lambda part: cot_ref,
        lambda block, part: cot_out.at[rows_at(block * rows, rows)],
        1,
        os,
        osr,
    )
    cot_keep = pltpu.make_async_copy(
        cot_ref, cot_out.at[rows_at(spot_s * rows, rows)], out.at[11]
    )

    token_step(0)
    hidden_blk(0).start()
    for copy in (rest_keep, text_keep, cot_keep):
        copy.start()
    rest_own.start()
    text_blk(spot_s, True).start()
    for copy in small_away:
        copy.wait_recv()
    keep[4].wait()
    small_pass = []
    for spot in range(n_sp):
        at = sall_ref.at[spot_b * n_sp + spot]
        copy = remote_copy(at, at, ps.at[spot], pr.at[spot], blk_id)
        copy.start()
        small_pass.append(copy)
    for j in range(3):
        keep[j].wait()
    blk_away = []
    core_away = []

    def pass_core(blk, spot, which):
        at = w_ref.at[w_rows(blk, spot, core)]
        copy = remote_copy(at, at, cs.at[which], cr.at[which], core_id)
        copy.start()
        core_away.append(copy)

    def pass_blk(step):
        at = w_ref.at[w_rows(spot_b, lax.rem(spot_s + n_sp - step, n_sp), core)]
        copy = remote_copy(at, at, xs.at[step], xr.at[step], blk_id)
        copy.start()
        blk_away.append(copy)

    pass_blk(0)
    for k in range(n_sp - 1):
        for j in range(3):
            w_away[3 * k + j].wait_recv()
        pass_blk(k + 1)
        pass_core(spot_b, lax.rem(spot_s + n_sp - k - 1, n_sp), k)

    for copy in small_pass:
        copy.wait_recv()
    lanes = wide // (2 * n_sp)
    at_row = lax.broadcasted_iota(jnp.int32, (2 * SMALL_LANES, 2 * lanes), 0)
    at_col = lax.broadcasted_iota(jnp.int32, (2 * SMALL_LANES, 2 * lanes), 1)
    place = jnp.where(at_row < SMALL_LANES, at_row, at_row - SMALL_LANES)
    goal = jnp.where(at_row < SMALL_LANES, place, place + lanes)
    chosen = jnp.logical_and(place < lanes, goal == at_col).astype(F32).astype(BF)
    for two in range(n_sp):
        both = jnp.concatenate(
            [sall_ref[2 * two, 16:, :], sall_ref[2 * two + 1, 16:, :]], axis=1
        )
        par_ref[:, 2 * lanes * two : 2 * lanes * (two + 1)] = mm(both, chosen)

    token_step(1)
    for step in range(n_sp):
        blk_away[step].wait_recv()
        pass_core(1 - spot_b, lax.rem(spot_s + n_sp - step, n_sp), n_sp - 1 + step)
    for copy in core_away:
        copy.wait_recv()
    w_keep = pltpu.make_async_copy(w_ref, w_out_ref, lo.at[5])
    w_keep.start()
    keep[3].wait()

    shift = time_ref[0:1, :] + par_ref[0:1, :]
    scale = 1.0 + (time_ref[1:2, :] + par_ref[1:2, :])
    own = lanes_at(spot_s * cols, cols)

    def project(block):
        at = rows_at(block * rows, rows)
        values = xall_ref[at, :].astype(F32)
        centre = values - jnp.mean(values, axis=-1, keepdims=True)
        spread = jnp.mean(centre * centre, axis=-1, keepdims=True)
        h1_ref[at, :] = (centre * lax.rsqrt(spread + EPS) * scale + shift).astype(BF)
        for j in range(3):
            lin = mm(h1_ref[at, :], w_ref[:, j * cols : (j + 1) * cols])
            lin = lin + par_ref[11 + j : 12 + j, own]
            if j < 2:
                lin_ref[j, at, :] = lin
                sums = exact_sums(lin * lin)
                sums_ref[spot_s, j : j + 1, lanes_at(block * rows, rows)] = sums[0:1]
            else:
                kv_ref[1, at, :] = lin.astype(BF)
        value_copy(block).start()
        angle = exact_first(
            sall_ref[spot_b * n_sp + block, 0:16, :].astype(F32), table_ref[...]
        )
        trig_ref[0, at, :] = jnp.cos(angle)
        trig_ref[1, at, :] = jnp.sin(angle)

    def kv_copy(which, block):
        return remote_copy(
            kv_ref.at[which, rows_at(block * rows, rows)],
            kv_ref.at[which, rows_at(total_rows + block * rows, rows)],
            vs.at[which * n_sp + block],
            vr.at[which * n_sp + block],
            blk_id,
        )

    def value_copy(block):
        return kv_copy(1, block)

    def arrived(k):
        first = (spot_s >= k).astype(jnp.int32)
        last = (spot_s + k < n_sp).astype(jnp.int32)

        def one(i, carry):
            ahead = jnp.logical_and(first == 1, i == 0)
            project(jnp.where(ahead, spot_s - k, spot_s + k))
            return carry

        lax.fori_loop(0, first + last, one, 0)

    project(spot_s)
    arrived(1)
    for k in range(2, n_sp):
        token_step(k)
        arrived(k)
    rest_step(0)

    sums_away = []
    for k in range(n_sp - 1):
        copy = remote_copy(
            sums_ref.at[spot_s], sums_ref.at[spot_s], qs.at[k], qr.at[k], line[k]
        )
        copy.start()
        sums_away.append(copy)
    for copy in sums_away:
        copy.wait_recv()
    squares = sums_ref[0]
    for k in range(1, n_sp):
        squares = squares + sums_ref[k]
    rho_rows = lax.rsqrt(squares / wide + EPS)
    sums_ref[n_sp] = rho_rows

    def turn_block(which, block):
        at = rows_at(block * rows, rows)
        rho = exact_first(sums_ref[n_sp, :, lanes_at(block * rows, rows)], row_pick(which))
        rho_ref[which, at, :] = rho
        cosine = trig_ref[0, at, :]
        sine = trig_ref[1, at, :]
        for h in range(heads_here):
            gain = par_ref[6 + which : 7 + which, lanes_at(spot_s * cols + h * HD, HD)]
            value = lin_ref[which, at, h * HD : (h + 1) * HD] * rho * gain
            value = turned(value, cosine, sine).astype(BF)
            if which == 0:
                q_ref[at, h * HD : (h + 1) * HD] = value
            else:
                kv_ref[0, at, h * HD : (h + 1) * HD] = value

    def turn_key(block, carry):
        turn_block(1, block)
        kv_copy(0, block).start()
        return carry

    def turn_query(block, carry):
        turn_block(0, block)
        return carry

    lax.fori_loop(0, n_sp, turn_key, 0)
    lax.fori_loop(0, n_sp, turn_query, 0)
    rest_from_blk(0)
    text_step(0)
    hidden_blk(0).wait_recv()
    hidden_core(0).start()
    saves = [
        pltpu.make_async_copy(h1_ref, h1_out, out.at[0]),
        pltpu.make_async_copy(lin_ref, lin_out, out.at[1]),
        pltpu.make_async_copy(rho_ref, rho_out, out.at[2]),
        pltpu.make_async_copy(trig_ref, trig_out, out.at[3]),
        pltpu.make_async_copy(q_ref, q_out, out.at[4]),
    ]
    for copy in saves:
        copy.start()
    score_scale = HD ** (-0.5)

    def attend(block, h, part):
        at = rows_at(block * rows, rows)
        head = pl.ds(h * HD, HD)
        keys = pl.ds(part * total_rows, total_rows)
        scores = mm_t(q_ref[at, head], kv_ref[0, keys, head]) * score_scale
        top = jnp.max(scores, -1, keepdims=True)
        if part == 1:
            before = stat_ref[0, h, at, 0:1]
            top = jnp.maximum(top, before)
        raised = jnp.exp(scores - top)
        total = jnp.sum(raised, -1, keepdims=True)
        result = mm(raised.astype(BF), kv_ref[1, keys, head])
        if part == 0:
            stat_ref[0, h, at, :] = jnp.broadcast_to(top, (rows, 128))
            stat_ref[1, h, at, :] = jnp.broadcast_to(total, (rows, 128))
            acc_ref[h, at, :] = result
        else:
            fade = jnp.exp(before - top)
            total = total + fade * stat_ref[1, h, at, 0:1]
            result = result + fade * acc_ref[h, at, :]
            att_ref[at, head] = (result / total).astype(BF)
            stat_ref[0, h, at, :] = jnp.broadcast_to(top + jnp.log(total), (rows, 128))

    def first_pass(block, carry):
        for h in range(heads_here):
            attend(block, h, 0)
        return carry

    lax.fori_loop(0, n_sp, first_pass, 0)
    rest_step(1)

    def key_wait(block, carry):
        kv_copy(0, block).wait_recv()
        kv_copy(1, block).wait_recv()
        return carry

    lax.fori_loop(0, n_sp, key_wait, 0)
    kv_save = pltpu.make_async_copy(kv_ref, kv_out, out.at[5])
    kv_save.start()
    hidden_blk(1).start()

    def att_copy(step):
        block = lax.rem(spot_s + step, n_sp)
        return remote_copy(
            att_ref.at[rows_at(block * rows, rows)],
            tok_out.at[:, lanes_at(spot_s * cols, cols)],
            ts.at[step - 1],
            tr.at[step - 1],
            {"sp": block},
        )

    for step in list(range(1, n_sp)) + [0]:
        block = lax.rem(spot_s + step, n_sp)

        def one_head(block=block):
            for h in range(heads_here):
                attend(block, h, 1)

        one_head()
        if step > 0:
            att_copy(step).start()
        if step == 1:
            rest_step(2)
            text_step(1)
        if step == 2:
            rest_from_blk(1)
            rest_from_pair(0)
    own_att = pltpu.make_async_copy(
        att_ref.at[rows_at(spot_s * rows, rows)],
        tok_out.at[:, lanes_at(spot_s * cols, cols)],
        out.at[6],
    )
    own_att.start()
    saves.append(own_att)
    last = [
        pltpu.make_async_copy(stat_ref.at[0], lse_out, out.at[7]),
        pltpu.make_async_copy(att_ref, att_out, out.at[8]),
    ]
    for copy in last:
        copy.start()
    rest_step(3)
    cot_step(0)
    text_step(2)
    rest_from_pair(1)
    rest_from_blk(2)
    text_step(3)
    rest_from_blk(3)
    cot_step(1)
    rest_from_pair(2)
    cot_step(2)
    hidden_blk(1).wait_recv()
    hidden_core(1).start()
    rest_from_pair(3)
    cot_step(3)
    for k in range(n_sp):
        rest_last(k)
        at_distance(k, lambda spot: text_blk(spot, False).wait_recv())
    for which in range(2):
        hidden_core(which).wait_recv()
    for step in range(1, n_sp):
        att_copy(step).wait_recv()
    for copy in (rest_keep, text_keep, cot_keep):
        copy.wait()
    for k in range(n_sp):
        rest_done(k)
        at_distance(k, lambda spot: text_blk(spot, False).wait_send())
    for which in range(2):
        hidden_blk(which).wait_send()
        hidden_core(which).wait_send()
    rest_sent()
    text_sent()
    cot_sent()
    token_sent()
    for copy in saves + last + [kv_save, w_keep]:
        copy.wait()
    for copy in small_away + w_away + blk_away + core_away + small_pass + sums_away:
        copy.wait_send()

    def kv_sent(block, carry):
        kv_copy(0, block).wait_send()
        kv_copy(1, block).wait_send()
        return carry

    lax.fori_loop(0, n_sp, kv_sent, 0)
    for step in range(1, n_sp):
        att_copy(step).wait_send()


def front(x_own, small_own, qkv, rest, shard_in, shard_out, text, cot, time_rows):
    n_sp = lax.axis_size("sp")
    groups = 2 * n_sp
    rows, width = x_own.shape
    total = n_sp * rows
    cols = qkv.shape[1] // 3 // n_sp
    heads_here = cols // HD
    table = np.zeros((16, HD), np.float32)
    pairs = rope_tables(HD)
    table[:3, : HD // 2] = pairs
    table[:3, HD // 2 :] = pairs
    any_place = pl.BlockSpec(memory_space=pl.ANY)
    in_vmem = pl.BlockSpec(memory_space=pltpu.VMEM)
    dma = pltpu.SemaphoreType.DMA
    line = n_sp - 1
    counts = [6, 4 * line, 4 * line, line, line, 3 * line, 3 * line, n_sp, n_sp]
    counts += [2 * n_sp - 1, 2 * n_sp - 1, n_sp, n_sp, 2 * n_sp, 2 * n_sp, line, line]
    counts += [line, line, 12]
    counts += [2 * line, 2 * line, n_sp, n_sp, groups, groups, 2 * groups, 2 * groups, 4, 4]
    counts += [2 * line, 2 * line, n_sp, n_sp, 2 * line, 2 * line]
    shape = jax.ShapeDtypeStruct
    outs = (
        shape((PARAM_ROWS, width), F32),
        shape((total, width), BF),
        shape((width, 3 * cols), BF),
        shape((2, total, cols), F32),
        shape((2, total, HD), F32),
        shape((2, total, HD), F32),
        shape((total, cols), BF),
        shape((2, 2 * total, cols), BF),
        shape((heads_here, total, HD), F32),
        shape((total, cols), BF),
        shape((rows, width), BF),
        shape((groups * rest.shape[0], rest.shape[1]), BF),
        shape(shard_in.shape, BF),
        shape(shard_out.shape, BF),
        shape((groups * text.shape[0], width), BF),
        shape((total, width), BF),
    )
    vmem = pltpu.VMEM
    return pl.pallas_call(
        functools.partial(front_kernel, n_sp),
        out_shape=outs,
        in_specs=[any_place] * 8 + [in_vmem] * 2,
        out_specs=(in_vmem,) + (any_place,) * (len(outs) - 1),
        scratch_shapes=[
            vmem((total, width), BF),
            vmem((groups, SMALL_ROWS, SMALL_LANES), BF),
            vmem((width, 3 * cols), BF),
            vmem((2, total, cols), F32),
            vmem((n_sp + 1, 8, total), F32),
            vmem((2, total, HD), F32),
            vmem((2, total, HD), F32),
            vmem((total, cols), BF),
            vmem((2, 2 * total, cols), BF),
            vmem((heads_here, total, HD), F32),
            vmem((2, heads_here, total, HD), F32),
            vmem((total, cols), BF),
            vmem((total, width), BF),
        ]
        + [dma((count,)) for count in counts],
        compiler_params=pltpu.CompilerParams(
            collective_id=1, has_side_effects=True, vmem_limit_bytes=56 * 2**20
        ),
    )(x_own, small_own, qkv, rest, shard_in, shard_out, text, cot, time_rows, jnp.asarray(table))


def dot(a, b):
    return jnp.dot(a, b, preferred_element_type=F32)


def dot_t(a, b):
    return jnp.einsum("te,de->td", a, b, preferred_element_type=F32)


def dot_g(a, b):
    return jnp.einsum("td,te->de", a, b, preferred_element_type=F32)


def after(value, *others):
    return lax.optimization_barrier((value, others))[0]


def from_back(value, step):
    size = lax.axis_size("sp")
    return lax.ppermute(value, "sp", [(i, (i + step) % size) for i in range(size)])


def to_back(value, step):
    size = lax.axis_size("sp")
    return lax.ppermute(value, "sp", [(i, (i - step) % size) for i in range(size)])


def swap_blk(value):
    return lax.ppermute(value, "blk", [(0, 1), (1, 0)])


def swap_dp(value, bit):
    size = lax.axis_size("dp")
    return lax.ppermute(value, "dp", [(i, i ^ bit) for i in range(size)])


def gather_sp(value):
    size = lax.axis_size("sp")
    return [value] + [from_back(value, step) for step in range(1, size)]


def total_sp(own, parts):
    total = own
    for step in range(1, len(parts)):
        total = total + to_back(parts[step].astype(BF), step).astype(F32)
    return total


def in_order_back(blocks, place, axis):
    size = len(blocks)
    back = blocks[::-1]
    whole = jnp.concatenate(back + back[:-1], axis)
    width = blocks[0].shape[axis]
    return lax.dynamic_slice_in_dim(whole, (size - 1 - place) * width, size * width, axis)


def in_order_ahead(blocks, place, axis):
    size = len(blocks)
    whole = jnp.concatenate(blocks + blocks[:-1], axis)
    width = blocks[0].shape[axis]
    return lax.dynamic_slice_in_dim(whole, ((size - place) % size) * width, size * width, axis)


def pair_order(own, other, place, axis):
    return jnp.where(
        place == 0, jnp.concatenate([own, other], axis), jnp.concatenate([other, own], axis)
    )


def part_of(value, index, count, axis):
    width = value.shape[axis] // count
    return lax.dynamic_slice_in_dim(value, index * width, width, axis)


def sum_sp_rows(sums):
    size = lax.axis_size("sp")
    total = sums
    for step in range(1, size):
        total = total + from_back(sums, step)
    return total


def local(
    clip_tokens,
    text_tokens,
    text_lengths,
    positions,
    time_embed,
    modulation,
    gains,
    biases,
    self_qkv,
    self_out,
    cross_qkv,
    cross_out,
    ffn_in,
    ffn_out,
    ffn_bias,
    cotangent,
):
    n_sp = lax.axis_size("sp")
    n_dp = lax.axis_size("dp")
    spot_dp = lax.axis_index("dp")
    spot_b = lax.axis_index("blk")
    spot_s = lax.axis_index("sp")
    core = spot_dp % 2
    pair = (spot_dp // 2) % 2
    x_own = clip_tokens[0]
    tok_rows, width = x_own.shape
    heads_here = H // n_sp
    cols_here = heads_here * HD
    shard_rows = self_qkv.shape[0]
    scale = HD ** (-0.5)

    small_rows = jnp.concatenate([modulation, gains, biases], 0)
    lanes_here = small_rows.shape[1]
    small_own = jnp.concatenate(
        [
            jnp.pad(
                positions[0].astype(BF), ((0, 13), (0, SMALL_LANES - positions.shape[2]))
            ),
            jnp.pad(
                small_rows, ((0, PARAM_ROWS - 21), (0, SMALL_LANES - lanes_here))
            ),
        ],
        0,
    )
    (
        params,
        h1_all,
        qkv_mine,
        lin_parts,
        rho,
        trig,
        q_flat,
        kv_flat,
        lse_wide,
        att_all,
        att_tok,
        rest_all,
        in_other,
        out_other,
        text_every,
        cot_every,
    ) = front(
        x_own,
        small_own,
        self_qkv,
        jnp.concatenate([self_out, cross_out, cross_qkv], 1),
        ffn_in,
        ffn_out,
        text_tokens[0],
        cotangent[0],
        time_embed[0],
    )
    out_self = rest_all[:, :width]
    out_cross = rest_all[:, width : 2 * width]
    qkv_cross = rest_all[:, 2 * width :]
    in_all = jnp.concatenate([ffn_in, in_other], 0)
    out_all = jnp.concatenate([ffn_out, out_other], 0)
    cot_blocks = [part_of(cot_every, (spot_s - step) % n_sp, n_sp, 0) for step in range(n_sp)]
    mods = time_embed[0] + params[:6]
    gain_all = params[6:11]
    bias_all = params[11:21]
    ff_here = ffn_in.shape[0]
    bias_own = ffn_bias.astype(F32)
    bias_ff = jnp.concatenate([bias_own, swap_blk(ffn_bias).astype(F32)])
    half_rows = shard_rows // 2

    def own_cols(row):
        return part_of(row, spot_s, n_sp, row.ndim - 1)

    gain_cols = own_cols(gain_all)
    q_lin = lin_parts[0]
    k_lin = lin_parts[1]
    rows_all = q_lin.shape[0]
    rho = rho[:, :, :1]
    cosine = trig[0]
    sine_part = trig[1]

    def heads(value):
        return value.reshape(-1, heads_here, HD)

    q_own = heads(q_flat)
    k_every = heads(kv_flat[0])
    v_every = heads(kv_flat[1])

    block_count = 2
    block_rows = rows_all // block_count
    lse_parts = [
        lse_wide[:, block * block_rows : (block + 1) * block_rows, 0]
        for block in range(block_count)
    ]

    tokens = x_own.astype(F32)
    a_lin = dot(att_tok, out_self) + bias_all[3]
    x_one = tokens + mods[2] * a_lin
    normed_three = layer_norm(x_one)
    cross_in = (normed_three * gain_all[2] + bias_all[8]).astype(BF)
    qc_lin = dot(cross_in, qkv_cross[:, :width]) + bias_all[4]
    q_cross = rms_norm(qc_lin, gain_all[3]).astype(BF).reshape(tok_rows, H, HD)
    kv_lin = dot(text_every, qkv_cross[:, width:]) + jnp.concatenate([bias_all[5], bias_all[6]])
    k_cross = rms_norm(kv_lin[:, :width], gain_all[4]).astype(BF).reshape(-1, H, HD)
    v_cross = kv_lin[:, width:].astype(BF).reshape(-1, H, HD)
    text_rows = text_tokens.shape[1]
    valid = jnp.arange(text_every.shape[0], dtype=jnp.int32) < text_lengths[0]
    scores_c = (
        jnp.einsum("rhe,khe->hrk", q_cross, k_cross, preferred_element_type=F32) * scale
    )
    probs_c = softmax_rows(jnp.where(valid[None, None, :], scores_c, NEG))
    probs_cb = probs_c.astype(BF)
    crossed = (
        jnp.einsum("hrk,khe->rhe", probs_cb, v_cross, preferred_element_type=F32)
        .reshape(tok_rows, width)
        .astype(BF)
    )
    c_lin = dot(crossed, out_cross) + bias_all[7]
    x_two = x_one + c_lin
    normed_two = layer_norm(x_two)
    ffn_rows = (normed_two * (1.0 + mods[4]) + mods[3]).astype(BF)

    h2_blocks = gather_sp(ffn_rows)
    z_parts = []
    dh2_parts = []
    g_blocks = []
    du_blocks = []
    dz_blocks = []
    for step in range(n_sp):
        u_lin = dot_t(h2_blocks[step], in_all) + bias_ff
        g_act, gelu_back = jax.vjp(gelu_tanh, u_lin)
        g_low = g_act.astype(BF)
        d_z = (cot_blocks[step].astype(F32) * mods[5]).astype(BF)
        d_g = dot_t(d_z, out_all)
        d_u = gelu_back(d_g)[0].astype(BF)
        dh2_parts.append(dot(d_u, in_all))
        z_parts.append(dot(g_low, out_all))
        g_blocks.append(g_low)
        du_blocks.append(d_u)
        dz_blocks.append(d_z)
    d_rows = total_sp(dh2_parts[0], dh2_parts)
    z_line = jnp.zeros((n_sp, tok_rows, width), BF)
    for step in range(n_sp):
        z_line = lax.dynamic_update_index_in_dim(
            z_line, z_parts[step].astype(BF), (spot_s - step) % n_sp, 0
        )
    z_lin = (
        lax.psum_scatter(z_line, "sp", scatter_dimension=0, tiled=False).astype(F32) + bias_all[9]
    )
    grad_y = cotangent[0].astype(F32)
    result = x_two + mods[5] * z_lin
    block_out = result.astype(BF)[None]
    d_gate2 = jnp.sum(grad_y * z_lin, 0)
    du_all = jnp.concatenate(du_blocks, 0)
    g_all = jnp.concatenate(g_blocks, 0)
    h2_all = jnp.concatenate(h2_blocks, 0)
    dz_all = jnp.concatenate(dz_blocks, 0)
    g_hidden_in = dot_g(du_all, h2_all).astype(BF)
    g_hidden_out = dot_g(g_all, dz_all).astype(BF)
    du_sums = col_sum(du_all)

    def round_add(own, got):
        return own.astype(F32) + got.astype(F32)

    def core_half(grad, which):
        return part_of(grad[:ff_here], which, 2, 0), part_of(grad[ff_here:], which, 2, 0)

    keep_in = core_half(g_hidden_in, core)
    keep_out = core_half(g_hidden_out, core)
    away_in = core_half(g_hidden_in, 1 - core)
    away_out = core_half(g_hidden_out, 1 - core)
    ff_core = swap_dp(jnp.stack([away_in[0], away_out[0], away_in[1], away_out[1]]), 1)
    ff_sum = round_add(
        jnp.stack([keep_in[0], keep_out[0], keep_in[1], keep_out[1]]), ff_core
    )
    ff_part = ff_sum[:2] + swap_blk(ff_sum[2:].astype(BF)).astype(F32)
    bit = 2
    while bit < n_dp:
        low = ff_part.astype(BF)
        ff_part = round_add(low, swap_dp(low, bit))
        bit *= 2
    ff_low = ff_part.astype(BF)
    ff_final = pair_order(ff_low, swap_dp(ff_low, 1), core, 1).astype(F32)

    d_shift2 = jnp.sum(d_rows, 0)
    d_scale2 = jnp.sum(d_rows * normed_two, 0)
    d_x_two = grad_y + layer_back(x_two, d_rows * (1.0 + mods[4]))

    def scatter_weight(rows, grads):
        def half(which):
            return dot_g(rows, part_of(grads, which, 2, 1))

        got = swap_dp(half(1 - core).astype(BF), 1)
        total = half(core) + got.astype(F32)
        away = part_of(total, 1 - pair, 2, 1).astype(BF)
        total = part_of(total, pair, 2, 1) + swap_dp(away, 2).astype(F32)
        return lax.psum_scatter(
            total.astype(BF), ("blk", "sp"), scatter_dimension=0, tiled=True
        ).astype(F32)

    def spread_weight(total):
        bit = 4
        while bit < n_dp:
            low = total.astype(BF)
            total = round_add(low, swap_dp(low, bit))
            bit *= 2
        low = total.astype(BF)
        low = pair_order(low, swap_dp(low, 2), pair, 1)
        return pair_order(low, swap_dp(low, 1), core, 1).astype(F32)

    d_c = d_x_two.astype(BF)
    g_out_cross = scatter_weight(crossed, d_c)
    d_oc = dot_t(d_c, out_cross).astype(BF).reshape(tok_rows, H, HD)
    d_vc = jnp.einsum("hrk,rhe->khe", probs_cb, d_oc, preferred_element_type=F32)
    d_pc = jnp.einsum("rhe,khe->hrk", d_oc, v_cross, preferred_element_type=F32)
    d_sc = (probs_c * (d_pc - jnp.sum(probs_c * d_pc, -1, keepdims=True))).astype(BF)
    d_qc = jnp.einsum("hrk,khe->rhe", d_sc, k_cross, preferred_element_type=F32) * scale
    d_kc = jnp.einsum("hrk,rhe->khe", d_sc, q_cross, preferred_element_type=F32) * scale
    d_qc_lin, d_gain3 = jax.vjp(rms_norm, qc_lin, gain_all[3])[1](d_qc.reshape(tok_rows, width))
    d_qc_low = d_qc_lin.astype(BF)
    d_cross_in = dot_t(d_qc_low, qkv_cross[:, :width])
    d_gain2 = jnp.sum(d_cross_in * normed_three, 0)
    d_bias8 = jnp.sum(d_cross_in, 0)
    d_x_one = d_x_two + layer_back(x_one, d_cross_in * gain_all[2])
    d_a = (d_x_one * mods[2]).astype(BF)
    d_gate1 = jnp.sum(d_x_one * a_lin, 0)
    d_att = dot_t(d_a, out_self).astype(BF)

    d_o_line = lax.all_to_all(
        d_att.reshape(tok_rows, n_sp, cols_here).transpose(1, 0, 2),
        "sp",
        split_axis=0,
        concat_axis=0,
        tiled=True,
    )
    d_o = heads(d_o_line.reshape(rows_all, cols_here))

    text_all = d_kc.shape[0]
    d_kc_lin, d_gain4 = jax.vjp(rms_norm, kv_lin[:, :width], gain_all[4])[1](
        d_kc.reshape(text_all, width)
    )
    d_kv_lin = jnp.concatenate(
        [d_kc_lin.astype(BF), d_vc.reshape(text_all, width).astype(BF)], -1
    )
    text_part = dot_t(d_kv_lin, qkv_cross[:, width:])
    grad_text = lax.psum_scatter(
        text_part.astype(BF), ("blk", "sp"), scatter_dimension=0, tiled=True
    ).astype(F32)
    g_q_cross = scatter_weight(cross_in, d_qc_low)
    g_kv_cross = scatter_weight(text_every, d_kv_lin)
    g_out_self = scatter_weight(att_tok, d_a)

    acc_k = jnp.zeros(k_every.shape, F32)
    acc_v = jnp.zeros(k_every.shape, F32)
    dq_parts = []
    for block in range(block_count):
        q_block = q_own[block * block_rows : (block + 1) * block_rows]
        do_block = d_o[block * block_rows : (block + 1) * block_rows]
        scores = (
            jnp.einsum("rhe,khe->hrk", q_block, k_every, preferred_element_type=F32) * scale
        )
        probs = jnp.exp(scores - lse_parts[block][..., None])
        acc_v = acc_v + jnp.einsum(
            "hrk,rhe->khe", probs.astype(BF), do_block, preferred_element_type=F32
        )
        d_p = jnp.einsum("rhe,khe->hrk", do_block, v_every, preferred_element_type=F32)
        d_s = (probs * (d_p - jnp.sum(probs * d_p, -1, keepdims=True))).astype(BF)
        dq_parts.append(
            jnp.einsum("hrk,khe->rhe", d_s, k_every, preferred_element_type=F32) * scale
        )
        acc_k = (
            acc_k
            + jnp.einsum("hrk,rhe->khe", d_s, q_block, preferred_element_type=F32) * scale
        )
    kv_away = jnp.stack([acc_k[rows_all:].astype(BF), acc_v[rows_all:].astype(BF)])
    kv_got = swap_blk(kv_away.reshape(2, rows_all, cols_here)).astype(F32)
    d_k = acc_k[:rows_all].reshape(rows_all, cols_here) + kv_got[0]
    d_v = acc_v[:rows_all].reshape(rows_all, cols_here) + kv_got[1]
    d_q = jnp.concatenate(dq_parts, 0)

    def unturn(grad):
        return rotate(heads(grad), cosine, -sine_part).reshape(rows_all, cols_here)

    e_q = unturn(d_q)
    e_k = unturn(d_k)
    vge_q = q_lin * gain_cols[0] * e_q
    vge_k = k_lin * gain_cols[1] * e_k
    means = jnp.stack([jnp.sum(vge_q, -1), jnp.sum(vge_k, -1)])
    means = sum_sp_rows(means) / width
    cubes = (rho * rho * rho) * means[..., None]
    d_q_lin = rho[0] * gain_cols[0] * e_q - q_lin * cubes[0]
    d_k_lin = rho[1] * gain_cols[1] * e_k - k_lin * cubes[1]
    d_gain0 = jnp.sum(e_q * q_lin * rho[0], 0)
    d_gain1 = jnp.sum(e_k * k_lin * rho[1], 0)
    d_proj = jnp.concatenate([d_q_lin.astype(BF), d_k_lin.astype(BF), d_v.astype(BF)], -1)
    dh1_part = dot_t(d_proj, qkv_mine)
    dh1_steps = [part_of(dh1_part, (spot_s - step) % n_sp, n_sp, 0) for step in range(n_sp)]
    d_shift = total_sp(dh1_steps[0], dh1_steps)
    normed_one = layer_norm(tokens)
    grad_tokens = d_x_one + layer_back(tokens, d_shift * (1.0 + mods[1]))
    d_shift1 = jnp.sum(d_shift, 0)
    d_scale1 = jnp.sum(d_shift * normed_one, 0)

    g_qkv = dot_g(h1_all, d_proj).astype(BF).reshape(2 * n_sp, 2, half_rows, 3 * cols_here)
    qkv_core = swap_dp(jnp.take(g_qkv, 1 - core, axis=1), 1)
    qkv_sum = round_add(jnp.take(g_qkv, core, axis=1), qkv_core)
    qkv_sum = part_of(qkv_sum, spot_b, 2, 0) + swap_blk(
        part_of(qkv_sum, 1 - spot_b, 2, 0).astype(BF)
    ).astype(F32)
    qkv_line = lax.all_to_all(
        qkv_sum.astype(BF), "sp", split_axis=0, concat_axis=0, tiled=True
    )
    bit = 2
    while bit < n_dp:
        qkv_line = round_add(qkv_line, swap_dp(qkv_line, bit)).astype(BF)
        bit *= 2
    qkv_rows = pair_order(qkv_line, swap_dp(qkv_line, 1), core, 1)
    part_sqkv = (
        qkv_rows.reshape(n_sp, shard_rows, 3, cols_here)
        .transpose(1, 2, 0, 3)
        .reshape(shard_rows, 3 * width)
        .astype(F32)
    )

    def wide(row):
        return lax.dynamic_update_slice_in_dim(
            jnp.zeros((width,), F32), row, spot_s * cols_here, 0
        )

    proj_sums = col_sum(d_proj)
    kv_sums = col_sum(d_kv_lin)
    ff_total = ff_here * 2 * n_sp
    ff_row = jnp.zeros((-(-ff_total // width) * width,), F32)
    own_at = (spot_b * n_sp + spot_s) * ff_here
    far_at = ((1 - spot_b) * n_sp + spot_s) * ff_here
    ff_row = lax.dynamic_update_slice_in_dim(ff_row, du_sums[:ff_here], own_at, 0)
    ff_row = lax.dynamic_update_slice_in_dim(ff_row, du_sums[ff_here:], far_at, 0)
    small = jnp.concatenate(
        [
            jnp.stack(
                [
                    d_shift1,
                    d_scale1,
                    d_gate1,
                    d_shift2,
                    d_scale2,
                    d_gate2,
                    wide(d_gain0),
                    wide(d_gain1),
                    d_gain2,
                    d_gain3,
                    d_gain4,
                    wide(proj_sums[:cols_here]),
                    wide(proj_sums[cols_here : 2 * cols_here]),
                    wide(proj_sums[2 * cols_here :]),
                    col_sum(d_a),
                    col_sum(d_qc_low),
                    kv_sums[:width],
                    kv_sums[width:],
                    col_sum(d_c),
                    d_bias8,
                    col_sum(dz_blocks[0]),
                ]
            ),
            ff_row.reshape(-1, width),
        ],
        0,
    )
    bit = 1
    while bit < n_dp:
        small = small + swap_dp(small, bit)
        bit *= 2
    small = small + swap_blk(small)
    bit = 1
    while bit < n_sp:
        small = small + lax.ppermute(small, "sp", [(i, i ^ bit) for i in range(n_sp)])
        bit *= 2
    spot = spot_b * n_sp + spot_s
    small_own = lax.dynamic_slice_in_dim(small[:21], spot * lanes_here, lanes_here, 1)
    part_bias = lax.dynamic_slice_in_dim(small[21:].reshape(-1), own_at, ff_here, 0)
    return (
        block_out,
        grad_tokens[None],
        grad_text[None],
        small_own[:6],
        small_own[6:11],
        small_own[11:21],
        part_sqkv,
        spread_weight(g_out_self),
        jnp.concatenate([spread_weight(g_q_cross), spread_weight(g_kv_cross)], 1),
        spread_weight(g_out_cross),
        ff_final[0],
        ff_final[1],
        part_bias,
    )


def solution(mesh):
    return jax.shard_map(
        local,
        mesh=mesh,
        in_specs=(
            P("dp", ("blk", "sp"), None),
            P("dp", ("blk", "sp"), None),
            P("dp"),
            P("dp", None, ("blk", "sp")),
            P("dp", None, None),
            P(None, ("blk", "sp")),
            P(None, ("blk", "sp")),
            P(None, ("blk", "sp")),
            P(("blk", "sp"), None),
            P(("blk", "sp"), None),
            P(("blk", "sp"), None),
            P(("blk", "sp"), None),
            P(("blk", "sp"), None),
            P(("blk", "sp"), None),
            P(("blk", "sp")),
            P("dp", ("blk", "sp"), None),
        ),
        out_specs=(
            P("dp", ("blk", "sp"), None),
            P("dp", ("blk", "sp"), None),
            P("dp", ("blk", "sp"), None),
            P(None, ("blk", "sp")),
            P(None, ("blk", "sp")),
            P(None, ("blk", "sp")),
            P(("blk", "sp"), None),
            P(("blk", "sp"), None),
            P(("blk", "sp"), None),
            P(("blk", "sp"), None),
            P(("blk", "sp"), None),
            P(("blk", "sp"), None),
            P(("blk", "sp")),
        ),
        check_vma=False,
    )
```

```python
import functools
import types

import jax
import jax.numpy as jnp
import numpy as np
from jax import lax
from jax.experimental import pallas as pl
from jax.experimental.pallas import tpu as pltpu
from jax.sharding import PartitionSpec as P

H = 12
HD = 128


DP, BLK, SP = "dp", "blk", "sp"
EPS = 1e-06
NEG = -1e30


def rope_tables(head_dim):
    pair_count = head_dim // 2
    side_count = head_dim // 6
    first_count = pair_count - 2 * side_count
    tables = np.zeros((3, pair_count))
    for column in range(pair_count):
        if column < first_count:
            tables[0, column] = 10000.0 ** (-column / first_count)
        elif column < first_count + side_count:
            tables[1, column] = 10000.0 ** (-(column - first_count) / side_count)
        else:
            tables[2, column] = 10000.0 ** (-(column - first_count - side_count) / side_count)
    return tables


BF = jnp.bfloat16
F32 = jnp.float32


MESH = pl.DeviceIdType.MESH
PARAM_ROWS = 32
SMALL_ROWS = 16 + PARAM_ROWS
SMALL_LANES = 256


def remote_copy(src, dst, send, recv, target):
    return pltpu.make_async_remote_copy(
        src_ref=src,
        dst_ref=dst,
        send_sem=send,
        recv_sem=recv,
        device_id=target,
        device_id_type=MESH,
    )


def meet(targets):
    barrier = pltpu.get_barrier_semaphore()
    for target in targets:
        pl.semaphore_signal(barrier, inc=1, device_id=target, device_id_type=MESH)
    pl.semaphore_wait(barrier, len(targets))


def rows_at(start, size):
    return pl.ds(pl.multiple_of(start, 16), size)


def lanes_at(start, size):
    return pl.ds(pl.multiple_of(start, 128), size)


def mm(a, b):
    return lax.dot_general(a, b, (((1,), (0,)), ((), ())), preferred_element_type=F32)


def mm_t(a, b):
    return lax.dot_general(a, b, (((1,), (1,)), ((), ())), preferred_element_type=F32)


def mm_first(a, b):
    return lax.dot_general(a, b, (((0,), (0,)), ((), ())), preferred_element_type=F32)


def exact_first(a, b):
    return lax.dot_general(
        a,
        b,
        (((0,), (0,)), ((), ())),
        precision=lax.Precision.HIGHEST,
        preferred_element_type=F32,
    )


def exact_sums(values):
    ones = jnp.ones((8, values.shape[1]), F32)
    return lax.dot_general(
        ones,
        values,
        (((1,), (1,)), ((), ())),
        precision=lax.Precision.HIGHEST,
        preferred_element_type=F32,
    )


def row_pick(which):
    return (lax.broadcasted_iota(jnp.int32, (8, 128), 0) == which).astype(F32)


def turn_sign():
    lane = lax.broadcasted_iota(jnp.int32, (1, HD), 1)
    return jnp.where(lane < HD // 2, -1.0, 1.0).astype(F32)


def turned(value, cosine, sine):
    return value * cosine + pltpu.roll(value, HD // 2, 1) * (sine * turn_sign())


def front_kernel(
    n_sp,
    x_ref,
    small_ref,
    qkv_ref,
    rest_ref,
    in_ref,
    out_ref,
    text_ref,
    cot_ref,
    time_ref,
    table_ref,
    par_ref,
    h1_out,
    w_out_ref,
    lin_out,
    rho_out,
    trig_out,
    q_out,
    kv_out,
    lse_out,
    att_out,
    tok_out,
    rest_out,
    in_out,
    out_out,
    text_out,
    cot_out,
    xall_ref,
    sall_ref,
    w_ref,
    lin_ref,
    sums_ref,
    rho_ref,
    trig_ref,
    q_ref,
    kv_ref,
    acc_ref,
    stat_ref,
    att_ref,
    h1_ref,
    *sems,
):
    lo, zs, zr, ss, sr, ws, wr, xs, xr, cs, cr, ps, pr, vs, vr, qs, qr, ts, tr, out = sems[:20]
    (ls, lr, lxs, lxr, lys, lyr, lcs, lcr, fs, fr, es, er, exs, exr, os, osr) = sems[20:]
    spot_d = lax.axis_index(DP)
    spot_b = lax.axis_index(BLK)
    spot_s = lax.axis_index(SP)
    core = lax.rem(spot_d, 2)
    pair = lax.rem(spot_d // 2, 2)
    core_id = {DP: spot_d + 1 - 2 * core}
    pair_id = {DP: spot_d + 2 - 4 * pair}
    blk_id = {BLK: 1 - spot_b}
    line = [{SP: lax.rem(spot_s + step, n_sp)} for step in range(1, n_sp)]
    rows = x_ref.shape[0]
    shard = qkv_ref.shape[0]
    half = shard // 2
    cols = w_ref.shape[1] // 3
    wide = qkv_ref.shape[1] // 3
    heads_here = cols // HD
    total_rows = n_sp * rows
    sums_ref[spot_s] = jnp.zeros((8, total_rows), F32)
    meet(line + [core_id, blk_id, pair_id])

    def w_rows(blk, spot, part):
        return rows_at((blk * n_sp + spot) * shard + part * half, half)

    here = spot_b * n_sp + spot_s
    keep = [
        pltpu.make_async_copy(
            qkv_ref.at[:, lanes_at(j * wide + spot_s * cols, cols)],
            w_ref.at[rows_at(here * shard, shard), pl.ds(j * cols, cols)],
            lo.at[j],
        )
        for j in range(3)
    ]
    keep.append(pltpu.make_async_copy(x_ref, xall_ref.at[rows_at(spot_s * rows, rows)], lo.at[3]))
    keep.append(pltpu.make_async_copy(small_ref, sall_ref.at[here], lo.at[4]))
    for copy in keep:
        copy.start()
    small_away = [
        remote_copy(small_ref, sall_ref.at[here], ss.at[k], sr.at[k], line[k])
        for k in range(n_sp - 1)
    ]
    for copy in small_away:
        copy.start()
    w_away = []
    for k in range(n_sp - 1):
        spot = lax.rem(spot_s + k + 1, n_sp)
        for j in range(3):
            copy = remote_copy(
                qkv_ref.at[rows_at(core * half, half), lanes_at(j * wide + spot * cols, cols)],
                w_ref.at[w_rows(spot_b, spot_s, core), pl.ds(j * cols, cols)],
                ws.at[3 * k + j],
                wr.at[3 * k + j],
                line[k],
            )
            copy.start()
            w_away.append(copy)

    def sends(way, k):
        if way == 0:
            return jnp.logical_and(spot_s < n_sp - 1, spot_s >= k)
        return jnp.logical_and(spot_s > 0, spot_s + k < n_sp)

    def gets(way, k):
        return spot_s > k if way == 0 else spot_s + k + 1 < n_sp

    def line_gather(first, place, pieces, send, recv, then=None):
        def copy(way, k, part):
            block = spot_s - k if way == 0 else spot_s + k
            at = place(block, part)
            src = first(part) if k == 0 else at
            target = {SP: spot_s + 1 if way == 0 else spot_s - 1}
            index = (way * (n_sp - 1) + k) * pieces + part
            return remote_copy(src, at, send.at[index], recv.at[index], target)

        def step(k):
            for part in range(pieces):
                for way in range(2):
                    if k > 0:

                        @pl.when(gets(way, k - 1))
                        def _():
                            copy(way, k - 1, part).wait_recv()

                    if k < n_sp - 1:

                        @pl.when(sends(way, k))
                        def _():
                            copy(way, k, part).start()

                    if k > 0 and then is not None:

                        @pl.when(gets(way, k - 1))
                        def _():
                            then(spot_s - k if way == 0 else spot_s + k)

        def sent():
            for k in range(n_sp - 1):
                for part in range(pieces):
                    for way in range(2):

                        @pl.when(sends(way, k))
                        def _():
                            copy(way, k, part).wait_send()

        return step, sent

    pieces = 2
    piece = rows // pieces
    token_step, token_sent = line_gather(
        lambda part: x_ref.at[pl.ds(part * piece, piece)],
        lambda block, part: xall_ref.at[rows_at(block * rows + part * piece, piece)],
        pieces,
        zs,
        zr,
    )

    fourth = shard // 4
    quarter = core * 2 + pair

    def rest_rows(blk, spot, which):
        return rest_out.at[rows_at((blk * n_sp + spot) * shard + which * fourth, fourth)]

    def rest_copy(sems, blk, spot, which, slot, target):
        at = rest_rows(blk, spot, which)
        index = (slot * 2 + blk) * n_sp + spot
        return remote_copy(at, at, sems[0].at[index], sems[1].at[index], target)

    def rest_core(blk, spot, slot):
        which = core * 2 + (pair if slot == 0 else 1 - pair)
        return rest_copy((lcs, lcr), blk, spot, which, slot, core_id)

    def rest_pair(blk, spot):
        return rest_copy((lys, lyr), blk, spot, quarter, 0, pair_id)

    def rest_blk(spot):
        at = rest_rows(spot_b, spot, quarter)
        return remote_copy(at, at, lxs.at[spot], lxr.at[spot], blk_id)

    def rest_arrived(spot):
        rest_blk(spot).start()
        rest_pair(spot_b, spot).start()
        rest_core(spot_b, spot, 0).start()

    rest_step, rest_sent = line_gather(
        lambda part: rest_ref.at[rows_at(quarter * fourth, fourth)],
        lambda block, part: rest_rows(spot_b, block, quarter),
        1,
        ls,
        lr,
        rest_arrived,
    )
    rest_own = remote_copy(
        rest_ref.at[rows_at(quarter * fourth, fourth)],
        rest_rows(spot_b, spot_s, quarter),
        lxs.at[spot_s],
        lxr.at[spot_s],
        blk_id,
    )
    rest_keep = pltpu.make_async_copy(
        rest_ref, rest_out.at[rows_at((spot_b * n_sp + spot_s) * shard, shard)], out.at[9]
    )

    def at_distance(k, call):
        if k == 0:
            call(spot_s)
        else:
            for way in range(2):

                @pl.when(gets(way, k - 1))
                def _():
                    call(spot_s - k if way == 0 else spot_s + k)

    def rest_from_blk(k):
        def one(spot):
            rest_blk(spot).wait_recv()
            rest_pair(1 - spot_b, spot).start()
            rest_core(1 - spot_b, spot, 0).start()

        at_distance(k, one)

    def rest_from_pair(k):
        def one(spot):
            if k > 0:
                rest_pair(spot_b, spot).wait_recv()
                rest_core(spot_b, spot, 1).start()
            rest_pair(1 - spot_b, spot).wait_recv()
            rest_core(1 - spot_b, spot, 1).start()

        at_distance(k, one)

    def rest_last(k):
        def one(spot):
            for slot in range(2):
                if k > 0:
                    rest_core(spot_b, spot, slot).wait_recv()
                rest_core(1 - spot_b, spot, slot).wait_recv()

        at_distance(k, one)

    def rest_done(k):
        def one(spot):
            rest_blk(spot).wait_send()
            for slot in range(2):
                if k > 0:
                    rest_core(spot_b, spot, slot).wait_send()
                rest_core(1 - spot_b, spot, slot).wait_send()
            if k > 0:
                rest_pair(spot_b, spot).wait_send()
            rest_pair(1 - spot_b, spot).wait_send()

        at_distance(k, one)

    hidden = in_ref.shape[0]
    hidden_half = hidden // 2

    def hidden_place(which, half):
        goal = in_out if which == 0 else out_out
        return goal.at[pl.ds(half * hidden_half, hidden_half)]

    def hidden_each(call):
        for which in range(2):
            for half in range(2):

                @pl.when(jnp.logical_and(core == half, pair == which))
                def _():
                    call(which, half)

    def hidden_blk(which, half):
        src = in_ref if which == 0 else out_ref
        return remote_copy(
            src.at[pl.ds(half * hidden_half, hidden_half)],
            hidden_place(which, half),
            fs.at[0],
            fr.at[0],
            blk_id,
        )

    def hidden_pair(which, half):
        at = hidden_place(which, half)
        return remote_copy(at, at, fs.at[1], fr.at[1], pair_id)

    def hidden_core(slot, which, half):
        at = hidden_place(which, half)
        return remote_copy(at, at, fs.at[2 + slot], fr.at[2 + slot], core_id)

    def hidden_next(which, half):
        hidden_blk(which, half).wait_recv()
        hidden_pair(which, half).start()
        hidden_core(0, which, half).start()

    def hidden_last(which, half):
        hidden_pair(which, half).wait_recv()
        hidden_core(1, 1 - which, half).start()

    def hidden_end(which, half):
        for slot in range(2):
            hidden_core(slot, which, half).wait_recv()
            hidden_core(slot, which, half).wait_send()
        hidden_pair(which, half).wait_send()
        hidden_blk(which, half).wait_send()

    text_rows = text_ref.shape[0]

    def text_at(blk, spot):
        return text_out.at[rows_at((blk * n_sp + spot) * text_rows, text_rows)]

    def text_blk(spot, own):
        at = text_at(spot_b, spot)
        src = text_ref if own else at
        return remote_copy(src, at, exs.at[spot], exr.at[spot], blk_id)

    text_step, text_sent = line_gather(
        lambda part: text_ref,
        lambda block, part: text_at(spot_b, block),
        1,
        es,
        er,
        lambda spot: text_blk(spot, False).start(),
    )
    text_keep = pltpu.make_async_copy(text_ref, text_at(spot_b, spot_s), out.at[10])
    cot_step, cot_sent = line_gather(
        lambda part: cot_ref,
        lambda block, part: cot_out.at[rows_at(block * rows, rows)],
        1,
        os,
        osr,
    )
    cot_keep = pltpu.make_async_copy(
        cot_ref, cot_out.at[rows_at(spot_s * rows, rows)], out.at[11]
    )

    token_step(0)
    rest_own.start()
    rest_step(0)
    for copy in (rest_keep, text_keep, cot_keep):
        copy.start()
    for copy in small_away:
        copy.wait_recv()
    keep[4].wait()
    small_pass = []
    for spot in range(n_sp):
        at = sall_ref.at[spot_b * n_sp + spot]
        copy = remote_copy(at, at, ps.at[spot], pr.at[spot], blk_id)
        copy.start()
        small_pass.append(copy)
    for j in range(3):
        keep[j].wait()
    blk_away = []
    core_away = []

    def pass_core(blk, spot, which):
        at = w_ref.at[w_rows(blk, spot, core)]
        copy = remote_copy(at, at, cs.at[which], cr.at[which], core_id)
        copy.start()
        core_away.append(copy)

    def pass_blk(step):
        at = w_ref.at[w_rows(spot_b, lax.rem(spot_s + n_sp - step, n_sp), core)]
        copy = remote_copy(at, at, xs.at[step], xr.at[step], blk_id)
        copy.start()
        blk_away.append(copy)

    pass_blk(0)
    for k in range(n_sp - 1):
        for j in range(3):
            w_away[3 * k + j].wait_recv()
        pass_blk(k + 1)
        pass_core(spot_b, lax.rem(spot_s + n_sp - k - 1, n_sp), k)

    for copy in small_pass:
        copy.wait_recv()
    lanes = wide // (2 * n_sp)
    at_row = lax.broadcasted_iota(jnp.int32, (2 * SMALL_LANES, 2 * lanes), 0)
    at_col = lax.broadcasted_iota(jnp.int32, (2 * SMALL_LANES, 2 * lanes), 1)
    place = jnp.where(at_row < SMALL_LANES, at_row, at_row - SMALL_LANES)
    goal = jnp.where(at_row < SMALL_LANES, place, place + lanes)
    chosen = jnp.logical_and(place < lanes, goal == at_col).astype(F32).astype(BF)
    for two in range(n_sp):
        both = jnp.concatenate(
            [sall_ref[2 * two, 16:, :], sall_ref[2 * two + 1, 16:, :]], axis=1
        )
        par_ref[:, 2 * lanes * two : 2 * lanes * (two + 1)] = mm(both, chosen)

    token_step(1)
    for step in range(n_sp):
        blk_away[step].wait_recv()
        pass_core(1 - spot_b, lax.rem(spot_s + n_sp - step, n_sp), n_sp - 1 + step)
    for copy in core_away:
        copy.wait_recv()
    w_keep = pltpu.make_async_copy(w_ref, w_out_ref, lo.at[5])
    w_keep.start()
    keep[3].wait()
    hidden_each(lambda which, half: hidden_blk(which, half).start())
    rest_from_blk(0)

    shift = time_ref[0:1, :] + par_ref[0:1, :]
    scale = 1.0 + (time_ref[1:2, :] + par_ref[1:2, :])
    own = lanes_at(spot_s * cols, cols)

    def project(block):
        at = rows_at(block * rows, rows)
        values = xall_ref[at, :].astype(F32)
        centre = values - jnp.mean(values, axis=-1, keepdims=True)
        spread = jnp.mean(centre * centre, axis=-1, keepdims=True)
        h1_ref[at, :] = (centre * lax.rsqrt(spread + EPS) * scale + shift).astype(BF)
        for j in range(3):
            lin = mm(h1_ref[at, :], w_ref[:, j * cols : (j + 1) * cols])
            lin = lin + par_ref[11 + j : 12 + j, own]
            if j < 2:
                lin_ref[j, at, :] = lin
                sums = exact_sums(lin * lin)
                sums_ref[spot_s, j : j + 1, lanes_at(block * rows, rows)] = sums[0:1]
            else:
                kv_ref[1, at, :] = lin.astype(BF)
        value_copy(block).start()
        angle = exact_first(
            sall_ref[spot_b * n_sp + block, 0:16, :].astype(F32), table_ref[...]
        )
        trig_ref[0, at, :] = jnp.cos(angle)
        trig_ref[1, at, :] = jnp.sin(angle)

    def kv_copy(which, block):
        return remote_copy(
            kv_ref.at[which, rows_at(block * rows, rows)],
            kv_ref.at[which, rows_at(total_rows + block * rows, rows)],
            vs.at[which * n_sp + block],
            vr.at[which * n_sp + block],
            blk_id,
        )

    def value_copy(block):
        return kv_copy(1, block)

    def arrived(k):
        first = (spot_s >= k).astype(jnp.int32)
        last = (spot_s + k < n_sp).astype(jnp.int32)

        def one(i, carry):
            ahead = jnp.logical_and(first == 1, i == 0)
            project(jnp.where(ahead, spot_s - k, spot_s + k))
            return carry

        lax.fori_loop(0, first + last, one, 0)

    project(spot_s)
    rest_step(1)
    arrived(1)
    token_step(2)
    rest_from_blk(1)
    arrived(2)
    rest_step(2)
    token_step(3)
    arrived(3)

    sums_away = []
    for k in range(n_sp - 1):
        copy = remote_copy(
            sums_ref.at[spot_s], sums_ref.at[spot_s], qs.at[k], qr.at[k], line[k]
        )
        copy.start()
        sums_away.append(copy)
    for copy in sums_away:
        copy.wait_recv()
    squares = sums_ref[0]
    for k in range(1, n_sp):
        squares = squares + sums_ref[k]
    rho_rows = lax.rsqrt(squares / wide + EPS)
    sums_ref[n_sp] = rho_rows

    def turn_block(which, block):
        at = rows_at(block * rows, rows)
        rho = exact_first(sums_ref[n_sp, :, lanes_at(block * rows, rows)], row_pick(which))
        rho_ref[which, at, :] = rho
        cosine = trig_ref[0, at, :]
        sine = trig_ref[1, at, :]
        for h in range(heads_here):
            gain = par_ref[6 + which : 7 + which, lanes_at(spot_s * cols + h * HD, HD)]
            value = lin_ref[which, at, h * HD : (h + 1) * HD] * rho * gain
            value = turned(value, cosine, sine).astype(BF)
            if which == 0:
                q_ref[at, h * HD : (h + 1) * HD] = value
            else:
                kv_ref[0, at, h * HD : (h + 1) * HD] = value

    def turn_key(block, carry):
        turn_block(1, block)
        kv_copy(0, block).start()
        return carry

    def turn_query(block, carry):
        turn_block(0, block)
        return carry

    lax.fori_loop(0, n_sp, turn_key, 0)
    lax.fori_loop(0, n_sp, turn_query, 0)
    text_blk(spot_s, True).start()
    text_step(0)
    rest_from_pair(0)
    rest_step(3)
    rest_from_blk(2)
    cot_step(0)
    saves = [
        pltpu.make_async_copy(h1_ref, h1_out, out.at[0]),
        pltpu.make_async_copy(lin_ref, lin_out, out.at[1]),
        pltpu.make_async_copy(rho_ref, rho_out, out.at[2]),
        pltpu.make_async_copy(trig_ref, trig_out, out.at[3]),
        pltpu.make_async_copy(q_ref, q_out, out.at[4]),
    ]
    for copy in saves:
        copy.start()
    score_scale = HD ** (-0.5)

    def attend(block, h, part):
        at = rows_at(block * rows, rows)
        head = pl.ds(h * HD, HD)
        keys = pl.ds(part * total_rows, total_rows)
        scores = mm_t(q_ref[at, head], kv_ref[0, keys, head]) * score_scale
        top = jnp.max(scores, -1, keepdims=True)
        if part == 1:
            before = stat_ref[0, h, at, 0:1]
            top = jnp.maximum(top, before)
        raised = jnp.exp(scores - top)
        total = jnp.sum(raised, -1, keepdims=True)
        result = mm(raised.astype(BF), kv_ref[1, keys, head])
        if part == 0:
            stat_ref[0, h, at, :] = jnp.broadcast_to(top, (rows, 128))
            stat_ref[1, h, at, :] = jnp.broadcast_to(total, (rows, 128))
            acc_ref[h, at, :] = result
        else:
            fade = jnp.exp(before - top)
            total = total + fade * stat_ref[1, h, at, 0:1]
            result = result + fade * acc_ref[h, at, :]
            att_ref[at, head] = (result / total).astype(BF)
            stat_ref[0, h, at, :] = jnp.broadcast_to(top + jnp.log(total), (rows, 128))

    def first_pass(block, carry):
        for h in range(heads_here):
            attend(block, h, 0)
        return carry

    lax.fori_loop(0, n_sp, first_pass, 0)
    hidden_each(hidden_next)

    def key_wait(block, carry):
        kv_copy(0, block).wait_recv()
        kv_copy(1, block).wait_recv()
        return carry

    lax.fori_loop(0, n_sp, key_wait, 0)
    kv_save = pltpu.make_async_copy(kv_ref, kv_out, out.at[5])
    kv_save.start()
    rest_from_blk(3)
    rest_from_pair(1)

    def att_copy(step):
        block = lax.rem(spot_s + step, n_sp)
        return remote_copy(
            att_ref.at[rows_at(block * rows, rows)],
            tok_out.at[:, lanes_at(spot_s * cols, cols)],
            ts.at[step - 1],
            tr.at[step - 1],
            {SP: block},
        )

    for step in list(range(1, n_sp)) + [0]:
        block = lax.rem(spot_s + step, n_sp)

        def one_head(block=block):
            for h in range(heads_here):
                attend(block, h, 1)

        one_head()
        if step > 0:
            att_copy(step).start()
        if step == 1:
            text_step(1)
            cot_step(1)
        if step == 2:
            rest_from_pair(2)
    own_att = pltpu.make_async_copy(
        att_ref.at[rows_at(spot_s * rows, rows)],
        tok_out.at[:, lanes_at(spot_s * cols, cols)],
        out.at[6],
    )
    own_att.start()
    saves.append(own_att)
    last = [
        pltpu.make_async_copy(stat_ref.at[0], lse_out, out.at[7]),
        pltpu.make_async_copy(att_ref, att_out, out.at[8]),
    ]
    for copy in last:
        copy.start()
    text_step(2)
    cot_step(2)
    hidden_each(hidden_last)
    text_step(3)
    rest_from_pair(3)
    cot_step(3)
    for k in range(n_sp):
        rest_last(k)
        at_distance(k, lambda spot: text_blk(spot, False).wait_recv())
    for step in range(1, n_sp):
        att_copy(step).wait_recv()
    for copy in (rest_keep, text_keep, cot_keep):
        copy.wait()
    for k in range(n_sp):
        rest_done(k)
        at_distance(k, lambda spot: text_blk(spot, False).wait_send())
    hidden_each(hidden_end)
    rest_sent()
    text_sent()
    cot_sent()
    token_sent()
    for copy in saves + last + [kv_save, w_keep]:
        copy.wait()
    for copy in small_away + w_away + blk_away + core_away + small_pass + sums_away:
        copy.wait_send()

    def kv_sent(block, carry):
        kv_copy(0, block).wait_send()
        kv_copy(1, block).wait_send()
        return carry

    lax.fori_loop(0, n_sp, kv_sent, 0)
    for step in range(1, n_sp):
        att_copy(step).wait_send()


def front(x_own, small_own, qkv, rest, shard_in, shard_out, text, cot, time_rows):
    n_sp = lax.axis_size(SP)
    groups = 2 * n_sp
    rows, width = x_own.shape
    total = n_sp * rows
    cols = qkv.shape[1] // 3 // n_sp
    heads_here = cols // HD
    table = np.zeros((16, HD), np.float32)
    pairs = rope_tables(HD)
    table[:3, : HD // 2] = pairs
    table[:3, HD // 2 :] = pairs
    any_place = pl.BlockSpec(memory_space=pl.ANY)
    in_vmem = pl.BlockSpec(memory_space=pltpu.VMEM)
    dma = pltpu.SemaphoreType.DMA
    line = n_sp - 1
    counts = [6, 4 * line, 4 * line, line, line, 3 * line, 3 * line, n_sp, n_sp]
    counts += [2 * n_sp - 1, 2 * n_sp - 1, n_sp, n_sp, 2 * n_sp, 2 * n_sp, line, line]
    counts += [line, line, 12]
    counts += [2 * line, 2 * line, n_sp, n_sp, groups, groups, 2 * groups, 2 * groups, 4, 4]
    counts += [2 * line, 2 * line, n_sp, n_sp, 2 * line, 2 * line]
    shape = jax.ShapeDtypeStruct
    outs = (
        shape((PARAM_ROWS, width), F32),
        shape((total, width), BF),
        shape((width, 3 * cols), BF),
        shape((2, total, cols), F32),
        shape((2, total, HD), F32),
        shape((2, total, HD), F32),
        shape((total, cols), BF),
        shape((2, 2 * total, cols), BF),
        shape((heads_here, total, HD), F32),
        shape((total, cols), BF),
        shape((rows, width), BF),
        shape((groups * rest.shape[0], rest.shape[1]), BF),
        shape(shard_in.shape, BF),
        shape(shard_out.shape, BF),
        shape((groups * text.shape[0], width), BF),
        shape((total, width), BF),
    )
    vmem = pltpu.VMEM
    return pl.pallas_call(
        functools.partial(front_kernel, n_sp),
        out_shape=outs,
        in_specs=[any_place] * 8 + [in_vmem] * 2,
        out_specs=(in_vmem,) + (any_place,) * (len(outs) - 1),
        scratch_shapes=[
            vmem((total, width), BF),
            vmem((groups, SMALL_ROWS, SMALL_LANES), BF),
            vmem((width, 3 * cols), BF),
            vmem((2, total, cols), F32),
            vmem((n_sp + 1, 8, total), F32),
            vmem((2, total, HD), F32),
            vmem((2, total, HD), F32),
            vmem((total, cols), BF),
            vmem((2, 2 * total, cols), BF),
            vmem((heads_here, total, HD), F32),
            vmem((2, heads_here, total, HD), F32),
            vmem((total, cols), BF),
            vmem((total, width), BF),
        ]
        + [dma((count,)) for count in counts],
        compiler_params=pltpu.CompilerParams(
            collective_id=1, has_side_effects=True, vmem_limit_bytes=56 * 2**20
        ),
    )(x_own, small_own, qkv, rest, shard_in, shard_out, text, cot, time_rows, jnp.asarray(table))


def normal(values):
    centre = values - jnp.mean(values, axis=-1, keepdims=True)
    spread = lax.rsqrt(jnp.mean(centre * centre, axis=-1, keepdims=True) + EPS)
    return centre * spread, spread


def normal_back(normed, spread, grad):
    lean = jnp.mean(grad, axis=-1, keepdims=True)
    tilt = jnp.mean(grad * normed, axis=-1, keepdims=True)
    return spread * (grad - lean - normed * tilt)


def column_total(values):
    return jnp.sum(values.astype(F32), 0, keepdims=True)


def wide_dot(dst, left, right, call=mm, tile=512, add=None):
    across = dst.shape[-1]
    for start in range(0, across, tile):
        at = pl.ds(start, min(tile, across - start))
        value = call(left, right[:, at])
        if add is not None:
            value = value + add[:, at]
        dst[:, at] = value.astype(dst.dtype)


def wide_dot_t(dst, left, right, tile=512, add=None):
    across = dst.shape[-1]
    for start in range(0, across, tile):
        at = pl.ds(start, min(tile, across - start))
        value = mm_t(left, right[at, :])
        if add is not None:
            value = value + add[:, at]
        dst[:, at] = value.astype(dst.dtype)


def rest_loads(rest_ref, goals, sems, order):
    width = goals[0].shape[1]
    copies = {}
    for slot in order:
        copies[slot] = pltpu.make_async_copy(
            rest_ref.at[:, pl.ds(slot * width, width)], goals[slot], sems.at[slot]
        )
        copies[slot].start()
    return copies


def own_kernel(
    len_ref,
    rest_ref,
    x_ref,
    att_ref,
    text_ref,
    time_ref,
    par_ref,
    a_out,
    one_out,
    cin_out,
    ql_out,
    kl_out,
    q_out,
    kv_out,
    lse_out,
    oc_out,
    two_out,
    h2_out,
    w_o,
    w_co,
    w_cq,
    w_ck,
    w_cv,
    sems,
):
    loads = rest_loads(rest_ref, (w_o, w_co, w_cq, w_ck, w_cv), sems, (0, 2, 3, 4, 1))
    mods = time_ref[...] + par_ref[0:6, :]
    width = x_ref.shape[1]
    loads[0].wait()
    wide_dot(a_out, att_ref[...], w_o, add=par_ref.at[14:15])
    x_one = x_ref[...].astype(F32) + mods[2:3] * a_out[...]
    one_out[...] = x_one
    normed, _ = normal(x_one)
    cin_out[...] = (normed * par_ref[8:9, :] + par_ref[19:20, :]).astype(BF)
    loads[2].wait()
    wide_dot(ql_out, cin_out[...], w_cq, add=par_ref.at[15:16])
    value = ql_out[...]
    rho = lax.rsqrt(jnp.mean(value * value, axis=-1, keepdims=True) + EPS)
    q_out[...] = (value * rho * par_ref[9:10, :]).astype(BF)
    loads[3].wait()
    wide_dot(kl_out, text_ref[...], w_ck, add=par_ref.at[16:17])
    value = kl_out[...]
    rho = lax.rsqrt(jnp.mean(value * value, axis=-1, keepdims=True) + EPS)
    kv_out[0] = (value * rho * par_ref[10:11, :]).astype(BF)
    loads[4].wait()
    wide_dot(kv_out.at[1], text_ref[...], w_cv, add=par_ref.at[17:18])
    texts = text_ref.shape[0]
    rows = x_ref.shape[0]
    valid = lax.broadcasted_iota(jnp.int32, (rows, texts), 1) < len_ref[0]

    def attend(h, carry):
        head = lanes_at(h * HD, HD)
        scores = mm_t(q_out[:, head], kv_out[0, :, head]) * (HD ** (-0.5))
        scores = jnp.where(valid, scores, NEG)
        top = jnp.max(scores, -1, keepdims=True)
        raised = jnp.exp(scores - top)
        total = jnp.sum(raised, -1, keepdims=True)
        result = mm((raised / total).astype(BF), kv_out[1, :, head])
        oc_out[:, head] = result.astype(BF)
        lse_out[h] = jnp.broadcast_to(top + jnp.log(total), (rows, HD))
        return carry

    lax.fori_loop(0, width // HD, attend, 0)
    loads[1].wait()
    wide_dot(two_out, oc_out[...], w_co, add=par_ref.at[18:19])
    x_two = one_out[...] + two_out[...]
    two_out[...] = x_two
    normed, _ = normal(x_two)
    h2_out[...] = (normed * (1.0 + mods[4:5]) + mods[3:4]).astype(BF)


def own_tokens(lengths, rest, x_own, att_tok, text, time_rows, params):
    rows, width = x_own.shape
    texts = text.shape[0]
    shape = jax.ShapeDtypeStruct
    in_vmem = pl.BlockSpec(memory_space=pltpu.VMEM)
    weight = pltpu.VMEM((width, width), BF)
    names = ("a", "one", "cin", "ql", "kl", "q", "kv", "lse", "oc", "two", "h2")
    outs = (
        shape((rows, width), F32),
        shape((rows, width), F32),
        shape((rows, width), BF),
        shape((rows, width), F32),
        shape((texts, width), F32),
        shape((rows, width), BF),
        shape((2, texts, width), BF),
        shape((width // HD, rows, HD), F32),
        shape((rows, width), BF),
        shape((rows, width), F32),
        shape((rows, width), BF),
    )
    results = pl.pallas_call(
        own_kernel,
        out_shape=outs,
        in_specs=[
            pl.BlockSpec(memory_space=pltpu.SMEM),
            pl.BlockSpec(memory_space=pl.ANY),
        ]
        + [in_vmem] * 5,
        out_specs=(in_vmem,) * len(outs),
        scratch_shapes=[weight] * 5 + [pltpu.SemaphoreType.DMA((5,))],
        compiler_params=pltpu.CompilerParams(vmem_limit_bytes=58 * 2**20),
    )(lengths, rest, x_own, att_tok, text, time_rows, params)
    return types.SimpleNamespace(**dict(zip(names, results)))


def own_back_kernel(names, *refs):
    ref = types.SimpleNamespace(**dict(zip(names, refs)))
    sems, out_sem = ref.sems, ref.out_sem
    w_a, w_b, w_c = (getattr(ref, name) for name in ("w_a", "w_b", "w_c"))
    loads = rest_loads(ref.rest, (w_a, w_a, w_b, w_c, w_b), sems, (1, 2, 3))
    par_ref, sums = ref.par, ref.sums
    mods = ref.time[...] + par_ref[0:6, :]
    rows, width = ref.x_two.shape
    texts = ref.text_in.shape[0]
    sums[...] = jnp.zeros(sums.shape, F32)
    grad_y = ref.cot[...].astype(F32)
    sums[20:21, :] = column_total((grad_y * mods[5:6]).astype(BF))
    d_rows = ref.d_rows[...]
    normed, spread = normal(ref.x_two[...])
    sums[3:4, :] = column_total(d_rows)
    sums[4:5, :] = column_total(d_rows * normed)
    dx_ref = ref.dx
    dx_ref[...] = grad_y + normal_back(normed, spread, d_rows * (1.0 + mods[4:5]))
    low_ref = ref.low
    low_ref[...] = dx_ref[...].astype(BF)
    sums[18:19, :] = column_total(low_ref[...])

    saves = []

    def weight_grad(name, left, right):
        stage = ref.stage
        tile = 384
        for k, start in enumerate(range(0, width, tile)):
            slot = len(saves) % 2
            if len(saves) >= 2:
                saves[-2].wait()
            stage[slot] = mm_first(left[:, start : start + tile], right[...]).astype(BF)
            copy = pltpu.make_async_copy(
                stage.at[slot], getattr(ref, name).at[pl.ds(start, tile)], out_sem.at[slot]
            )
            copy.start()
            saves.append(copy)

    weight_grad("co", ref.oc, low_ref)
    loads[1].wait()
    doc_ref = ref.doc
    wide_dot_t(doc_ref, low_ref[...], w_a)
    loads.update(rest_loads(ref.rest, (w_a,), sems, (0,)))
    dq_ref, dkv_ref = ref.dq, ref.dkv
    q_ref, kv_ref = ref.q, ref.kv
    scale = HD ** (-0.5)
    valid = lax.broadcasted_iota(jnp.int32, (rows, texts), 1) < ref.len[0]

    def attend(h, carry):
        head = lanes_at(h * HD, HD)
        query, keys, grad = q_ref[:, head], kv_ref[0, :, head], doc_ref[:, head]
        scores = mm_t(query, keys) * scale
        scores = jnp.where(valid, scores, NEG)
        probs = jnp.exp(scores - ref.lse[h, :, 0:1])
        dkv_ref[1, :, head] = mm_first(probs.astype(BF), grad)
        d_probs = mm_t(grad, kv_ref[1, :, head])
        lean = jnp.sum(probs * d_probs, -1, keepdims=True)
        d_scores = (probs * (d_probs - lean)).astype(BF)
        dq_ref[:, head] = mm(d_scores, keys) * scale
        dkv_ref[0, :, head] = mm_first(d_scores, query) * scale
        return carry

    lax.fori_loop(0, width // HD, attend, 0)

    def rms_back(value, gain, grad):
        rho = lax.rsqrt(jnp.mean(value * value, axis=-1, keepdims=True) + EPS)
        lean = jnp.mean(value * gain * grad, axis=-1, keepdims=True)
        return (
            rho * gain * grad - value * (rho * rho * rho * lean),
            jnp.sum(grad * value * rho, 0, keepdims=True),
        )

    back_q, gain_q = rms_back(ref.ql[...], par_ref[9:10, :], dq_ref[...])
    low_ref[...] = back_q.astype(BF)
    sums[9:10, :] = gain_q
    sums[15:16, :] = column_total(low_ref[...])
    loads[2].wait()
    wide_dot_t(dq_ref, low_ref[...], w_b)
    loads.update(rest_loads(ref.rest, (w_b,) * 5, sems, (4,)))
    d_cin = dq_ref[...]
    normed, spread = normal(ref.x_one[...])
    sums[8:9, :] = column_total(d_cin * normed)
    sums[19:20, :] = column_total(d_cin)
    dx_ref[...] += normal_back(normed, spread, d_cin * par_ref[8:9, :])
    weight_grad("cq", ref.cin, low_ref)
    sums[2:3, :] = column_total(dx_ref[...] * ref.a[...])
    low_ref[...] = (dx_ref[...] * mods[2:3]).astype(BF)
    sums[14:15, :] = column_total(low_ref[...])
    loads[0].wait()
    wide_dot_t(ref.d_att, low_ref[...], w_a)
    weight_grad("o", ref.att, low_ref)
    back_k, gain_k = rms_back(ref.kl[...], par_ref[10:11, :], dkv_ref[0])
    sums[10:11, :] = gain_k
    klow_ref, vlow_ref = ref.klow, ref.vlow
    klow_ref[...] = back_k.astype(BF)
    vlow_ref[...] = dkv_ref[1].astype(BF)
    sums[16:17, :] = column_total(klow_ref[...])
    sums[17:18, :] = column_total(vlow_ref[...])
    weight_grad("ck", ref.text_in, klow_ref)
    weight_grad("cv", ref.text_in, vlow_ref)
    loads[3].wait()
    wide_dot_t(dkv_ref.at[0], klow_ref[...], w_c)
    loads[4].wait()
    wide_dot_t(ref.text_part, vlow_ref[...], w_b, add=dkv_ref.at[0])
    for copy in saves[-2:]:
        copy.wait()


def own_back(**values):
    arrays = types.SimpleNamespace(**values)
    shape = jax.ShapeDtypeStruct
    rows, width = arrays.x_two.shape
    texts = arrays.text_in.shape[0]
    in_any = ["rest"]
    ins = ["x_two", "x_one", "d_rows", "cot", "time", "par", "a", "cin", "ql", "kl", "q", "kv"]
    ins += ["lse", "oc", "att", "text_in"]
    any_outs = {name: shape((width, width), BF) for name in ("o", "co", "cq", "ck", "cv")}
    outs = dict(
        d_att=shape((rows, width), BF),
        dx=shape((rows, width), F32),
        text_part=shape((texts, width), BF),
        sums=shape((32, width), F32),
    )
    vmem = pltpu.VMEM
    weight = vmem((width, width), BF)
    scratch = {name: weight for name in ("w_a", "w_b", "w_c")}
    scratch.update(
        dict(
            low=vmem((rows, width), BF),
            doc=vmem((rows, width), BF),
            dq=vmem((rows, width), F32),
            dkv=vmem((2, texts, width), F32),
            klow=vmem((texts, width), BF),
            vlow=vmem((texts, width), BF),
            stage=vmem((2, 384, width), BF),
            sems=pltpu.SemaphoreType.DMA((5,)),
            out_sem=pltpu.SemaphoreType.DMA((2,)),
        )
    )
    any_place = pl.BlockSpec(memory_space=pl.ANY)
    in_vmem = pl.BlockSpec(memory_space=pltpu.VMEM)
    names = ["len"] + in_any + ins + list(any_outs) + list(outs) + list(scratch)
    results = pl.pallas_call(
        functools.partial(own_back_kernel, names),
        out_shape=tuple(any_outs.values()) + tuple(outs.values()),
        in_specs=[pl.BlockSpec(memory_space=pltpu.SMEM), any_place] + [in_vmem] * len(ins),
        out_specs=(any_place,) * len(any_outs) + (in_vmem,) * len(outs),
        scratch_shapes=list(scratch.values()),
        compiler_params=pltpu.CompilerParams(vmem_limit_bytes=60 * 2**20),
    )(*[getattr(arrays, name) for name in ["len"] + in_any + ins])
    return types.SimpleNamespace(**dict(zip(list(any_outs) + list(outs), results)))


def feed_kernel(n_sp, names, *refs):
    ref = types.SimpleNamespace(**dict(zip(names, refs)))
    zs, zr, ds, dr, local, cs, cr, saves_sem = (
        getattr(ref, name) for name in ("zs", "zr", "ds", "dr", "local", "cs", "cr", "saves")
    )
    spot_d = lax.axis_index(DP)
    spot_s = lax.axis_index(SP)
    core = lax.rem(spot_d, 2)
    core_id = {DP: spot_d + 1 - 2 * core}
    line = [{SP: lax.rem(spot_s + step, n_sp)} for step in range(1, n_sp)]
    h2_ref, all_ref = ref.h2, ref.h2_all
    rows, width = h2_ref.shape
    hidden = ref.in_own.shape[0]
    win, wout = ref.win, ref.wout
    meet(line + [core_id])

    pieces = 2
    piece = rows // pieces

    def token_copy(way, k, part):
        block = spot_s - k if way == 0 else spot_s + k
        at = all_ref.at[rows_at(block * rows + part * piece, piece)]
        src = h2_ref.at[pl.ds(part * piece, piece)] if k == 0 else at
        target = {SP: spot_s + 1 if way == 0 else spot_s - 1}
        index = (way * (n_sp - 1) + k) * pieces + part
        return remote_copy(src, at, zs.at[index], zr.at[index], target)

    def sends(way, k):
        if way == 0:
            return jnp.logical_and(spot_s < n_sp - 1, spot_s >= k)
        return jnp.logical_and(spot_s > 0, spot_s + k < n_sp)

    def gets(way, k):
        return spot_s > k if way == 0 else spot_s + k + 1 < n_sp

    def token_step(k):
        for part in range(pieces):
            for way in range(2):
                if k > 0:

                    @pl.when(gets(way, k - 1))
                    def _():
                        token_copy(way, k - 1, part).wait_recv()

                if k < n_sp - 1:

                    @pl.when(sends(way, k))
                    def _():
                        token_copy(way, k, part).start()

    token_step(0)
    keep = pltpu.make_async_copy(h2_ref, all_ref.at[rows_at(spot_s * rows, rows)], local.at[0])
    keep.start()
    loads = [
        pltpu.make_async_copy(getattr(ref, src), goal.at[pl.ds(part * hidden, hidden)], local.at[1 + k])
        for k, (src, goal, part) in enumerate(
            (("in_own", win, 0), ("in_other", win, 1), ("out_own", wout, 0), ("out_other", wout, 1))
        )
    ]
    for copy in loads:
        copy.start()
    gate = ref.time[5:6, :] + ref.par[5:6, :]
    ref.du_sums[...] = jnp.zeros(ref.du_sums.shape, F32)
    cot_ref, dz_ref, g_ref, du_ref = ref.cot, ref.dz, ref.g, ref.du
    z_ref, part_ref, recv_ref, own_ref = ref.z, ref.part, ref.recv, ref.own
    tiles = []
    start = 0
    while start < 2 * hidden:
        tiles.append((start, min(768, 2 * hidden - start)))
        start += 768
    bend = (2.0 / np.pi) ** 0.5
    keep.wait()
    for copy in loads:
        copy.wait()

    def near(k):
        first = (spot_s >= k).astype(jnp.int32)
        return first, first + (spot_s + k < n_sp).astype(jnp.int32)

    def grad_copy(block, owner):
        return remote_copy(
            part_ref.at[block],
            recv_ref.at[spot_s],
            ds.at[block],
            dr.at[owner],
            {SP: block},
        )

    def one(i, carry):
        block = spot_s
        before = jnp.int32(1)
        for k in range(1, n_sp):
            first, count = near(k)

            @pl.when(i == before)
            def _(k=k):
                token_step(k)

            here = jnp.logical_and(i >= before, i < before + count)
            ahead = jnp.logical_and(first == 1, i == before)
            block = jnp.where(here, jnp.where(ahead, spot_s - k, spot_s + k), block)
            before = before + count
        at = rows_at(block * rows, rows)
        dz_ref[at, :] = (cot_ref[at, :].astype(F32) * gate).astype(BF)
        for start, size in tiles:
            place = pl.ds(start, size)
            u = mm_t(all_ref[at, :], win[place, :]) + ref.bias[:, place]
            cube = bend * (u + 0.044715 * (u * u * u))
            t = jnp.tanh(cube)
            g_ref[at, place] = (0.5 * u * (1.0 + t)).astype(BF)
            slope = 0.5 * (1.0 + t) + (0.5 * bend) * u * (1.0 - t * t) * (
                1.0 + (3 * 0.044715) * (u * u)
            )
            grad = (mm_t(dz_ref[at, :], wout[place, :]) * slope).astype(BF)
            du_ref[at, place] = grad
            ref.du_sums[:, place] += column_total(grad)
        for start in range(0, width, 512):
            place = pl.ds(start, 512)
            value = mm(du_ref[at, :], win[:, place])
            part_ref[block, :, place] = value.astype(BF)

            @pl.when(i == 0)
            def _():
                own_ref[:, place] = value

        @pl.when(i > 0)
        def _():
            grad_copy(block, spot_s).start()

        for start in range(0, width, 512):
            place = pl.ds(start, 512)
            z_ref[block, :, place] = mm(g_ref[at, :], wout[:, place]).astype(BF)
        return carry

    lax.fori_loop(0, n_sp, one, 0)
    z_save = pltpu.make_async_copy(z_ref, ref.z_out, local.at[5])
    z_save.start()

    def weight_grad(goal, left, right):
        start = 0
        while start < 2 * hidden:
            size = min(256, 2 * hidden - start)
            goal[start : start + size, :] = mm_first(
                left[:, start : start + size], right[...]
            ).astype(BF)
            start += size

    half = hidden // 2
    core_copies = []

    def core_hop(which, goal):
        for part in range(2):
            copy = remote_copy(
                goal.at[rows_at(part * hidden + (1 - core) * half, half)],
                ref.core_recv.at[which, part],
                cs.at[2 * which + part],
                cr.at[2 * which + part],
                core_id,
            )
            copy.start()
            core_copies.append(copy)

    weight_grad(win, du_ref, all_ref)
    core_hop(0, win)
    weight_grad(wout, g_ref, dz_ref)
    core_hop(1, wout)
    low_ref = ref.core_recv
    out_copies = []
    chunk = half // 5
    for which, goal in enumerate((win, wout)):
        for part in range(2):
            core_copies[2 * which + part].wait_recv()
            for k in range(5):
                at = rows_at(part * hidden + core * half + k * chunk, chunk)
                value = goal[at, :].astype(F32) + low_ref[
                    which, part, k * chunk : (k + 1) * chunk
                ].astype(F32)
                low_ref[which, part, k * chunk : (k + 1) * chunk] = value.astype(BF)
            copy = pltpu.make_async_copy(
                low_ref.at[which, part],
                ref.f_out.at[which, part],
                saves_sem.at[2 * which + part],
            )
            copy.start()
            out_copies.append(copy)
    for step in range(1, n_sp):
        other = lax.rem(spot_s + step, n_sp)
        grad_copy(other, other).wait_recv()
    total = own_ref[...]
    for step in range(1, n_sp):
        total = total + recv_ref[lax.rem(spot_s + step, n_sp)].astype(F32)
    ref.d_rows[...] = total
    for copy in out_copies + [z_save]:
        copy.wait()
    for copy in core_copies:
        copy.wait_send()
    for step in range(1, n_sp):
        other = lax.rem(spot_s + step, n_sp)
        grad_copy(other, other).wait_send()
    for k in range(n_sp - 1):
        for part in range(pieces):
            for way in range(2):

                @pl.when(sends(way, k))
                def _():
                    token_copy(way, k, part).wait_send()


def feed(**values):
    arrays = types.SimpleNamespace(**values)
    n_sp = lax.axis_size(SP)
    shape = jax.ShapeDtypeStruct
    rows, width = arrays.h2.shape
    hidden = arrays.in_own.shape[0]
    total = n_sp * rows
    ins_any = ["in_own", "in_other", "out_own", "out_other", "h2"]
    ins = ["cot", "bias", "time", "par"]
    any_outs = dict(
        z_out=shape((n_sp, rows, width), BF),
        f_out=shape((2, 2, hidden // 2, width), BF),
    )
    outs = {"d_rows": shape((rows, width), F32), "du_sums": shape((1, 2 * hidden), F32)}
    vmem = pltpu.VMEM
    dma = pltpu.SemaphoreType.DMA
    scratch = dict(
        h2_all=vmem((total, width), BF),
        win=vmem((2 * hidden, width), BF),
        wout=vmem((2 * hidden, width), BF),
        dz=vmem((total, width), BF),
        g=vmem((total, 2 * hidden), BF),
        du=vmem((total, 2 * hidden), BF),
        z=vmem((n_sp, rows, width), BF),
        part=vmem((n_sp, rows, width), BF),
        recv=vmem((n_sp, rows, width), BF),
        own=vmem((rows, width), F32),
        core_recv=vmem((2, 2, hidden // 2, width), BF),
        zs=dma((4 * (n_sp - 1),)),
        zr=dma((4 * (n_sp - 1),)),
        ds=dma((n_sp,)),
        dr=dma((n_sp,)),
        local=dma((6,)),
        cs=dma((4,)),
        cr=dma((4,)),
        saves=dma((4,)),
    )
    any_place = pl.BlockSpec(memory_space=pl.ANY)
    in_vmem = pl.BlockSpec(memory_space=pltpu.VMEM)
    names = ins_any + ins + list(any_outs) + list(outs) + list(scratch)
    results = pl.pallas_call(
        functools.partial(feed_kernel, n_sp, names),
        out_shape=tuple(any_outs.values()) + tuple(outs.values()),
        in_specs=[any_place] * len(ins_any) + [in_vmem] * len(ins),
        out_specs=(any_place,) * len(any_outs) + (in_vmem,) * len(outs),
        scratch_shapes=list(scratch.values()),
        compiler_params=pltpu.CompilerParams(
            collective_id=3, has_side_effects=True, vmem_limit_bytes=60 * 2**20
        ),
    )(*[getattr(arrays, name) for name in ins_any + ins])
    return types.SimpleNamespace(**dict(zip(list(any_outs) + list(outs), results)))


class Later:
    def __init__(self, make):
        self.make = make

    def wait_recv(self):
        self.make().wait_recv()

    def wait_send(self):
        self.make().wait_send()


def back_kernel(n_sp, n_dp, names, *refs):
    ref = types.SimpleNamespace(**dict(zip(names, refs)))
    sem_send, sem_recv, sem_local = ref.send, ref.recv, ref.local
    spot_d = lax.axis_index(DP)
    spot_b = lax.axis_index(BLK)
    spot_s = lax.axis_index(SP)
    core = lax.rem(spot_d, 2)
    pair = lax.rem(spot_d // 2, 2)

    def dp_id(bit):
        return {DP: spot_d + bit - 2 * bit * lax.rem(spot_d // bit, 2)}

    bits = []
    bit = 4
    while bit < n_dp:
        bits.append(bit)
        bit *= 2
    core_id, pair_id, blk_id = dp_id(1), dp_id(2), {BLK: 1 - spot_b}
    line = [{SP: lax.rem(spot_s + step, n_sp)} for step in range(1, n_sp)]
    used = [0]
    sent = []

    def send(src, dst, target, view=None):
        index = used[0]
        used[0] += 1
        copy = remote_copy(src, dst, sem_send.at[index], sem_recv.at[index], target)
        copy.start()
        if view is not None:
            copy = Later(
                lambda: remote_copy(
                    view(), view(), sem_send.at[index], sem_recv.at[index], target
                )
            )
        sent.append(copy)
        return copy

    def add_blocks(dst, sources):
        lead = len(dst.shape) - 2

        def body(*blocks):
            total = blocks[0][...].astype(F32)
            for block in blocks[1:-1]:
                total = total + block[...].astype(F32)
            blocks[-1][...] = total.astype(blocks[-1].dtype)

        if lead == 0:
            grid = (dst.shape[0] // 16,)
            spec = pl.BlockSpec((16, dst.shape[1]), lambda place: (place, 0))
        else:
            group = 1
            each = 2 * int(np.prod(dst.shape[1:]))
            while dst.shape[0] % (2 * group) == 0 and 2 * group * each <= 700_000:
                group *= 2
            grid = (dst.shape[0] // group,)
            spec = pl.BlockSpec(
                (group,) + tuple(dst.shape[1:]), lambda place: (place,) + (0,) * (lead + 1)
            )
        pltpu.emit_pipeline(
            body,
            grid=grid,
            in_specs=[spec] * len(sources),
            out_specs=[spec],
        )(*sources, dst)

    meet(line + [core_id, pair_id, blk_id] + [dp_id(bit) for bit in bits])
    d_att, do_ref = ref.d_att, ref.do
    rows = d_att.shape[0]
    total_rows = n_sp * rows
    cols = do_ref.shape[1]
    heads_here = cols // HD
    width = d_att.shape[1]

    def tok(block):
        return rows_at(block * rows, rows)

    do_own = pltpu.make_async_copy(
        d_att.at[:, lanes_at(spot_s * cols, cols)], do_ref.at[tok(spot_s)], sem_local.at[0]
    )
    do_own.start()
    do_away = [
        send(
            d_att.at[:, lanes_at(lax.rem(spot_s + step, n_sp) * cols, cols)],
            do_ref.at[tok(spot_s)],
            line[step - 1],
        )
        for step in range(1, n_sp)
    ]
    groups = ("co", "ckv")
    hop = {}
    for name in groups:
        hop[name] = send(getattr(ref, name).at[:, 1 - core], getattr(ref, name + "_rc"), core_id)
    hop["text"] = send(ref.text.at[1 - spot_b], ref.text_rx, blk_id)

    blocks8 = 2 * n_sp

    def core_done(name):
        hop[name].wait_recv()
        add_blocks(getattr(ref, name + "_kc"), [getattr(ref, name).at[:, core], getattr(ref, name + "_rc")])

    score_scale = HD ** (-0.5)
    dq_ref, dkv_ref = ref.dq, ref.dkv

    def ff_last(name):
        at = getattr(ref, name + "_out").at[core]
        ry = getattr(ref, name + "_ry")
        kx = getattr(ref, name + "_kx")
        hop[name].wait_recv()
        for k in range(len(bits) + 1):
            goal = at if k == len(bits) else getattr(ref, name + "_ky").at[k]
            source = kx if k == 0 else getattr(ref, name + "_ky").at[k - 1]
            add_blocks(goal, [source, ry.at[k]])
            if k < len(bits):
                send(goal, ry.at[k + 1], dp_id(bits[k])).wait_recv()
        hop[name] = send(at, at, core_id)

    def pair_done(name, go=True):
        if name in hop:
            hop[name].wait_recv()
            add_blocks(getattr(ref, name + "_ky"), [getattr(ref, name + "_kc").at[:, pair], getattr(ref, name + "_ry")])
            del hop[name]
        if not go:
            return
        hop[name] = send(
            getattr(ref, name + "_ky").at[pl.ds((1 - spot_b) * n_sp, n_sp)], getattr(ref, name + "_rx"), blk_id
        )

    def blk_done(name):
        hop[name].wait_recv()
        own_blk = getattr(ref, name + "_ky").at[pl.ds(spot_b * n_sp, n_sp)]
        add_blocks(getattr(ref, name + "_kx"), [own_blk, getattr(ref, name + "_rx")])

    def line_send(name):
        hop[name] = [
            send(
                getattr(ref, name + "_kx").at[lax.rem(spot_s + step, n_sp)],
                getattr(ref, name + "_rz").at[step - 1],
                line[step - 1],
            )
            for step in range(1, n_sp)
        ]

    def first_blk_done(name):
        hop[name].wait_recv()
        own_blk = getattr(ref, name + "_kc").at[pl.ds(spot_b * n_sp, n_sp)]
        add_blocks(getattr(ref, name + "_ky"), [own_blk, getattr(ref, name + "_rx")])
        hop[name] = send(getattr(ref, name + "_ky").at[:, 1 - pair], getattr(ref, name + "_ry"), pair_id)

    def then_pair_done(name):
        hop[name].wait_recv()
        add_blocks(getattr(ref, name + "_kx"), [getattr(ref, name + "_ky").at[:, pair], getattr(ref, name + "_ry")])
        line_send(name)

    def attention(q_here, kv_here, lse_here):
        ref.q_here, ref.kv_here, ref.lse_here = q_here, kv_here, lse_here
        loads = [
            pltpu.make_async_copy(getattr(ref, name), getattr(ref, name + "_here"), sem_local.at[2 + k])
            for k, name in enumerate(("q", "kv", "lse"))
        ]
        for copy in loads:
            copy.start()
        q_ref, kv_ref, lse_ref = ref.q_here, ref.kv_here, ref.lse_here
        dkv_ref[...] = jnp.zeros(dkv_ref.shape, F32)

        def attend(block, carry):
            at = tok(block)
            for h in range(heads_here):
                head = pl.ds(h * HD, HD)
                query = q_ref[at, head]
                grad = do_ref[at, head]
                keys = kv_ref[0, :, head]
                scores = mm_t(query, keys) * score_scale
                probs = jnp.exp(scores - lse_ref[h, at, 0:1])
                dkv_ref[1, :, head] += mm_first(probs.astype(BF), grad)
                d_probs = mm_t(grad, kv_ref[1, :, head])
                lean = jnp.sum(probs * d_probs, -1, keepdims=True)
                d_scores = (probs * (d_probs - lean)).astype(BF)
                dq_ref[at, head] = mm(d_scores, keys) * score_scale
                dkv_ref[0, :, head] += mm_first(d_scores, query) * score_scale
            return carry

        for name in ("fi", "fo"):
            add_blocks(getattr(ref, name + "_kx"), [getattr(ref, name), getattr(ref, name + "_rx")])
            if name == "fi":
                goal = lambda: ref.fi_ry.at[0]
                hop[name] = send(ref.fi_kx, goal(), pair_id, goal)
        for copy in loads:
            copy.wait()
        do_own.wait()
        for copy in do_away:
            copy.wait_recv()
        lax.fori_loop(0, 1, attend, 0)
        core_done("co")
        goal = lambda: ref.co_rx
        hop["co"] = send(
            ref.co_kc.at[pl.ds((1 - spot_b) * n_sp, n_sp)], goal(), blk_id, goal
        )
        core_done("ckv")
        goal = lambda: ref.ckv_ry
        hop["ckv"] = send(ref.ckv_kc.at[:, 1 - pair], goal(), pair_id, goal)
        for name in ("cq", "o"):
            goal = lambda name=name: getattr(ref, name + "_rc")
            hop[name] = send(getattr(ref, name).at[:, 1 - core], goal(), core_id, goal)
        lax.fori_loop(1, 2, attend, 0)
        core_done("cq")
        goal = lambda: ref.cq_rx
        hop["cq"] = send(
            ref.cq_kc.at[pl.ds((1 - spot_b) * n_sp, n_sp)], goal(), blk_id, goal
        )
        lax.fori_loop(2, n_sp, attend, 0)

    pl.run_scoped(
        attention,
        pltpu.VMEM(ref.q.shape, BF),
        pltpu.VMEM(ref.kv.shape, BF),
        pltpu.VMEM(ref.lse.shape, F32),
    )

    kv_recv, proj_ref = ref.kv_recv, ref.proj
    kv_away = []
    for which in range(2):
        place = pl.ds(which * cols, cols)
        proj_ref[:, place] = dkv_ref[which, total_rows:, :].astype(BF)
        kv_away.append(send(proj_ref.at[:, place], kv_recv.at[which], blk_id))
    core_done("o")
    hop["text"].wait_recv()
    text_kx = ref.text_kx
    add_blocks(text_kx, [ref.text.at[spot_b], ref.text_rx])
    hop["text"] = [
        send(
            text_kx.at[lax.rem(spot_s + step, n_sp)],
            ref.text_rz.at[step - 1],
            line[step - 1],
        )
        for step in range(1, n_sp)
    ]

    lin_ref, rho_ref, trig_ref = ref.lin, ref.rho, ref.trig
    par_ref, sums_ref = ref.par, ref.sums
    sums_ref[spot_s] = jnp.zeros((8, total_rows), F32)

    def gain_of(which, h):
        return par_ref[6 + which : 7 + which, lanes_at(spot_s * cols + h * HD, HD)]

    def unturn(which, block, carry):
        at = tok(block)
        cosine = trig_ref[0, at, :]
        sine = trig_ref[1, at, :]
        lean = jnp.zeros((rows, HD), F32)
        for h in range(heads_here):
            head = pl.ds(h * HD, HD)
            if which == 0:
                grad = dq_ref[at, head]
            else:
                grad = dkv_ref[0, at, head] + kv_recv[0, at, head].astype(F32)
            grad = turned(grad, cosine, -sine)
            if which == 0:
                dq_ref[at, head] = grad
            else:
                dkv_ref[0, at, head] = grad
            lean = lean + lin_ref[which, at, head] * gain_of(which, h) * grad
        total = exact_sums(lean)
        sums_ref[spot_s, which : which + 1, lanes_at(block * rows, rows)] = total[0:1]
        return carry

    lax.fori_loop(0, n_sp, functools.partial(unturn, 0), 0)
    first_blk_done("co")
    ff_last("fi")
    for copy in kv_away:
        copy.wait()
    sent[:] = [copy for copy in sent if all(copy is not other for other in kv_away)]
    def first_blk_send(name):
        hop[name] = send(
            getattr(ref, name + "_kc").at[pl.ds((1 - spot_b) * n_sp, n_sp)], getattr(ref, name + "_rx"), blk_id
        )

    first_blk_send("o")
    first_blk_done("cq")
    hop["fo"] = send(ref.fo_kx, ref.fo_ry.at[0], pair_id)
    lax.fori_loop(0, n_sp, functools.partial(unturn, 1), 0)
    sums_away = [
        send(sums_ref.at[spot_s], sums_ref.at[spot_s], line[k]) for k in range(n_sp - 1)
    ]
    then_pair_done("co")
    for copy in sums_away:
        copy.wait_recv()
    means = sums_ref[0]
    for k in range(1, n_sp):
        means = means + sums_ref[k]
    sums_ref[n_sp] = means / width
    small_ref = ref.small
    own = lanes_at(spot_s * cols, cols)
    small_ref[0] = ref.small_in[...]
    for row in (6, 7, 11, 12, 13):
        small_ref[0, row : row + 1, :] = jnp.zeros((1, width), F32)

    def project(block, carry):
        at = tok(block)
        for which in range(2):
            mean = exact_first(sums_ref[n_sp, :, lanes_at(block * rows, rows)], row_pick(which))
            rho = rho_ref[which, at, :]
            cube = rho * rho * rho * mean
            for h in range(heads_here):
                head = pl.ds(h * HD, HD)
                grad = dq_ref[at, head] if which == 0 else dkv_ref[0, at, head]
                value = lin_ref[which, at, head]
                low = (rho * gain_of(which, h) * grad - value * cube).astype(BF)
                place = pl.ds(which * cols + h * HD, HD)
                proj_ref[at, place] = low
                here = lanes_at(spot_s * cols + h * HD, HD)
                small_ref[0, 6 + which : 7 + which, here] += jnp.sum(
                    grad * value * rho, 0, keepdims=True
                )
                small_ref[0, 11 + which : 12 + which, here] += jnp.sum(
                    low.astype(F32), 0, keepdims=True
                )
        low = (dkv_ref[1, at, :] + kv_recv[1, at, :].astype(F32)).astype(BF)
        proj_ref[at, 2 * cols :] = low
        small_ref[0, 13:14, own] += jnp.sum(low.astype(F32), 0, keepdims=True)
        return carry

    lax.fori_loop(0, n_sp, project, 0)
    dh1_ref, dh1_recv, sw_ref = ref.dh1, ref.dh1_recv, ref.sw
    chain_send, chain_recv = ref.chain_send, ref.chain_recv

    def chain_copy(way, block):
        if way == 0:
            slot, target = block, {SP: spot_s + 1}
        else:
            slot = jnp.where(block == spot_s - 1, n_sp, block)
            target = {SP: spot_s - 1}
        return remote_copy(
            dh1_ref.at[block],
            dh1_recv.at[slot],
            chain_send.at[way * n_sp + block],
            chain_recv.at[slot],
            target,
        )

    def chain_wait(slot):
        at = dh1_recv.at[slot]
        remote_copy(at, at, chain_send.at[0], chain_recv.at[slot], blk_id).wait_recv()

    def chain_pass(way, block, slot):
        total = dh1_ref[block].astype(F32) + dh1_recv[slot].astype(F32)
        dh1_ref[block] = total.astype(BF)
        chain_copy(way, block).start()

    def chain_step(time):
        right = n_sp - 1 + spot_s - time
        inside = jnp.logical_and(right >= spot_s, right < n_sp)

        @pl.when(jnp.logical_and(spot_s > 0, inside))
        def _():
            chain_wait(right)

            @pl.when(right > spot_s)
            def _():
                chain_pass(0, right, right)

        left = time - (n_sp - 1 - spot_s)
        inside = jnp.logical_and(left >= 0, left <= spot_s)

        @pl.when(jnp.logical_and(spot_s < n_sp - 1, inside))
        def _():
            slot = jnp.where(left == spot_s, n_sp, left)
            chain_wait(slot)

            @pl.when(left < spot_s)
            def _():
                chain_pass(1, left, slot)

    def products(w_ref, h1_ref, stage):
        sw_copies = []
        w_load = pltpu.make_async_copy(ref.w, w_ref, sem_local.at[0])
        h1_load = pltpu.make_async_copy(ref.h1, h1_ref, sem_local.at[1])
        w_load.start()
        h1_load.start()
        w_load.wait()
        def away(step, carry):
            turn = jnp.where(spot_s < n_sp // 2, n_sp - step, step)
            block = lax.rem(spot_s + turn, n_sp)
            for part in range(width // cols):
                place = pl.ds(part * cols, cols)
                value = mm_t(proj_ref[tok(block), :], w_ref[place, :])
                dh1_ref[block, :, place] = value.astype(BF)

            @pl.when(spot_s == 0)
            def _():
                chain_copy(0, block).start()

            @pl.when(spot_s == n_sp - 1)
            def _():
                chain_copy(1, block).start()

            return carry

        lax.fori_loop(1, n_sp, away, 0)
        for part in range(width // cols):
            place = pl.ds(part * cols, cols)
            ref.dh1_own[:, place] = mm_t(proj_ref[tok(spot_s), :], w_ref[place, :])
        h1_load.wait()
        for part in range(n_sp):
            value = mm_first(h1_ref[:, part * cols : (part + 1) * cols], proj_ref[...])
            value = value.astype(BF)
            slot = part % 2
            if part > 1:
                sw_copies[part - 2].wait()
            for k in range(4):
                half = cols // 4
                stage[slot, k // 2, k % 2] = value[k * half : (k + 1) * half]
            copy = pltpu.make_async_copy(
                stage.at[slot], sw_ref.at[pl.ds(2 * part, 2)], sem_local.at[2 + slot]
            )
            copy.start()
            sw_copies.append(copy)
        for copy in sw_copies[-2:]:
            copy.wait()
        hop["s"] = send(
            sw_ref.at[:, 1 - core], ref.s_rc, core_id, lambda: ref.s_rc
        )

    pl.run_scoped(
        products,
        pltpu.VMEM(ref.w.shape, BF),
        pltpu.VMEM(ref.h1.shape, BF),
        pltpu.VMEM((2, 2, 2, cols // 4, 3 * cols), BF),
    )

    pair_done("ckv")
    chain_step(1)
    hop["s"].wait_recv()
    add_blocks(ref.s_kc, [ref.sw.at[:, core], ref.s_rc])
    hop["s"] = send(ref.s_kc.at[pl.ds((1 - spot_b) * n_sp, n_sp)], ref.s_rx, blk_id)
    first_blk_done("o")
    for k in range(2, n_sp - 1):
        chain_step(k)
    then_pair_done("cq")
    for copy in hop["text"]:
        copy.wait_recv()
    add_blocks(
        ref.text_out.at[0],
        [text_kx.at[spot_s]] + [ref.text_rz.at[k] for k in range(n_sp - 1)],
    )

    chain_step(n_sp - 1)

    @pl.when(spot_s > 0)
    def _():
        ref.dh1_own[...] += dh1_recv[spot_s].astype(F32)

    @pl.when(spot_s < n_sp - 1)
    def _():
        ref.dh1_own[...] += dh1_recv[n_sp].astype(F32)

    d_shift = ref.dh1_own[...]
    values = ref.x[...].astype(F32)
    centre = values - jnp.mean(values, axis=-1, keepdims=True)
    spread = lax.rsqrt(jnp.mean(centre * centre, axis=-1, keepdims=True) + EPS)
    normed = centre * spread
    scale = 1.0 + (ref.time[1:2, :] + par_ref[1:2, :])
    grad = d_shift * scale
    lean = jnp.mean(grad, axis=-1, keepdims=True)
    tilt = jnp.mean(grad * normed, axis=-1, keepdims=True)
    ref.tokens_out[...] = ref.dx1[...] + spread * (grad - lean - normed * tilt)
    small_ref[0, 0:1, :] = jnp.sum(d_shift, 0, keepdims=True)
    small_ref[0, 1:2, :] = jnp.sum(d_shift * normed, 0, keepdims=True)
    partners = [core_id, pair_id] + [dp_id(bit) for bit in bits] + [blk_id]
    bit = 1
    while bit < n_sp:
        partners.append({SP: spot_s + bit - 2 * bit * lax.rem(spot_s // bit, 2)})
        bit *= 2

    def small_send(k):
        hop["small"] = send(small_ref.at[k], ref.small_recv.at[k], partners[k])

    def small_done(k):
        hop["small"].wait_recv()
        small_ref[k + 1] = small_ref[k] + ref.small_recv[k]
        if k + 1 < len(partners):
            small_send(k + 1)
        else:
            ref.small_out[...] = small_ref[k + 1]

    small_send(0)
    blk_done("ckv")
    line_send("ckv")
    hop["s"].wait_recv()
    own_blk = ref.s_kc.at[pl.ds(spot_b * n_sp, n_sp)]
    add_blocks(ref.s_kx, [own_blk, ref.s_rx])
    small_done(0)
    s_line = []
    s_keep = []
    for j in range(3):
        place = lanes_at(j * width + spot_s * cols, cols)
        part = pl.ds(j * cols, cols)
        copy = pltpu.make_async_copy(
            ref.s_kx.at[spot_s, :, part], ref.s_z.at[:, place], sem_local.at[2 + j]
        )
        copy.start()
        s_keep.append(copy)
        for step in range(1, n_sp):
            s_line.append(
                send(
                    ref.s_kx.at[lax.rem(spot_s + step, n_sp), :, part],
                    ref.s_z.at[:, place],
                    line[step - 1],
                )
            )
    then_pair_done("o")

    def line_done(name):
        for copy in hop[name]:
            copy.wait_recv()
        kx, rz = getattr(ref, name + "_kx"), getattr(ref, name + "_rz")
        out = getattr(ref, name + "_out").at[core]
        kz = getattr(ref, name + "_kz")
        add_blocks(
            kz.at[0], [kx.at[spot_s]] + [rz.at[k] for k in range(n_sp - 1)]
        )
        for k, bit in enumerate(bits):
            got = getattr(ref, name + "_rw").at[k]
            send(kz.at[k], got, dp_id(bit)).wait_recv()
            add_blocks(kz.at[k + 1], [kz.at[k], got])
        last = kz.at[len(bits)]
        own_copy = pltpu.make_async_copy(last, out.at[pair], sem_local.at[1])
        own_copy.start()
        hop[name] = send(last, out.at[pair], pair_id)
        own_copy.wait()

    def pair_back(name):
        hop[name].wait_recv()
        out = getattr(ref, name + "_out").at[core]
        hop[name] = send(out, out, core_id)

    small_done(1)
    line_done("co")
    for k in range(2, len(partners) - 2):
        small_done(k)
    line_done("cq")
    for copy in s_keep:
        copy.wait()
    for copy in s_line:
        copy.wait_recv()
    hop["s"] = send(ref.s_z, ref.s_ry.at[0], pair_id)
    small_done(len(partners) - 2)
    line_done("ckv")
    ff_last("fo")
    small_done(len(partners) - 1)
    pair_back("co")
    pair_back("cq")
    line_done("o")
    hop["s"].wait_recv()
    s_ry, s_out = ref.s_ry, ref.s_out
    for k in range(len(bits) + 1):
        source = ref.s_z if k == 0 else ref.s_kw.at[k - 1]
        goal = s_out.at[core] if k == len(bits) else ref.s_kw.at[k]
        add_blocks(goal, [source, s_ry.at[k]])
        if k < len(bits):
            send(goal, s_ry.at[k + 1], dp_id(bits[k])).wait_recv()
    hop["s"] = send(s_out.at[core], s_out.at[core], core_id)
    pair_back("ckv")
    pair_back("o")
    for name in ("ckv", "co", "cq", "o", "fi", "fo", "s"):
        hop[name].wait_recv()
    for copy in sent:
        copy.wait_send()
    for block in range(n_sp):

        @pl.when(block > spot_s)
        def _():
            chain_copy(0, block).wait_send()

        @pl.when(block < spot_s)
        def _():
            chain_copy(1, block).wait_send()


def back(**values):
    arrays = types.SimpleNamespace(**values)
    n_sp = lax.axis_size(SP)
    n_dp = lax.axis_size(DP)
    shape = jax.ShapeDtypeStruct
    rows, width = arrays.d_att.shape
    total = n_sp * rows
    cols = arrays.q.shape[1]
    g8 = 2 * n_sp
    more = max(n_dp.bit_length() - 3, 0)
    any_names = ["ckv", "cq", "co", "o", "fi", "fo", "fi_rx", "fo_rx", "d_att", "text", "q", "kv", "lse", "w", "h1"]
    vmem_names = ["lin", "rho", "trig", "par", "x", "dx1", "time", "small_in"]
    outs = {}
    for name in ("ckv", "cq", "co", "o"):
        quarter, lanes = getattr(arrays, name).shape[3:]
        outs[name + "_rc"] = shape((g8, 2, quarter, lanes), BF)
        outs[name + "_kc"] = shape((g8, 2, quarter, lanes), BF)
        if name == "ckv":
            outs[name + "_ry"] = shape((g8, quarter, lanes), BF)
            outs[name + "_ky"] = shape((g8, quarter, lanes), BF)
            outs[name + "_rx"] = shape((n_sp, quarter, lanes), BF)
        else:
            outs[name + "_rx"] = shape((n_sp, 2, quarter, lanes), BF)
            outs[name + "_ky"] = shape((n_sp, 2, quarter, lanes), BF)
            outs[name + "_ry"] = shape((n_sp, quarter, lanes), BF)
        outs[name + "_kx"] = shape((n_sp, quarter, lanes), BF)
        outs[name + "_rz"] = shape((n_sp - 1, quarter, lanes), BF)
        outs[name + "_kz"] = shape((more + 1, quarter, lanes), BF)
        outs[name + "_rw"] = shape((more + 1, quarter, lanes), BF)
        outs[name + "_out"] = shape((2, 2, quarter, lanes), BF)
    for name in ("fi", "fo"):
        half = getattr(arrays, name).shape
        outs[name + "_kx"] = shape(half, BF)
        outs[name + "_ry"] = shape((more + 1,) + half, BF)
        outs[name + "_ky"] = shape((more + 1,) + half, BF)
        outs[name + "_out"] = shape((2,) + half, BF)
    text_rows = arrays.text.shape[2]
    outs.update(text_rx=shape((n_sp, text_rows, width), BF))
    outs.update(text_kx=shape((n_sp, text_rows, width), BF))
    outs.update(text_rz=shape((n_sp - 1, text_rows, width), BF))
    outs.update(text_out=shape((1, text_rows, width), F32))
    half_rows = width // g8 // 2
    outs.update(sw=shape((g8, 2, half_rows, 3 * cols), BF))
    outs.update(s_rc=shape((g8, half_rows, 3 * cols), BF))
    outs.update(s_kc=shape((g8, half_rows, 3 * cols), BF))
    outs.update(s_rx=shape((n_sp, half_rows, 3 * cols), BF))
    outs.update(s_kx=shape((n_sp, half_rows, 3 * cols), BF))
    outs.update(s_z=shape((half_rows, 3 * width), BF))
    outs.update(s_ry=shape((more + 1, half_rows, 3 * width), BF))
    outs.update(s_kw=shape((more + 1, half_rows, 3 * width), BF))
    outs.update(s_out=shape((2, half_rows, 3 * width), BF))
    in_any = len(outs)
    outs.update(tokens_out=shape((rows, width), F32))
    outs.update(small_out=shape(arrays.small_in.shape, F32))
    steps = 3 + more + n_sp.bit_length() - 1
    vmem = pltpu.VMEM
    scratch = dict(
        do=vmem((total, cols), BF),
        dq=vmem((total, cols), F32),
        dkv=vmem((2, 2 * total, cols), F32),
        kv_recv=vmem((2, total, cols), BF),
        sums=vmem((n_sp + 1, 8, total), F32),
        proj=vmem((total, 3 * cols), BF),
        dh1=vmem((n_sp, rows, width), BF),
        dh1_own=vmem((rows, width), F32),
        dh1_recv=vmem((n_sp + 1, rows, width), BF),
        chain_send=pltpu.SemaphoreType.DMA((2 * n_sp,)),
        chain_recv=pltpu.SemaphoreType.DMA((n_sp + 1,)),
        small=vmem((steps + 1,) + arrays.small_in.shape, F32),
        small_recv=vmem((steps,) + arrays.small_in.shape, F32),
        send=pltpu.SemaphoreType.DMA((128,)),
        recv=pltpu.SemaphoreType.DMA((128,)),
        local=pltpu.SemaphoreType.DMA((5,)),
    )
    any_place = pl.BlockSpec(memory_space=pl.ANY)
    in_vmem = pl.BlockSpec(memory_space=pltpu.VMEM)
    names = any_names + vmem_names + list(outs) + list(scratch)
    results = pl.pallas_call(
        functools.partial(back_kernel, n_sp, n_dp, names),
        out_shape=tuple(outs.values()),
        in_specs=[any_place] * len(any_names) + [in_vmem] * len(vmem_names),
        out_specs=(any_place,) * in_any + (in_vmem,) * (len(outs) - in_any),
        scratch_shapes=list(scratch.values()),
        compiler_params=pltpu.CompilerParams(
            collective_id=2, has_side_effects=True, vmem_limit_bytes=60 * 2**20
        ),
    )(*[getattr(arrays, name) for name in any_names + vmem_names])
    return types.SimpleNamespace(**dict(zip(outs, results)))


def swap_blk(value):
    return lax.ppermute(value, BLK, [(0, 1), (1, 0)])


def local(
    clip_tokens,
    text_tokens,
    text_lengths,
    positions,
    time_embed,
    modulation,
    gains,
    biases,
    self_qkv,
    self_out,
    cross_qkv,
    cross_out,
    ffn_in,
    ffn_out,
    ffn_bias,
    cotangent,
):
    n_sp = lax.axis_size(SP)
    n_dp = lax.axis_size(DP)
    spot_dp = lax.axis_index(DP)
    spot_b = lax.axis_index(BLK)
    spot_s = lax.axis_index(SP)
    core = spot_dp % 2
    pair = (spot_dp // 2) % 2
    x_own = clip_tokens[0]
    tok_rows, width = x_own.shape
    heads_here = H // n_sp
    cols_here = heads_here * HD
    shard_rows = self_qkv.shape[0]
    scale = HD ** (-0.5)

    small_rows = jnp.concatenate([modulation, gains, biases], 0)
    lanes_here = small_rows.shape[1]
    small_own = jnp.concatenate(
        [
            jnp.pad(
                positions[0].astype(BF), ((0, 13), (0, SMALL_LANES - positions.shape[2]))
            ),
            jnp.pad(
                small_rows, ((0, PARAM_ROWS - 21), (0, SMALL_LANES - lanes_here))
            ),
        ],
        0,
    )
    (
        params,
        h1_all,
        qkv_mine,
        lin_parts,
        rho,
        trig,
        q_flat,
        kv_flat,
        lse_wide,
        att_all,
        att_tok,
        rest_all,
        in_other,
        out_other,
        text_every,
        cot_every,
    ) = front(
        x_own,
        small_own,
        self_qkv,
        jnp.concatenate([self_out, cross_out, cross_qkv], 1),
        ffn_in,
        ffn_out,
        text_tokens[0],
        cotangent[0],
        time_embed[0],
    )
    mods = time_embed[0] + params[:6]
    gain_all = params[6:11]
    bias_all = params[11:21]
    ff_here = ffn_in.shape[0]
    bias_own = ffn_bias.astype(F32)
    bias_ff = jnp.concatenate([bias_own, swap_blk(ffn_bias).astype(F32)])
    own = own_tokens(
        text_lengths, rest_all, x_own, att_tok, text_every, time_embed[0], params
    )
    ffn_rows = own.h2
    x_two = own.two

    fed = feed(**dict(
            in_own=ffn_in,
            in_other=in_other,
            out_own=ffn_out,
            out_other=out_other,
            h2=ffn_rows,
            cot=cot_every,
            bias=bias_ff[None],
            time=time_embed[0],
            par=params,
        )
    )
    d_rows = fed.d_rows
    du_sums = fed.du_sums[0]
    z_lin = (
        lax.psum_scatter(fed.z_out, SP, scatter_dimension=0, tiled=False).astype(F32)
        + bias_all[9]
    )
    grad_y = cotangent[0].astype(F32)
    result = x_two + mods[5] * z_lin
    block_out = result.astype(BF)[None]
    d_gate2 = jnp.sum(grad_y * z_lin, 0)
    last = own_back(**dict(
            len=text_lengths,
            rest=rest_all,
            x_two=x_two,
            x_one=own.one,
            d_rows=d_rows,
            cot=cotangent[0],
            time=time_embed[0],
            par=params,
            a=own.a,
            cin=own.cin,
            ql=own.ql,
            kl=own.kl,
            q=own.q,
            kv=own.kv,
            lse=own.lse,
            oc=own.oc,
            att=att_tok,
            text_in=text_every,
        )
    )

    ff_total = ff_here * 2 * n_sp
    ff_row = jnp.zeros((-(-ff_total // width) * width,), F32)
    own_at = (spot_b * n_sp + spot_s) * ff_here
    far_at = ((1 - spot_b) * n_sp + spot_s) * ff_here
    ff_row = lax.dynamic_update_slice_in_dim(ff_row, du_sums[:ff_here], own_at, 0)
    ff_row = lax.dynamic_update_slice_in_dim(ff_row, du_sums[ff_here:], far_at, 0)
    small = last.sums
    small = lax.dynamic_update_slice(small, d_gate2[None], (5, 0))
    small = lax.dynamic_update_slice(small, ff_row.reshape(-1, width), (21, 0))

    def quarters(grad):
        return grad.reshape(2 * n_sp, 2, 2, shard_rows // 4, grad.shape[1])

    ff_low = fed.f_out.reshape(2, 2, 5, ff_here // 10, width)
    ff_got = swap_blk(ff_low[:, 1])

    ended = back(**dict(
            ckv=quarters(jnp.concatenate([last.ck, last.cv], 1)),
            cq=quarters(last.cq),
            co=quarters(last.co),
            o=quarters(last.o),
            fi=ff_low[0, 0],
            fo=ff_low[1, 0],
            fi_rx=ff_got[0],
            fo_rx=ff_got[1],
            d_att=last.d_att,
            text=last.text_part.reshape(2, n_sp, -1, width),
            q=q_flat,
            kv=kv_flat,
            lse=lse_wide,
            w=qkv_mine,
            h1=h1_all,
            lin=lin_parts,
            rho=rho,
            trig=trig,
            par=params,
            x=x_own,
            dx1=last.dx,
            time=time_embed[0],
            small_in=small,
        )
    )
    small = ended.small_out
    spot = spot_b * n_sp + spot_s
    small_own = lax.dynamic_slice_in_dim(small[:21], spot * lanes_here, lanes_here, 1)
    part_bias = lax.dynamic_slice_in_dim(small[21:].reshape(-1), own_at, ff_here, 0)

    def whole(name, rows):
        return getattr(ended, name + "_out").reshape(rows, -1).astype(F32)

    return (
        block_out,
        ended.tokens_out[None],
        ended.text_out,
        small_own[:6],
        small_own[6:11],
        small_own[11:21],
        whole("s", shard_rows),
        whole("o", shard_rows),
        jnp.concatenate(
            [
                whole("cq", shard_rows),
                whole("ckv", shard_rows),
            ],
            1,
        ),
        whole("co", shard_rows),
        whole("fi", ff_here),
        whole("fo", ff_here),
        part_bias,
    )


def solution(mesh):
    return jax.shard_map(
        local,
        mesh=mesh,
        in_specs=(
            P(DP, (BLK, SP), None),
            P(DP, (BLK, SP), None),
            P(DP),
            P(DP, None, (BLK, SP)),
            P(DP, None, None),
            P(None, (BLK, SP)),
            P(None, (BLK, SP)),
            P(None, (BLK, SP)),
            P((BLK, SP), None),
            P((BLK, SP), None),
            P((BLK, SP), None),
            P((BLK, SP), None),
            P((BLK, SP), None),
            P((BLK, SP), None),
            P((BLK, SP)),
            P(DP, (BLK, SP), None),
        ),
        out_specs=(
            P(DP, (BLK, SP), None),
            P(DP, (BLK, SP), None),
            P(DP, (BLK, SP), None),
            P(None, (BLK, SP)),
            P(None, (BLK, SP)),
            P(None, (BLK, SP)),
            P((BLK, SP), None),
            P((BLK, SP), None),
            P((BLK, SP), None),
            P((BLK, SP), None),
            P((BLK, SP), None),
            P((BLK, SP), None),
            P((BLK, SP)),
        ),
        check_vma=False,
    )
```

```python
import functools
import types

import jax
import jax.numpy as jnp
import numpy as np
from jax import lax
from jax.experimental import pallas as pl
from jax.experimental.pallas import tpu as pltpu
from jax.sharding import PartitionSpec as P

H = 12
HD = 128


DP, BLK, SP = "dp", "blk", "sp"
EPS = 1e-06
NEG = -1e30


def rope_tables(head_dim):
    pair_count = head_dim // 2
    side_count = head_dim // 6
    first_count = pair_count - 2 * side_count
    tables = np.zeros((3, pair_count))
    for column in range(pair_count):
        if column < first_count:
            tables[0, column] = 10000.0 ** (-column / first_count)
        elif column < first_count + side_count:
            tables[1, column] = 10000.0 ** (-(column - first_count) / side_count)
        else:
            tables[2, column] = 10000.0 ** (-(column - first_count - side_count) / side_count)
    return tables


BF = jnp.bfloat16
F32 = jnp.float32


MESH = pl.DeviceIdType.MESH
PARAM_ROWS = 32
SMALL_ROWS = 16 + PARAM_ROWS
SMALL_LANES = 256


def remote_copy(src, dst, send, recv, target):
    return pltpu.make_async_remote_copy(
        src_ref=src,
        dst_ref=dst,
        send_sem=send,
        recv_sem=recv,
        device_id=target,
        device_id_type=MESH,
    )


def meet(targets):
    barrier = pltpu.get_barrier_semaphore()
    for target in targets:
        pl.semaphore_signal(barrier, inc=1, device_id=target, device_id_type=MESH)
    pl.semaphore_wait(barrier, len(targets))


def rows_at(start, size):
    return pl.ds(pl.multiple_of(start, 16), size)


def lanes_at(start, size):
    return pl.ds(pl.multiple_of(start, 128), size)


def mm(a, b):
    return lax.dot_general(a, b, (((1,), (0,)), ((), ())), preferred_element_type=F32)


def mm_t(a, b):
    return lax.dot_general(a, b, (((1,), (1,)), ((), ())), preferred_element_type=F32)


def mm_first(a, b):
    return lax.dot_general(a, b, (((0,), (0,)), ((), ())), preferred_element_type=F32)


def exact_first(a, b):
    return lax.dot_general(
        a,
        b,
        (((0,), (0,)), ((), ())),
        precision=lax.Precision.HIGHEST,
        preferred_element_type=F32,
    )


def exact_sums(values):
    ones = jnp.ones((8, values.shape[1]), F32)
    return lax.dot_general(
        ones,
        values,
        (((1,), (1,)), ((), ())),
        precision=lax.Precision.HIGHEST,
        preferred_element_type=F32,
    )


def row_pick(which):
    return (lax.broadcasted_iota(jnp.int32, (8, 128), 0) == which).astype(F32)


def turn_sign():
    lane = lax.broadcasted_iota(jnp.int32, (1, HD), 1)
    return jnp.where(lane < HD // 2, -1.0, 1.0).astype(F32)


def turned(value, cosine, sine):
    return value * cosine + pltpu.roll(value, HD // 2, 1) * (sine * turn_sign())


def front_kernel(
    n_sp,
    x_ref,
    small_ref,
    qkv_ref,
    rest_ref,
    in_ref,
    out_ref,
    text_ref,
    cot_ref,
    time_ref,
    table_ref,
    par_ref,
    h1_out,
    w_out_ref,
    lin_out,
    rho_out,
    trig_out,
    q_out,
    kv_out,
    lse_out,
    att_out,
    tok_out,
    rest_out,
    in_out,
    out_out,
    text_out,
    cot_out,
    small_out,
    xall_ref,
    sall_ref,
    w_ref,
    lin_ref,
    sums_ref,
    rho_ref,
    trig_ref,
    q_ref,
    kv_ref,
    acc_ref,
    stat_ref,
    att_ref,
    h1_ref,
    *sems,
):
    lo, zs, zr, ss, sr, ws, wr, xs, xr, cs, cr, ps, pr, vs, vr, qs, qr, ts, tr, out = sems[:20]
    (ls, lr, lxs, lxr, lys, lyr, lcs, lcr, fs, fr, es, er, exs, exr, os, osr) = sems[20:]
    spot_d = lax.axis_index(DP)
    spot_b = lax.axis_index(BLK)
    spot_s = lax.axis_index(SP)
    core = lax.rem(spot_d, 2)
    pair = lax.rem(spot_d // 2, 2)
    core_id = {DP: spot_d + 1 - 2 * core}
    pair_id = {DP: spot_d + 2 - 4 * pair}
    blk_id = {BLK: 1 - spot_b}
    line = [{SP: lax.rem(spot_s + step, n_sp)} for step in range(1, n_sp)]
    rows = x_ref.shape[0]
    shard = qkv_ref.shape[0]
    half = shard // 2
    cols = w_ref.shape[1] // 3
    wide = qkv_ref.shape[1] // 3
    heads_here = cols // HD
    total_rows = n_sp * rows
    sums_ref[spot_s] = jnp.zeros((8, total_rows), F32)
    meet(line + [core_id, blk_id, pair_id])

    def w_rows(blk, spot, part):
        return rows_at((blk * n_sp + spot) * shard + part * half, half)

    here = spot_b * n_sp + spot_s
    keep = [
        pltpu.make_async_copy(
            qkv_ref.at[:, lanes_at(j * wide + spot_s * cols, cols)],
            w_ref.at[rows_at(here * shard, shard), pl.ds(j * cols, cols)],
            lo.at[j],
        )
        for j in range(3)
    ]
    keep.append(pltpu.make_async_copy(x_ref, xall_ref.at[rows_at(spot_s * rows, rows)], lo.at[3]))
    keep.append(pltpu.make_async_copy(small_ref, sall_ref.at[here], lo.at[4]))
    for copy in keep:
        copy.start()
    small_away = [
        remote_copy(small_ref, sall_ref.at[here], ss.at[k], sr.at[k], line[k])
        for k in range(n_sp - 1)
    ]
    for copy in small_away:
        copy.start()
    w_away = []
    for k in range(n_sp - 1):
        spot = lax.rem(spot_s + k + 1, n_sp)
        for j in range(3):
            copy = remote_copy(
                qkv_ref.at[rows_at(core * half, half), lanes_at(j * wide + spot * cols, cols)],
                w_ref.at[w_rows(spot_b, spot_s, core), pl.ds(j * cols, cols)],
                ws.at[3 * k + j],
                wr.at[3 * k + j],
                line[k],
            )
            copy.start()
            w_away.append(copy)

    def sends(way, k):
        if way == 0:
            return jnp.logical_and(spot_s < n_sp - 1, spot_s >= k)
        return jnp.logical_and(spot_s > 0, spot_s + k < n_sp)

    def gets(way, k):
        return spot_s > k if way == 0 else spot_s + k + 1 < n_sp

    def line_gather(first, place, pieces, send, recv, then=None):
        def copy(way, k, part):
            block = spot_s - k if way == 0 else spot_s + k
            at = place(block, part)
            src = first(part) if k == 0 else at
            target = {SP: spot_s + 1 if way == 0 else spot_s - 1}
            index = (way * (n_sp - 1) + k) * pieces + part
            return remote_copy(src, at, send.at[index], recv.at[index], target)

        def step(k):
            for part in range(pieces):
                for way in range(2):
                    if k > 0:

                        @pl.when(gets(way, k - 1))
                        def _():
                            copy(way, k - 1, part).wait_recv()

                    if k < n_sp - 1:

                        @pl.when(sends(way, k))
                        def _():
                            copy(way, k, part).start()

                    if k > 0 and then is not None:

                        @pl.when(gets(way, k - 1))
                        def _():
                            then(spot_s - k if way == 0 else spot_s + k)

        def sent():
            for k in range(n_sp - 1):
                for part in range(pieces):
                    for way in range(2):

                        @pl.when(sends(way, k))
                        def _():
                            copy(way, k, part).wait_send()

        return step, sent

    pieces = 2
    piece = rows // pieces
    token_step, token_sent = line_gather(
        lambda part: x_ref.at[pl.ds(part * piece, piece)],
        lambda block, part: xall_ref.at[rows_at(block * rows + part * piece, piece)],
        pieces,
        zs,
        zr,
    )

    fourth = shard // 4
    quarter = core * 2 + pair

    def rest_rows(blk, spot, which):
        return rest_out.at[rows_at((blk * n_sp + spot) * shard + which * fourth, fourth)]

    def rest_copy(sems, blk, spot, which, slot, target):
        at = rest_rows(blk, spot, which)
        index = (slot * 2 + blk) * n_sp + spot
        return remote_copy(at, at, sems[0].at[index], sems[1].at[index], target)

    def rest_core(blk, spot, slot):
        which = core * 2 + (pair if slot == 0 else 1 - pair)
        return rest_copy((lcs, lcr), blk, spot, which, slot, core_id)

    def rest_pair(blk, spot):
        return rest_copy((lys, lyr), blk, spot, quarter, 0, pair_id)

    def rest_blk(spot):
        at = rest_rows(spot_b, spot, quarter)
        return remote_copy(at, at, lxs.at[spot], lxr.at[spot], blk_id)

    def rest_arrived(spot):
        rest_blk(spot).start()
        rest_pair(spot_b, spot).start()
        rest_core(spot_b, spot, 0).start()

    rest_step, rest_sent = line_gather(
        lambda part: rest_ref.at[rows_at(quarter * fourth, fourth)],
        lambda block, part: rest_rows(spot_b, block, quarter),
        1,
        ls,
        lr,
        rest_arrived,
    )
    rest_own = remote_copy(
        rest_ref.at[rows_at(quarter * fourth, fourth)],
        rest_rows(spot_b, spot_s, quarter),
        lxs.at[spot_s],
        lxr.at[spot_s],
        blk_id,
    )
    rest_keep = pltpu.make_async_copy(
        rest_ref, rest_out.at[rows_at((spot_b * n_sp + spot_s) * shard, shard)], out.at[9]
    )

    def at_distance(k, call):
        if k == 0:
            call(spot_s)
        else:
            for way in range(2):

                @pl.when(gets(way, k - 1))
                def _():
                    call(spot_s - k if way == 0 else spot_s + k)

    def rest_from_blk(k):
        def one(spot):
            rest_blk(spot).wait_recv()
            rest_pair(1 - spot_b, spot).start()
            rest_core(1 - spot_b, spot, 0).start()

        at_distance(k, one)

    def rest_from_pair(k):
        def one(spot):
            if k > 0:
                rest_pair(spot_b, spot).wait_recv()
                rest_core(spot_b, spot, 1).start()
            rest_pair(1 - spot_b, spot).wait_recv()
            rest_core(1 - spot_b, spot, 1).start()

        at_distance(k, one)

    def rest_last(k):
        def one(spot):
            for slot in range(2):
                if k > 0:
                    rest_core(spot_b, spot, slot).wait_recv()
                rest_core(1 - spot_b, spot, slot).wait_recv()

        at_distance(k, one)

    def rest_done(k):
        def one(spot):
            rest_blk(spot).wait_send()
            for slot in range(2):
                if k > 0:
                    rest_core(spot_b, spot, slot).wait_send()
                rest_core(1 - spot_b, spot, slot).wait_send()
            if k > 0:
                rest_pair(spot_b, spot).wait_send()
            rest_pair(1 - spot_b, spot).wait_send()

        at_distance(k, one)

    hidden = in_ref.shape[0]
    hidden_half = hidden // 2

    def hidden_place(which, half):
        goal = in_out if which == 0 else out_out
        return goal.at[pl.ds(half * hidden_half, hidden_half)]

    def hidden_each(call):
        for which in range(2):
            for half in range(2):

                @pl.when(jnp.logical_and(core == half, pair == which))
                def _():
                    call(which, half)

    def hidden_blk(which, half):
        src = in_ref if which == 0 else out_ref
        return remote_copy(
            src.at[pl.ds(half * hidden_half, hidden_half)],
            hidden_place(which, half),
            fs.at[0],
            fr.at[0],
            blk_id,
        )

    def hidden_pair(which, half):
        at = hidden_place(which, half)
        return remote_copy(at, at, fs.at[1], fr.at[1], pair_id)

    def hidden_core(slot, which, half):
        at = hidden_place(which, half)
        return remote_copy(at, at, fs.at[2 + slot], fr.at[2 + slot], core_id)

    def hidden_next(which, half):
        hidden_blk(which, half).wait_recv()
        hidden_pair(which, half).start()
        hidden_core(0, which, half).start()

    def hidden_last(which, half):
        hidden_pair(which, half).wait_recv()
        hidden_core(1, 1 - which, half).start()

    def hidden_end(which, half):
        for slot in range(2):
            hidden_core(slot, which, half).wait_recv()
            hidden_core(slot, which, half).wait_send()
        hidden_pair(which, half).wait_send()
        hidden_blk(which, half).wait_send()

    text_rows = text_ref.shape[0]

    def text_at(blk, spot):
        return text_out.at[rows_at((blk * n_sp + spot) * text_rows, text_rows)]

    def text_blk(spot, own):
        at = text_at(spot_b, spot)
        src = text_ref if own else at
        return remote_copy(src, at, exs.at[spot], exr.at[spot], blk_id)

    text_step, text_sent = line_gather(
        lambda part: text_ref,
        lambda block, part: text_at(spot_b, block),
        1,
        es,
        er,
        lambda spot: text_blk(spot, False).start(),
    )
    text_keep = pltpu.make_async_copy(text_ref, text_at(spot_b, spot_s), out.at[10])
    cot_step, cot_sent = line_gather(
        lambda part: cot_ref,
        lambda block, part: cot_out.at[rows_at(block * rows, rows)],
        1,
        os,
        osr,
    )
    cot_keep = pltpu.make_async_copy(
        cot_ref, cot_out.at[rows_at(spot_s * rows, rows)], out.at[11]
    )

    token_step(0)
    rest_own.start()
    rest_step(0)
    for copy in (rest_keep, text_keep, cot_keep):
        copy.start()
    for copy in small_away:
        copy.wait_recv()
    keep[4].wait()
    small_pass = []
    for spot in range(n_sp):
        at = sall_ref.at[spot_b * n_sp + spot]
        copy = remote_copy(at, at, ps.at[spot], pr.at[spot], blk_id)
        copy.start()
        small_pass.append(copy)
    for j in range(3):
        keep[j].wait()
    blk_away = []
    core_away = []

    def pass_core(blk, spot, which):
        at = w_ref.at[w_rows(blk, spot, core)]
        copy = remote_copy(at, at, cs.at[which], cr.at[which], core_id)
        copy.start()
        core_away.append(copy)

    def pass_blk(step):
        at = w_ref.at[w_rows(spot_b, lax.rem(spot_s + n_sp - step, n_sp), core)]
        copy = remote_copy(at, at, xs.at[step], xr.at[step], blk_id)
        copy.start()
        blk_away.append(copy)

    pass_blk(0)
    for k in range(n_sp - 1):
        for j in range(3):
            w_away[3 * k + j].wait_recv()
        pass_blk(k + 1)
        pass_core(spot_b, lax.rem(spot_s + n_sp - k - 1, n_sp), k)

    for copy in small_pass:
        copy.wait_recv()
    lanes = wide // (2 * n_sp)
    at_row = lax.broadcasted_iota(jnp.int32, (2 * SMALL_LANES, 2 * lanes), 0)
    at_col = lax.broadcasted_iota(jnp.int32, (2 * SMALL_LANES, 2 * lanes), 1)
    place = jnp.where(at_row < SMALL_LANES, at_row, at_row - SMALL_LANES)
    goal = jnp.where(at_row < SMALL_LANES, place, place + lanes)
    chosen = jnp.logical_and(place < lanes, goal == at_col).astype(F32).astype(BF)
    for two in range(n_sp):
        both = jnp.concatenate(
            [sall_ref[2 * two, 16:, :], sall_ref[2 * two + 1, 16:, :]], axis=1
        )
        par_ref[:, 2 * lanes * two : 2 * lanes * (two + 1)] = mm(both, chosen)

    token_step(1)
    for step in range(n_sp):
        blk_away[step].wait_recv()
        pass_core(1 - spot_b, lax.rem(spot_s + n_sp - step, n_sp), n_sp - 1 + step)
    for copy in core_away:
        copy.wait_recv()
    w_keep = pltpu.make_async_copy(w_ref, w_out_ref, lo.at[5])
    w_keep.start()
    keep[3].wait()
    hidden_each(lambda which, half: hidden_blk(which, half).start())
    rest_from_blk(0)

    shift = time_ref[0:1, :] + par_ref[0:1, :]
    scale = 1.0 + (time_ref[1:2, :] + par_ref[1:2, :])
    own = lanes_at(spot_s * cols, cols)

    def project(block):
        at = rows_at(block * rows, rows)
        values = xall_ref[at, :].astype(F32)
        centre = values - jnp.mean(values, axis=-1, keepdims=True)
        spread = jnp.mean(centre * centre, axis=-1, keepdims=True)
        h1_ref[at, :] = (centre * lax.rsqrt(spread + EPS) * scale + shift).astype(BF)
        for j in range(3):
            lin = mm(h1_ref[at, :], w_ref[:, j * cols : (j + 1) * cols])
            lin = lin + par_ref[11 + j : 12 + j, own]
            if j < 2:
                lin_ref[j, at, :] = lin
                sums = exact_sums(lin * lin)
                sums_ref[spot_s, j : j + 1, lanes_at(block * rows, rows)] = sums[0:1]
            else:
                kv_ref[1, at, :] = lin.astype(BF)
        value_copy(block).start()
        angle = exact_first(
            sall_ref[spot_b * n_sp + block, 0:16, :].astype(F32), table_ref[...]
        )
        trig_ref[0, at, :] = jnp.cos(angle)
        trig_ref[1, at, :] = jnp.sin(angle)

    def kv_copy(which, block):
        return remote_copy(
            kv_ref.at[which, rows_at(block * rows, rows)],
            kv_ref.at[which, rows_at(total_rows + block * rows, rows)],
            vs.at[which * n_sp + block],
            vr.at[which * n_sp + block],
            blk_id,
        )

    def value_copy(block):
        return kv_copy(1, block)

    def arrived(k):
        first = (spot_s >= k).astype(jnp.int32)
        last = (spot_s + k < n_sp).astype(jnp.int32)

        def one(i, carry):
            ahead = jnp.logical_and(first == 1, i == 0)
            project(jnp.where(ahead, spot_s - k, spot_s + k))
            return carry

        lax.fori_loop(0, first + last, one, 0)

    project(spot_s)
    rest_step(1)
    arrived(1)
    token_step(2)
    rest_from_blk(1)
    arrived(2)
    rest_step(2)
    token_step(3)
    arrived(3)

    sums_away = []
    for k in range(n_sp - 1):
        copy = remote_copy(
            sums_ref.at[spot_s], sums_ref.at[spot_s], qs.at[k], qr.at[k], line[k]
        )
        copy.start()
        sums_away.append(copy)
    for copy in sums_away:
        copy.wait_recv()
    squares = sums_ref[0]
    for k in range(1, n_sp):
        squares = squares + sums_ref[k]
    rho_rows = lax.rsqrt(squares / wide + EPS)
    sums_ref[n_sp] = rho_rows

    def turn_block(which, block):
        at = rows_at(block * rows, rows)
        rho = exact_first(sums_ref[n_sp, :, lanes_at(block * rows, rows)], row_pick(which))
        rho_ref[which, at, :] = rho
        cosine = trig_ref[0, at, :]
        sine = trig_ref[1, at, :]
        for h in range(heads_here):
            gain = par_ref[6 + which : 7 + which, lanes_at(spot_s * cols + h * HD, HD)]
            value = lin_ref[which, at, h * HD : (h + 1) * HD] * rho * gain
            value = turned(value, cosine, sine).astype(BF)
            if which == 0:
                q_ref[at, h * HD : (h + 1) * HD] = value
            else:
                kv_ref[0, at, h * HD : (h + 1) * HD] = value

    def turn_key(block, carry):
        turn_block(1, block)
        kv_copy(0, block).start()
        return carry

    def turn_query(block, carry):
        turn_block(0, block)
        return carry

    lax.fori_loop(0, n_sp, turn_key, 0)
    lax.fori_loop(0, n_sp, turn_query, 0)
    text_blk(spot_s, True).start()
    text_step(0)
    rest_from_pair(0)
    rest_step(3)
    rest_from_blk(2)
    cot_step(0)
    saves = [
        pltpu.make_async_copy(sall_ref, small_out, out.at[12]),
        pltpu.make_async_copy(h1_ref, h1_out, out.at[0]),
        pltpu.make_async_copy(lin_ref, lin_out, out.at[1]),
        pltpu.make_async_copy(rho_ref, rho_out, out.at[2]),
        pltpu.make_async_copy(trig_ref, trig_out, out.at[3]),
        pltpu.make_async_copy(q_ref, q_out, out.at[4]),
    ]
    for copy in saves:
        copy.start()
    score_scale = HD ** (-0.5)

    def attend(block, h, part):
        at = rows_at(block * rows, rows)
        head = pl.ds(h * HD, HD)
        keys = pl.ds(part * total_rows, total_rows)
        scores = mm_t(q_ref[at, head], kv_ref[0, keys, head]) * score_scale
        top = jnp.max(scores, -1, keepdims=True)
        if part == 1:
            before = stat_ref[0, h, at, 0:1]
            top = jnp.maximum(top, before)
        raised = jnp.exp(scores - top)
        total = jnp.sum(raised, -1, keepdims=True)
        result = mm(raised.astype(BF), kv_ref[1, keys, head])
        if part == 0:
            stat_ref[0, h, at, :] = jnp.broadcast_to(top, (rows, 128))
            stat_ref[1, h, at, :] = jnp.broadcast_to(total, (rows, 128))
            acc_ref[h, at, :] = result
        else:
            fade = jnp.exp(before - top)
            total = total + fade * stat_ref[1, h, at, 0:1]
            result = result + fade * acc_ref[h, at, :]
            att_ref[at, head] = (result / total).astype(BF)
            stat_ref[0, h, at, :] = jnp.broadcast_to(top + jnp.log(total), (rows, 128))

    def first_pass(block, carry):
        for h in range(heads_here):
            attend(block, h, 0)
        return carry

    lax.fori_loop(0, n_sp, first_pass, 0)
    hidden_each(hidden_next)

    def key_wait(block, carry):
        kv_copy(0, block).wait_recv()
        kv_copy(1, block).wait_recv()
        return carry

    lax.fori_loop(0, n_sp, key_wait, 0)
    kv_save = pltpu.make_async_copy(kv_ref, kv_out, out.at[5])
    kv_save.start()
    rest_from_blk(3)
    rest_from_pair(1)

    def att_copy(step):
        block = lax.rem(spot_s + step, n_sp)
        return remote_copy(
            att_ref.at[rows_at(block * rows, rows)],
            tok_out.at[:, lanes_at(spot_s * cols, cols)],
            ts.at[step - 1],
            tr.at[step - 1],
            {SP: block},
        )

    for step in list(range(1, n_sp)) + [0]:
        block = lax.rem(spot_s + step, n_sp)

        def one_head(block=block):
            for h in range(heads_here):
                attend(block, h, 1)

        one_head()
        if step > 0:
            att_copy(step).start()
        if step == 1:
            text_step(1)
            cot_step(1)
        if step == 2:
            rest_from_pair(2)
    own_att = pltpu.make_async_copy(
        att_ref.at[rows_at(spot_s * rows, rows)],
        tok_out.at[:, lanes_at(spot_s * cols, cols)],
        out.at[6],
    )
    own_att.start()
    saves.append(own_att)
    last = [
        pltpu.make_async_copy(stat_ref.at[0], lse_out, out.at[7]),
        pltpu.make_async_copy(att_ref, att_out, out.at[8]),
    ]
    for copy in last:
        copy.start()
    text_step(2)
    cot_step(2)
    hidden_each(hidden_last)
    text_step(3)
    rest_from_pair(3)
    cot_step(3)
    for k in range(n_sp):
        rest_last(k)
        at_distance(k, lambda spot: text_blk(spot, False).wait_recv())
    for step in range(1, n_sp):
        att_copy(step).wait_recv()
    for copy in (rest_keep, text_keep, cot_keep):
        copy.wait()
    for k in range(n_sp):
        rest_done(k)
        at_distance(k, lambda spot: text_blk(spot, False).wait_send())
    hidden_each(hidden_end)
    rest_sent()
    text_sent()
    cot_sent()
    token_sent()
    for copy in saves + last + [kv_save, w_keep]:
        copy.wait()
    for copy in small_away + w_away + blk_away + core_away + small_pass + sums_away:
        copy.wait_send()

    def kv_sent(block, carry):
        kv_copy(0, block).wait_send()
        kv_copy(1, block).wait_send()
        return carry

    lax.fori_loop(0, n_sp, kv_sent, 0)
    for step in range(1, n_sp):
        att_copy(step).wait_send()


def front(x_own, small_own, qkv, rest, shard_in, shard_out, text, cot, time_rows):
    n_sp = lax.axis_size(SP)
    groups = 2 * n_sp
    rows, width = x_own.shape
    total = n_sp * rows
    cols = qkv.shape[1] // 3 // n_sp
    heads_here = cols // HD
    table = np.zeros((16, HD), np.float32)
    pairs = rope_tables(HD)
    table[:3, : HD // 2] = pairs
    table[:3, HD // 2 :] = pairs
    any_place = pl.BlockSpec(memory_space=pl.ANY)
    in_vmem = pl.BlockSpec(memory_space=pltpu.VMEM)
    dma = pltpu.SemaphoreType.DMA
    line = n_sp - 1
    counts = [6, 4 * line, 4 * line, line, line, 3 * line, 3 * line, n_sp, n_sp]
    counts += [2 * n_sp - 1, 2 * n_sp - 1, n_sp, n_sp, 2 * n_sp, 2 * n_sp, line, line]
    counts += [line, line, 13]
    counts += [2 * line, 2 * line, n_sp, n_sp, groups, groups, 2 * groups, 2 * groups, 4, 4]
    counts += [2 * line, 2 * line, n_sp, n_sp, 2 * line, 2 * line]
    shape = jax.ShapeDtypeStruct
    outs = (
        shape((PARAM_ROWS, width), F32),
        shape((total, width), BF),
        shape((width, 3 * cols), BF),
        shape((2, total, cols), F32),
        shape((2, total, HD), F32),
        shape((2, total, HD), F32),
        shape((total, cols), BF),
        shape((2, 2 * total, cols), BF),
        shape((heads_here, total, HD), F32),
        shape((total, cols), BF),
        shape((rows, width), BF),
        shape((groups * rest.shape[0], rest.shape[1]), BF),
        shape(shard_in.shape, BF),
        shape(shard_out.shape, BF),
        shape((groups * text.shape[0], width), BF),
        shape((total, width), BF),
        shape((groups,) + small_own.shape, BF),
    )
    vmem = pltpu.VMEM
    return pl.pallas_call(
        functools.partial(front_kernel, n_sp),
        out_shape=outs,
        in_specs=[any_place] * 8 + [in_vmem] * 2,
        out_specs=(in_vmem,) + (any_place,) * (len(outs) - 1),
        scratch_shapes=[
            vmem((total, width), BF),
            vmem((groups, SMALL_ROWS, SMALL_LANES), BF),
            vmem((width, 3 * cols), BF),
            vmem((2, total, cols), F32),
            vmem((n_sp + 1, 8, total), F32),
            vmem((2, total, HD), F32),
            vmem((2, total, HD), F32),
            vmem((total, cols), BF),
            vmem((2, 2 * total, cols), BF),
            vmem((heads_here, total, HD), F32),
            vmem((2, heads_here, total, HD), F32),
            vmem((total, cols), BF),
            vmem((total, width), BF),
        ]
        + [dma((count,)) for count in counts],
        compiler_params=pltpu.CompilerParams(
            collective_id=1, has_side_effects=True, vmem_limit_bytes=56 * 2**20
        ),
    )(x_own, small_own, qkv, rest, shard_in, shard_out, text, cot, time_rows, jnp.asarray(table))


def normal(values):
    centre = values - jnp.mean(values, axis=-1, keepdims=True)
    spread = lax.rsqrt(jnp.mean(centre * centre, axis=-1, keepdims=True) + EPS)
    return centre * spread, spread


def normal_back(normed, spread, grad):
    lean = jnp.mean(grad, axis=-1, keepdims=True)
    tilt = jnp.mean(grad * normed, axis=-1, keepdims=True)
    return spread * (grad - lean - normed * tilt)


def column_total(values):
    return jnp.sum(values.astype(F32), 0, keepdims=True)


def wide_dot(dst, left, right, call=mm, tile=512, add=None):
    across = dst.shape[-1]
    for start in range(0, across, tile):
        at = pl.ds(start, min(tile, across - start))
        value = call(left, right[:, at])
        if add is not None:
            value = value + add[:, at]
        dst[:, at] = value.astype(dst.dtype)


def wide_dot_t(dst, left, right, tile=512, add=None):
    across = dst.shape[-1]
    for start in range(0, across, tile):
        at = pl.ds(start, min(tile, across - start))
        value = mm_t(left, right[at, :])
        if add is not None:
            value = value + add[:, at]
        dst[:, at] = value.astype(dst.dtype)


def rest_loads(rest_ref, goals, sems, order):
    width = goals[0].shape[1]
    copies = {}
    for slot in order:
        copies[slot] = pltpu.make_async_copy(
            rest_ref.at[:, pl.ds(slot * width, width)], goals[slot], sems.at[slot]
        )
        copies[slot].start()
    return copies


def own_kernel(
    len_ref,
    rest_ref,
    x_ref,
    att_ref,
    text_ref,
    time_ref,
    par_ref,
    a_out,
    one_out,
    cin_out,
    ql_out,
    kl_out,
    q_out,
    kv_out,
    lse_out,
    oc_out,
    two_out,
    h2_out,
    w_o,
    w_co,
    w_cq,
    w_ck,
    w_cv,
    sems,
):
    loads = rest_loads(rest_ref, (w_o, w_co, w_cq, w_ck, w_cv), sems, (0, 2, 3, 4, 1))
    mods = time_ref[...] + par_ref[0:6, :]
    width = x_ref.shape[1]
    loads[0].wait()
    wide_dot(a_out, att_ref[...], w_o, add=par_ref.at[14:15])
    x_one = x_ref[...].astype(F32) + mods[2:3] * a_out[...]
    one_out[...] = x_one
    normed, _ = normal(x_one)
    cin_out[...] = (normed * par_ref[8:9, :] + par_ref[19:20, :]).astype(BF)
    loads[2].wait()
    wide_dot(ql_out, cin_out[...], w_cq, add=par_ref.at[15:16])
    value = ql_out[...]
    rho = lax.rsqrt(jnp.mean(value * value, axis=-1, keepdims=True) + EPS)
    q_out[...] = (value * rho * par_ref[9:10, :]).astype(BF)
    loads[3].wait()
    wide_dot(kl_out, text_ref[...], w_ck, add=par_ref.at[16:17])
    value = kl_out[...]
    rho = lax.rsqrt(jnp.mean(value * value, axis=-1, keepdims=True) + EPS)
    kv_out[0] = (value * rho * par_ref[10:11, :]).astype(BF)
    loads[4].wait()
    wide_dot(kv_out.at[1], text_ref[...], w_cv, add=par_ref.at[17:18])
    texts = text_ref.shape[0]
    rows = x_ref.shape[0]
    valid = lax.broadcasted_iota(jnp.int32, (rows, texts), 1) < len_ref[0]

    def attend(h, carry):
        head = lanes_at(h * HD, HD)
        scores = mm_t(q_out[:, head], kv_out[0, :, head]) * (HD ** (-0.5))
        scores = jnp.where(valid, scores, NEG)
        top = jnp.max(scores, -1, keepdims=True)
        raised = jnp.exp(scores - top)
        total = jnp.sum(raised, -1, keepdims=True)
        result = mm((raised / total).astype(BF), kv_out[1, :, head])
        oc_out[:, head] = result.astype(BF)
        lse_out[h] = jnp.broadcast_to(top + jnp.log(total), (rows, HD))
        return carry

    lax.fori_loop(0, width // HD, attend, 0)
    loads[1].wait()
    wide_dot(two_out, oc_out[...], w_co, add=par_ref.at[18:19])
    x_two = one_out[...] + two_out[...]
    two_out[...] = x_two
    normed, _ = normal(x_two)
    h2_out[...] = (normed * (1.0 + mods[4:5]) + mods[3:4]).astype(BF)


def own_tokens(lengths, rest, x_own, att_tok, text, time_rows, params):
    rows, width = x_own.shape
    texts = text.shape[0]
    shape = jax.ShapeDtypeStruct
    in_vmem = pl.BlockSpec(memory_space=pltpu.VMEM)
    weight = pltpu.VMEM((width, width), BF)
    names = ("a", "one", "cin", "ql", "kl", "q", "kv", "lse", "oc", "two", "h2")
    outs = (
        shape((rows, width), F32),
        shape((rows, width), F32),
        shape((rows, width), BF),
        shape((rows, width), F32),
        shape((texts, width), F32),
        shape((rows, width), BF),
        shape((2, texts, width), BF),
        shape((width // HD, rows, HD), F32),
        shape((rows, width), BF),
        shape((rows, width), F32),
        shape((rows, width), BF),
    )
    results = pl.pallas_call(
        own_kernel,
        out_shape=outs,
        in_specs=[
            pl.BlockSpec(memory_space=pltpu.SMEM),
            pl.BlockSpec(memory_space=pl.ANY),
        ]
        + [in_vmem] * 5,
        out_specs=(in_vmem,) * len(outs),
        scratch_shapes=[weight] * 5 + [pltpu.SemaphoreType.DMA((5,))],
        compiler_params=pltpu.CompilerParams(vmem_limit_bytes=58 * 2**20),
    )(lengths, rest, x_own, att_tok, text, time_rows, params)
    return types.SimpleNamespace(**dict(zip(names, results)))


def own_back_kernel(names, *refs):
    ref = types.SimpleNamespace(**dict(zip(names, refs)))
    sems, out_sem = ref.sems, ref.out_sem
    w_a, w_b, w_c = (getattr(ref, name) for name in ("w_a", "w_b", "w_c"))
    loads = rest_loads(ref.rest, (w_a, w_a, w_b, w_c, w_b), sems, (1, 2, 3))
    par_ref, sums = ref.par, ref.sums
    mods = ref.time[...] + par_ref[0:6, :]
    rows, width = ref.x_two.shape
    texts = ref.text_in.shape[0]
    sums[...] = jnp.zeros(sums.shape, F32)
    grad_y = ref.cot[...].astype(F32)
    sums[20:21, :] = column_total((grad_y * mods[5:6]).astype(BF))
    d_rows = ref.d_rows[...]
    normed, spread = normal(ref.x_two[...])
    sums[3:4, :] = column_total(d_rows)
    sums[4:5, :] = column_total(d_rows * normed)
    dx_ref = ref.dx
    dx_ref[...] = grad_y + normal_back(normed, spread, d_rows * (1.0 + mods[4:5]))
    low_ref = ref.low
    low_ref[...] = dx_ref[...].astype(BF)
    sums[18:19, :] = column_total(low_ref[...])

    saves = []

    def weight_grad(name, left, right, column=0):
        stage = ref.stage
        tile = 384
        for k, start in enumerate(range(0, width, tile)):
            slot = len(saves) % 2
            if len(saves) >= 2:
                saves[-2].wait()
            stage[slot] = mm_first(left[:, start : start + tile], right[...]).astype(BF)
            copy = pltpu.make_async_copy(
                stage.at[slot],
                getattr(ref, name).at[pl.ds(start, tile), pl.ds(column, width)],
                out_sem.at[slot],
            )
            copy.start()
            saves.append(copy)

    weight_grad("co", ref.oc, low_ref)
    loads[1].wait()
    doc_ref = ref.doc
    wide_dot_t(doc_ref, low_ref[...], w_a)
    loads.update(rest_loads(ref.rest, (w_a,), sems, (0,)))
    dq_ref, dkv_ref = ref.dq, ref.dkv
    q_ref, kv_ref = ref.q, ref.kv
    scale = HD ** (-0.5)
    valid = lax.broadcasted_iota(jnp.int32, (rows, texts), 1) < ref.len[0]

    def attend(h, carry):
        head = lanes_at(h * HD, HD)
        query, keys, grad = q_ref[:, head], kv_ref[0, :, head], doc_ref[:, head]
        scores = mm_t(query, keys) * scale
        scores = jnp.where(valid, scores, NEG)
        probs = jnp.exp(scores - ref.lse[h, :, 0:1])
        dkv_ref[1, :, head] = mm_first(probs.astype(BF), grad)
        d_probs = mm_t(grad, kv_ref[1, :, head])
        lean = jnp.sum(probs * d_probs, -1, keepdims=True)
        d_scores = (probs * (d_probs - lean)).astype(BF)
        dq_ref[:, head] = mm(d_scores, keys) * scale
        dkv_ref[0, :, head] = mm_first(d_scores, query) * scale
        return carry

    lax.fori_loop(0, width // HD, attend, 0)

    def rms_back(value, gain, grad):
        rho = lax.rsqrt(jnp.mean(value * value, axis=-1, keepdims=True) + EPS)
        lean = jnp.mean(value * gain * grad, axis=-1, keepdims=True)
        return (
            rho * gain * grad - value * (rho * rho * rho * lean),
            jnp.sum(grad * value * rho, 0, keepdims=True),
        )

    back_q, gain_q = rms_back(ref.ql[...], par_ref[9:10, :], dq_ref[...])
    low_ref[...] = back_q.astype(BF)
    sums[9:10, :] = gain_q
    sums[15:16, :] = column_total(low_ref[...])
    loads[2].wait()
    wide_dot_t(dq_ref, low_ref[...], w_b)
    loads.update(rest_loads(ref.rest, (w_b,) * 5, sems, (4,)))
    d_cin = dq_ref[...]
    normed, spread = normal(ref.x_one[...])
    sums[8:9, :] = column_total(d_cin * normed)
    sums[19:20, :] = column_total(d_cin)
    dx_ref[...] += normal_back(normed, spread, d_cin * par_ref[8:9, :])
    weight_grad("cq", ref.cin, low_ref)
    sums[2:3, :] = column_total(dx_ref[...] * ref.a[...])
    low_ref[...] = (dx_ref[...] * mods[2:3]).astype(BF)
    sums[14:15, :] = column_total(low_ref[...])
    loads[0].wait()
    wide_dot_t(ref.d_att, low_ref[...], w_a)
    weight_grad("o", ref.att, low_ref)
    back_k, gain_k = rms_back(ref.kl[...], par_ref[10:11, :], dkv_ref[0])
    sums[10:11, :] = gain_k
    klow_ref, vlow_ref = ref.klow, ref.vlow
    klow_ref[...] = back_k.astype(BF)
    vlow_ref[...] = dkv_ref[1].astype(BF)
    sums[16:17, :] = column_total(klow_ref[...])
    sums[17:18, :] = column_total(vlow_ref[...])
    weight_grad("ckv", ref.text_in, klow_ref)
    weight_grad("ckv", ref.text_in, vlow_ref, width)
    loads[3].wait()
    wide_dot_t(dkv_ref.at[0], klow_ref[...], w_c)
    loads[4].wait()
    wide_dot_t(ref.text_part, vlow_ref[...], w_b, add=dkv_ref.at[0])
    for copy in saves[-2:]:
        copy.wait()


def own_back(**values):
    arrays = types.SimpleNamespace(**values)
    shape = jax.ShapeDtypeStruct
    rows, width = arrays.x_two.shape
    texts = arrays.text_in.shape[0]
    in_any = ["rest"]
    ins = ["x_two", "x_one", "d_rows", "cot", "time", "par", "a", "cin", "ql", "kl", "q", "kv"]
    ins += ["lse", "oc", "att", "text_in"]
    any_outs = {name: shape((width, width), BF) for name in ("o", "co", "cq")}
    any_outs.update(ckv=shape((width, 2 * width), BF))
    outs = dict(
        d_att=shape((rows, width), BF),
        dx=shape((rows, width), F32),
        text_part=shape((texts, width), BF),
        sums=shape((32, width), F32),
    )
    vmem = pltpu.VMEM
    weight = vmem((width, width), BF)
    scratch = {name: weight for name in ("w_a", "w_b", "w_c")}
    scratch.update(
        dict(
            low=vmem((rows, width), BF),
            doc=vmem((rows, width), BF),
            dq=vmem((rows, width), F32),
            dkv=vmem((2, texts, width), F32),
            klow=vmem((texts, width), BF),
            vlow=vmem((texts, width), BF),
            stage=vmem((2, 384, width), BF),
            sems=pltpu.SemaphoreType.DMA((5,)),
            out_sem=pltpu.SemaphoreType.DMA((2,)),
        )
    )
    any_place = pl.BlockSpec(memory_space=pl.ANY)
    in_vmem = pl.BlockSpec(memory_space=pltpu.VMEM)
    names = ["len"] + in_any + ins + list(any_outs) + list(outs) + list(scratch)
    results = pl.pallas_call(
        functools.partial(own_back_kernel, names),
        out_shape=tuple(any_outs.values()) + tuple(outs.values()),
        in_specs=[pl.BlockSpec(memory_space=pltpu.SMEM), any_place] + [in_vmem] * len(ins),
        out_specs=(any_place,) * len(any_outs) + (in_vmem,) * len(outs),
        scratch_shapes=list(scratch.values()),
        compiler_params=pltpu.CompilerParams(vmem_limit_bytes=60 * 2**20),
    )(*[getattr(arrays, name) for name in ["len"] + in_any + ins])
    return types.SimpleNamespace(**dict(zip(list(any_outs) + list(outs), results)))


def feed_kernel(n_sp, names, *refs):
    ref = types.SimpleNamespace(**dict(zip(names, refs)))
    zs, zr, ds, dr, local, cs, cr, saves_sem = (
        getattr(ref, name) for name in ("zs", "zr", "ds", "dr", "local", "cs", "cr", "saves")
    )
    spot_d = lax.axis_index(DP)
    spot_s = lax.axis_index(SP)
    core = lax.rem(spot_d, 2)
    core_id = {DP: spot_d + 1 - 2 * core}
    line = [{SP: lax.rem(spot_s + step, n_sp)} for step in range(1, n_sp)]
    h2_ref, all_ref = ref.h2, ref.h2_all
    rows, width = h2_ref.shape
    hidden = ref.in_own.shape[0]
    win, wout = ref.win, ref.wout
    meet(line + [core_id])

    pieces = 2
    piece = rows // pieces

    def token_copy(way, k, part):
        block = spot_s - k if way == 0 else spot_s + k
        at = all_ref.at[rows_at(block * rows + part * piece, piece)]
        src = h2_ref.at[pl.ds(part * piece, piece)] if k == 0 else at
        target = {SP: spot_s + 1 if way == 0 else spot_s - 1}
        index = (way * (n_sp - 1) + k) * pieces + part
        return remote_copy(src, at, zs.at[index], zr.at[index], target)

    def sends(way, k):
        if way == 0:
            return jnp.logical_and(spot_s < n_sp - 1, spot_s >= k)
        return jnp.logical_and(spot_s > 0, spot_s + k < n_sp)

    def gets(way, k):
        return spot_s > k if way == 0 else spot_s + k + 1 < n_sp

    def token_step(k):
        for part in range(pieces):
            for way in range(2):
                if k > 0:

                    @pl.when(gets(way, k - 1))
                    def _():
                        token_copy(way, k - 1, part).wait_recv()

                if k < n_sp - 1:

                    @pl.when(sends(way, k))
                    def _():
                        token_copy(way, k, part).start()

    token_step(0)
    keep = pltpu.make_async_copy(h2_ref, all_ref.at[rows_at(spot_s * rows, rows)], local.at[0])
    keep.start()
    loads = [
        pltpu.make_async_copy(getattr(ref, src), goal.at[pl.ds(part * hidden, hidden)], local.at[1 + k])
        for k, (src, goal, part) in enumerate(
            (("in_own", win, 0), ("in_other", win, 1), ("out_own", wout, 0), ("out_other", wout, 1))
        )
    ]
    for copy in loads:
        copy.start()
    gate = ref.time[5:6, :] + ref.par[5:6, :]
    ref.du_sums[...] = jnp.zeros(ref.du_sums.shape, F32)
    cot_ref, dz_ref, g_ref, du_ref = ref.cot, ref.dz, ref.g, ref.du
    z_ref, part_ref, recv_ref, own_ref = ref.z, ref.part, ref.recv, ref.own
    tiles = []
    start = 0
    while start < 2 * hidden:
        tiles.append((start, min(768, 2 * hidden - start)))
        start += 768
    bend = (2.0 / np.pi) ** 0.5
    keep.wait()
    for copy in loads:
        copy.wait()

    def near(k):
        first = (spot_s >= k).astype(jnp.int32)
        return first, first + (spot_s + k < n_sp).astype(jnp.int32)

    def grad_copy(block, owner):
        return remote_copy(
            part_ref.at[block],
            recv_ref.at[spot_s],
            ds.at[block],
            dr.at[owner],
            {SP: block},
        )

    def one(i, carry):
        block = spot_s
        before = jnp.int32(1)
        for k in range(1, n_sp):
            first, count = near(k)

            @pl.when(i == before)
            def _(k=k):
                token_step(k)

            here = jnp.logical_and(i >= before, i < before + count)
            ahead = jnp.logical_and(first == 1, i == before)
            block = jnp.where(here, jnp.where(ahead, spot_s - k, spot_s + k), block)
            before = before + count
        at = rows_at(block * rows, rows)
        dz_ref[at, :] = (cot_ref[at, :].astype(F32) * gate).astype(BF)
        for start, size in tiles:
            place = pl.ds(start, size)
            u = mm_t(all_ref[at, :], win[place, :]) + ref.bias[:, place]
            cube = bend * (u + 0.044715 * (u * u * u))
            t = jnp.tanh(cube)
            g_ref[at, place] = (0.5 * u * (1.0 + t)).astype(BF)
            slope = 0.5 * (1.0 + t) + (0.5 * bend) * u * (1.0 - t * t) * (
                1.0 + (3 * 0.044715) * (u * u)
            )
            grad = (mm_t(dz_ref[at, :], wout[place, :]) * slope).astype(BF)
            du_ref[at, place] = grad
            ref.du_sums[:, place] += column_total(grad)
        for start in range(0, width, 512):
            place = pl.ds(start, 512)
            value = mm(du_ref[at, :], win[:, place])
            part_ref[block, :, place] = value.astype(BF)

            @pl.when(i == 0)
            def _():
                own_ref[:, place] = value

        @pl.when(i > 0)
        def _():
            grad_copy(block, spot_s).start()

        for start in range(0, width, 512):
            place = pl.ds(start, 512)
            z_ref[block, :, place] = mm(g_ref[at, :], wout[:, place]).astype(BF)
        return carry

    lax.fori_loop(0, n_sp, one, 0)
    z_save = pltpu.make_async_copy(z_ref, ref.z_out, local.at[5])
    z_save.start()

    def weight_grad(goal, left, right):
        start = 0
        while start < 2 * hidden:
            size = min(256, 2 * hidden - start)
            goal[start : start + size, :] = mm_first(
                left[:, start : start + size], right[...]
            ).astype(BF)
            start += size

    half = hidden // 2
    core_copies = []

    def core_hop(which, goal):
        for part in range(2):
            copy = remote_copy(
                goal.at[rows_at(part * hidden + (1 - core) * half, half)],
                ref.core_recv.at[which, part],
                cs.at[2 * which + part],
                cr.at[2 * which + part],
                core_id,
            )
            copy.start()
            core_copies.append(copy)

    weight_grad(win, du_ref, all_ref)
    core_hop(0, win)
    weight_grad(wout, g_ref, dz_ref)
    core_hop(1, wout)
    low_ref = ref.core_recv
    out_copies = []
    chunk = half // 5
    for which, goal in enumerate((win, wout)):
        for part in range(2):
            core_copies[2 * which + part].wait_recv()
            for k in range(5):
                at = rows_at(part * hidden + core * half + k * chunk, chunk)
                value = goal[at, :].astype(F32) + low_ref[
                    which, part, k * chunk : (k + 1) * chunk
                ].astype(F32)
                low_ref[which, part, k * chunk : (k + 1) * chunk] = value.astype(BF)
            copy = pltpu.make_async_copy(
                low_ref.at[which, part],
                (ref.fi_own, ref.fi_far, ref.fo_own, ref.fo_far)[2 * which + part],
                saves_sem.at[2 * which + part],
            )
            copy.start()
            out_copies.append(copy)
    for step in range(1, n_sp):
        other = lax.rem(spot_s + step, n_sp)
        grad_copy(other, other).wait_recv()
    total = own_ref[...]
    for step in range(1, n_sp):
        total = total + recv_ref[lax.rem(spot_s + step, n_sp)].astype(F32)
    ref.d_rows[...] = total
    for copy in out_copies + [z_save]:
        copy.wait()
    for copy in core_copies:
        copy.wait_send()
    for step in range(1, n_sp):
        other = lax.rem(spot_s + step, n_sp)
        grad_copy(other, other).wait_send()
    for k in range(n_sp - 1):
        for part in range(pieces):
            for way in range(2):

                @pl.when(sends(way, k))
                def _():
                    token_copy(way, k, part).wait_send()


def feed(**values):
    arrays = types.SimpleNamespace(**values)
    n_sp = lax.axis_size(SP)
    shape = jax.ShapeDtypeStruct
    rows, width = arrays.h2.shape
    hidden = arrays.in_own.shape[0]
    total = n_sp * rows
    ins_any = ["in_own", "in_other", "out_own", "out_other", "h2"]
    ins = ["cot", "bias", "time", "par"]
    any_outs = dict(
        z_out=shape((n_sp, rows, width), BF),
        fi_own=shape((hidden // 2, width), BF),
        fi_far=shape((hidden // 2, width), BF),
        fo_own=shape((hidden // 2, width), BF),
        fo_far=shape((hidden // 2, width), BF),
    )
    outs = {"d_rows": shape((rows, width), F32), "du_sums": shape((1, 2 * hidden), F32)}
    vmem = pltpu.VMEM
    dma = pltpu.SemaphoreType.DMA
    scratch = dict(
        h2_all=vmem((total, width), BF),
        win=vmem((2 * hidden, width), BF),
        wout=vmem((2 * hidden, width), BF),
        dz=vmem((total, width), BF),
        g=vmem((total, 2 * hidden), BF),
        du=vmem((total, 2 * hidden), BF),
        z=vmem((n_sp, rows, width), BF),
        part=vmem((n_sp, rows, width), BF),
        recv=vmem((n_sp, rows, width), BF),
        own=vmem((rows, width), F32),
        core_recv=vmem((2, 2, hidden // 2, width), BF),
        zs=dma((4 * (n_sp - 1),)),
        zr=dma((4 * (n_sp - 1),)),
        ds=dma((n_sp,)),
        dr=dma((n_sp,)),
        local=dma((6,)),
        cs=dma((4,)),
        cr=dma((4,)),
        saves=dma((4,)),
    )
    any_place = pl.BlockSpec(memory_space=pl.ANY)
    in_vmem = pl.BlockSpec(memory_space=pltpu.VMEM)
    names = ins_any + ins + list(any_outs) + list(outs) + list(scratch)
    results = pl.pallas_call(
        functools.partial(feed_kernel, n_sp, names),
        out_shape=tuple(any_outs.values()) + tuple(outs.values()),
        in_specs=[any_place] * len(ins_any) + [in_vmem] * len(ins),
        out_specs=(any_place,) * len(any_outs) + (in_vmem,) * len(outs),
        scratch_shapes=list(scratch.values()),
        compiler_params=pltpu.CompilerParams(
            collective_id=3, has_side_effects=True, vmem_limit_bytes=60 * 2**20
        ),
    )(*[getattr(arrays, name) for name in ins_any + ins])
    return types.SimpleNamespace(**dict(zip(list(any_outs) + list(outs), results)))


class Later:
    def __init__(self, make):
        self.make = make

    def wait_recv(self):
        self.make().wait_recv()

    def wait_send(self):
        self.make().wait_send()


def back_kernel(n_sp, n_dp, names, *refs):
    ref = types.SimpleNamespace(**dict(zip(names, refs)))
    sem_send, sem_recv, sem_local = ref.send, ref.recv, ref.local
    spot_d = lax.axis_index(DP)
    spot_b = lax.axis_index(BLK)
    spot_s = lax.axis_index(SP)
    core = lax.rem(spot_d, 2)
    pair = lax.rem(spot_d // 2, 2)

    def dp_id(bit):
        return {DP: spot_d + bit - 2 * bit * lax.rem(spot_d // bit, 2)}

    bits = []
    bit = 4
    while bit < n_dp:
        bits.append(bit)
        bit *= 2
    core_id, pair_id, blk_id = dp_id(1), dp_id(2), {BLK: 1 - spot_b}
    line = [{SP: lax.rem(spot_s + step, n_sp)} for step in range(1, n_sp)]
    used = [0]
    sent = []

    def send(src, dst, target, view=None):
        index = used[0]
        used[0] += 1
        copy = remote_copy(src, dst, sem_send.at[index], sem_recv.at[index], target)
        copy.start()
        if view is not None:
            copy = Later(
                lambda: remote_copy(
                    view(), view(), sem_send.at[index], sem_recv.at[index], target
                )
            )
        sent.append(copy)
        return copy

    def add_blocks(dst, sources):
        lead = len(dst.shape) - 2

        def body(*blocks):
            total = blocks[0][...].astype(F32)
            for block in blocks[1:-1]:
                total = total + block[...].astype(F32)
            blocks[-1][...] = total.astype(blocks[-1].dtype)

        if lead == 0:
            grid = (dst.shape[0] // 16,)
            spec = pl.BlockSpec((16, dst.shape[1]), lambda place: (place, 0))
        else:
            group = 1
            each = 2 * int(np.prod(dst.shape[1:]))
            while dst.shape[0] % (2 * group) == 0 and 2 * group * each <= 700_000:
                group *= 2
            grid = (dst.shape[0] // group,)
            spec = pl.BlockSpec(
                (group,) + tuple(dst.shape[1:]), lambda place: (place,) + (0,) * (lead + 1)
            )
        pltpu.emit_pipeline(
            body,
            grid=grid,
            in_specs=[spec] * len(sources),
            out_specs=[spec],
        )(*sources, dst)

    meet(line + [core_id, pair_id, blk_id] + [dp_id(bit) for bit in bits])
    d_att, do_ref = ref.d_att, ref.do
    rows = d_att.shape[0]
    total_rows = n_sp * rows
    cols = do_ref.shape[1]
    heads_here = cols // HD
    width = d_att.shape[1]

    def tok(block):
        return rows_at(block * rows, rows)

    do_own = pltpu.make_async_copy(
        d_att.at[:, lanes_at(spot_s * cols, cols)], do_ref.at[tok(spot_s)], sem_local.at[0]
    )
    do_own.start()
    do_away = [
        send(
            d_att.at[:, lanes_at(lax.rem(spot_s + step, n_sp) * cols, cols)],
            do_ref.at[tok(spot_s)],
            line[step - 1],
        )
        for step in range(1, n_sp)
    ]
    groups = ("co", "ckv")
    hop = {}
    for name in groups:
        hop[name] = send(getattr(ref, name).at[:, 1 - core], getattr(ref, name + "_rc"), core_id)
    hop["text"] = send(ref.text.at[1 - spot_b], ref.text_rx, blk_id)

    blocks8 = 2 * n_sp

    def core_done(name):
        hop[name].wait_recv()
        add_blocks(getattr(ref, name + "_kc"), [getattr(ref, name).at[:, core], getattr(ref, name + "_rc")])

    score_scale = HD ** (-0.5)
    dq_ref, dkv_ref = ref.dq, ref.dkv

    def ff_last(name):
        at = getattr(ref, name + "_out").at[core]
        ry = getattr(ref, name + "_ry")
        kx = getattr(ref, name + "_kx")
        hop[name].wait_recv()
        for k in range(len(bits) + 1):
            goal = at if k == len(bits) else getattr(ref, name + "_ky").at[k]
            source = kx if k == 0 else getattr(ref, name + "_ky").at[k - 1]
            add_blocks(goal, [source, ry.at[k]])
            if k < len(bits):
                send(goal, ry.at[k + 1], dp_id(bits[k])).wait_recv()
        hop[name] = send(at, at, core_id)

    def pair_done(name, go=True):
        if name in hop:
            hop[name].wait_recv()
            add_blocks(getattr(ref, name + "_ky"), [getattr(ref, name + "_kc").at[:, pair], getattr(ref, name + "_ry")])
            del hop[name]
        if not go:
            return
        hop[name] = send(
            getattr(ref, name + "_ky").at[pl.ds((1 - spot_b) * n_sp, n_sp)], getattr(ref, name + "_rx"), blk_id
        )

    def blk_done(name):
        hop[name].wait_recv()
        own_blk = getattr(ref, name + "_ky").at[pl.ds(spot_b * n_sp, n_sp)]
        add_blocks(getattr(ref, name + "_kx"), [own_blk, getattr(ref, name + "_rx")])

    def line_send(name):
        hop[name] = [
            send(
                getattr(ref, name + "_kx").at[lax.rem(spot_s + step, n_sp)],
                getattr(ref, name + "_rz").at[step - 1],
                line[step - 1],
            )
            for step in range(1, n_sp)
        ]

    def first_blk_done(name):
        hop[name].wait_recv()
        own_blk = getattr(ref, name + "_kc").at[pl.ds(spot_b * n_sp, n_sp)]
        add_blocks(getattr(ref, name + "_ky"), [own_blk, getattr(ref, name + "_rx")])
        hop[name] = send(getattr(ref, name + "_ky").at[:, 1 - pair], getattr(ref, name + "_ry"), pair_id)

    def then_pair_done(name):
        hop[name].wait_recv()
        add_blocks(getattr(ref, name + "_kx"), [getattr(ref, name + "_ky").at[:, pair], getattr(ref, name + "_ry")])
        line_send(name)

    def attention(q_here, kv_here, lse_here):
        ref.q_here, ref.kv_here, ref.lse_here = q_here, kv_here, lse_here
        loads = [
            pltpu.make_async_copy(getattr(ref, name), getattr(ref, name + "_here"), sem_local.at[2 + k])
            for k, name in enumerate(("q", "kv", "lse"))
        ]
        for copy in loads:
            copy.start()
        q_ref, kv_ref, lse_ref = ref.q_here, ref.kv_here, ref.lse_here
        dkv_ref[...] = jnp.zeros(dkv_ref.shape, F32)

        def attend(block, carry):
            at = tok(block)
            for h in range(heads_here):
                head = pl.ds(h * HD, HD)
                query = q_ref[at, head]
                grad = do_ref[at, head]
                keys = kv_ref[0, :, head]
                scores = mm_t(query, keys) * score_scale
                probs = jnp.exp(scores - lse_ref[h, at, 0:1])
                dkv_ref[1, :, head] += mm_first(probs.astype(BF), grad)
                d_probs = mm_t(grad, kv_ref[1, :, head])
                lean = jnp.sum(probs * d_probs, -1, keepdims=True)
                d_scores = (probs * (d_probs - lean)).astype(BF)
                dq_ref[at, head] = mm(d_scores, keys) * score_scale
                dkv_ref[0, :, head] += mm_first(d_scores, query) * score_scale
            return carry

        add_blocks(ref.fi_kx, [ref.fi, ref.fi_rx])
        goal = lambda: ref.fi_ry.at[0]
        hop["fi"] = send(ref.fi_kx, goal(), pair_id, goal)
        for copy in loads:
            copy.wait()
        do_own.wait()
        for copy in do_away:
            copy.wait_recv()
        lax.fori_loop(0, 1, attend, 0)
        core_done("co")
        goal = lambda: ref.co_rx
        hop["co"] = send(
            ref.co_kc.at[pl.ds((1 - spot_b) * n_sp, n_sp)], goal(), blk_id, goal
        )
        core_done("ckv")
        goal = lambda: ref.ckv_ry
        hop["ckv"] = send(ref.ckv_kc.at[:, 1 - pair], goal(), pair_id, goal)
        for name in ("cq", "o"):
            goal = lambda name=name: getattr(ref, name + "_rc")
            hop[name] = send(getattr(ref, name).at[:, 1 - core], goal(), core_id, goal)
        lax.fori_loop(1, 2, attend, 0)
        core_done("o")
        hop["o"] = []
        for step in range(1, n_sp):
            for half in range(2):
                goal = lambda step=step, half=half: ref.o_rz.at[step - 1, half]
                src = ref.o_kc.at[half * n_sp + lax.rem(spot_s + step, n_sp)]
                hop["o"].append(send(src, goal(), line[step - 1], goal))
        core_done("cq")
        lax.fori_loop(2, n_sp, attend, 0)

    pl.run_scoped(
        attention,
        pltpu.VMEM(ref.q.shape, BF),
        pltpu.VMEM(ref.kv.shape, BF),
        pltpu.VMEM(ref.lse.shape, F32),
    )

    kv_recv, proj_ref = ref.kv_recv, ref.proj
    kv_away = []
    for which in range(2):
        place = pl.ds(which * cols, cols)
        proj_ref[:, place] = dkv_ref[which, total_rows:, :].astype(BF)
        kv_away.append(send(proj_ref.at[:, place], kv_recv.at[which], blk_id))
    hop["text"].wait_recv()
    text_kx = ref.text_kx
    add_blocks(text_kx, [ref.text.at[spot_b], ref.text_rx])
    hop["text"] = [
        send(
            text_kx.at[lax.rem(spot_s + step, n_sp)],
            ref.text_rz.at[step - 1],
            line[step - 1],
        )
        for step in range(1, n_sp)
    ]

    lin_ref, rho_ref, trig_ref = ref.lin, ref.rho, ref.trig
    par_ref, sums_ref = ref.par, ref.sums
    sums_ref[spot_s] = jnp.zeros((8, total_rows), F32)

    def gain_of(which, h):
        return par_ref[6 + which : 7 + which, lanes_at(spot_s * cols + h * HD, HD)]

    def unturn(which, block, carry):
        at = tok(block)
        cosine = trig_ref[0, at, :]
        sine = trig_ref[1, at, :]
        lean = jnp.zeros((rows, HD), F32)
        for h in range(heads_here):
            head = pl.ds(h * HD, HD)
            if which == 0:
                grad = dq_ref[at, head]
            else:
                grad = dkv_ref[0, at, head] + kv_recv[0, at, head].astype(F32)
            grad = turned(grad, cosine, -sine)
            if which == 0:
                dq_ref[at, head] = grad
            else:
                dkv_ref[0, at, head] = grad
            lean = lean + lin_ref[which, at, head] * gain_of(which, h) * grad
        total = exact_sums(lean)
        sums_ref[spot_s, which : which + 1, lanes_at(block * rows, rows)] = total[0:1]
        return carry

    lax.fori_loop(0, n_sp, functools.partial(unturn, 0), 0)
    first_blk_done("co")
    ff_last("fi")
    for copy in kv_away:
        copy.wait()
    sent[:] = [copy for copy in sent if all(copy is not other for other in kv_away)]
    def first_blk_send(name):
        hop[name] = send(
            getattr(ref, name + "_kc").at[pl.ds((1 - spot_b) * n_sp, n_sp)], getattr(ref, name + "_rx"), blk_id
        )

    first_blk_send("cq")
    early, late = pl.ds(0, 2), pl.ds(2, 3)
    hop["fo"] = send(ref.fo_far.at[late], ref.fo_rx, blk_id)
    add_blocks(ref.fo_kx.at[early], [ref.fo.at[early], ref.fo_rx1])
    fo_early = send(ref.fo_kx.at[early], ref.fo_ry.at[0, early], pair_id)
    lax.fori_loop(0, n_sp, functools.partial(unturn, 1), 0)
    sums_away = [
        send(sums_ref.at[spot_s], sums_ref.at[spot_s], line[k]) for k in range(n_sp - 1)
    ]
    then_pair_done("co")
    for copy in hop["o"]:
        copy.wait_recv()
    for half in range(2):
        add_blocks(
            ref.o_kl.at[half],
            [ref.o_kc.at[half * n_sp + spot_s]]
            + [ref.o_rz.at[k, half] for k in range(n_sp - 1)],
        )
    hop["o"] = send(ref.o_kl.at[1 - spot_b], ref.o_rx, blk_id)
    for copy in sums_away:
        copy.wait_recv()
    means = sums_ref[0]
    for k in range(1, n_sp):
        means = means + sums_ref[k]
    sums_ref[n_sp] = means / width
    small_ref = ref.small
    own = lanes_at(spot_s * cols, cols)
    small_ref[0] = ref.small_in[...]
    small_ref[0, 5:6, :] = ref.gate2[...]
    small_ref[0, 21 : 21 + ref.hidden_rows.shape[0], :] = ref.hidden_rows[...]
    for row in (6, 7, 11, 12, 13):
        small_ref[0, row : row + 1, :] = jnp.zeros((1, width), F32)

    def project(block, carry):
        at = tok(block)
        for which in range(2):
            mean = exact_first(sums_ref[n_sp, :, lanes_at(block * rows, rows)], row_pick(which))
            rho = rho_ref[which, at, :]
            cube = rho * rho * rho * mean
            for h in range(heads_here):
                head = pl.ds(h * HD, HD)
                grad = dq_ref[at, head] if which == 0 else dkv_ref[0, at, head]
                value = lin_ref[which, at, head]
                low = (rho * gain_of(which, h) * grad - value * cube).astype(BF)
                place = pl.ds(which * cols + h * HD, HD)
                proj_ref[at, place] = low
                here = lanes_at(spot_s * cols + h * HD, HD)
                small_ref[0, 6 + which : 7 + which, here] += jnp.sum(
                    grad * value * rho, 0, keepdims=True
                )
                small_ref[0, 11 + which : 12 + which, here] += jnp.sum(
                    low.astype(F32), 0, keepdims=True
                )
        low = (dkv_ref[1, at, :] + kv_recv[1, at, :].astype(F32)).astype(BF)
        proj_ref[at, 2 * cols :] = low
        small_ref[0, 13:14, own] += jnp.sum(low.astype(F32), 0, keepdims=True)
        return carry

    lax.fori_loop(0, n_sp, project, 0)
    dh1_ref, dh1_recv, sw_ref = ref.dh1, ref.dh1_recv, ref.sw
    chain_send, chain_recv = ref.chain_send, ref.chain_recv

    def chain_copy(way, block):
        if way == 0:
            slot, target = block, {SP: spot_s + 1}
        else:
            slot = jnp.where(block == spot_s - 1, n_sp, block)
            target = {SP: spot_s - 1}
        return remote_copy(
            dh1_ref.at[block],
            dh1_recv.at[slot],
            chain_send.at[way * n_sp + block],
            chain_recv.at[slot],
            target,
        )

    def chain_wait(slot):
        at = dh1_recv.at[slot]
        remote_copy(at, at, chain_send.at[0], chain_recv.at[slot], blk_id).wait_recv()

    def chain_pass(way, block, slot):
        total = dh1_ref[block].astype(F32) + dh1_recv[slot].astype(F32)
        dh1_ref[block] = total.astype(BF)
        chain_copy(way, block).start()

    def chain_step(time):
        right = n_sp - 1 + spot_s - time
        inside = jnp.logical_and(right >= spot_s, right < n_sp)

        @pl.when(jnp.logical_and(spot_s > 0, inside))
        def _():
            chain_wait(right)

            @pl.when(right > spot_s)
            def _():
                chain_pass(0, right, right)

        left = time - (n_sp - 1 - spot_s)
        inside = jnp.logical_and(left >= 0, left <= spot_s)

        @pl.when(jnp.logical_and(spot_s < n_sp - 1, inside))
        def _():
            slot = jnp.where(left == spot_s, n_sp, left)
            chain_wait(slot)

            @pl.when(left < spot_s)
            def _():
                chain_pass(1, left, slot)

    def products(w_ref, h1_ref, stage):
        sw_copies = []
        w_load = pltpu.make_async_copy(ref.w, w_ref, sem_local.at[0])
        h1_load = pltpu.make_async_copy(ref.h1, h1_ref, sem_local.at[1])
        w_load.start()
        h1_load.start()
        w_load.wait()
        def away(step, carry):
            turn = jnp.where(spot_s < n_sp // 2, n_sp - step, step)
            block = lax.rem(spot_s + turn, n_sp)
            for part in range(width // cols):
                place = pl.ds(part * cols, cols)
                value = mm_t(proj_ref[tok(block), :], w_ref[place, :])
                dh1_ref[block, :, place] = value.astype(BF)

            @pl.when(spot_s == 0)
            def _():
                chain_copy(0, block).start()

            @pl.when(spot_s == n_sp - 1)
            def _():
                chain_copy(1, block).start()

            return carry

        lax.fori_loop(1, n_sp, away, 0)
        for part in range(width // cols):
            place = pl.ds(part * cols, cols)
            ref.dh1_own[:, place] = mm_t(proj_ref[tok(spot_s), :], w_ref[place, :])
        h1_load.wait()
        for part in range(n_sp):
            value = mm_first(h1_ref[:, part * cols : (part + 1) * cols], proj_ref[...])
            value = value.astype(BF)
            slot = part % 2
            if part > 1:
                sw_copies[part - 2].wait()
            for k in range(4):
                half = cols // 4
                stage[slot, k // 2, k % 2] = value[k * half : (k + 1) * half]
            copy = pltpu.make_async_copy(
                stage.at[slot], sw_ref.at[pl.ds(2 * part, 2)], sem_local.at[2 + slot]
            )
            copy.start()
            sw_copies.append(copy)
        for copy in sw_copies[-2:]:
            copy.wait()
        hop["s"] = send(
            sw_ref.at[:, 1 - core], ref.s_rc, core_id, lambda: ref.s_rc
        )

    pl.run_scoped(
        products,
        pltpu.VMEM(ref.w.shape, BF),
        pltpu.VMEM(ref.h1.shape, BF),
        pltpu.VMEM((2, 2, 2, cols // 4, 3 * cols), BF),
    )

    pair_done("ckv")
    chain_step(1)
    hop["s"].wait_recv()
    add_blocks(ref.s_kc, [ref.sw.at[:, core], ref.s_rc])
    hop["s"] = send(ref.s_kc.at[pl.ds((1 - spot_b) * n_sp, n_sp)], ref.s_rx, blk_id)
    hop["o"].wait_recv()
    add_blocks(ref.o_kx, [ref.o_kl.at[spot_b], ref.o_rx])
    hop["o"] = send(ref.o_kx.at[1 - pair], ref.o_ry, pair_id)
    first_blk_done("cq")
    for k in range(2, n_sp - 1):
        chain_step(k)
    hop["fo"].wait_recv()
    add_blocks(ref.fo_kx.at[late], [ref.fo.at[late], ref.fo_rx])
    hop["fo"] = send(ref.fo_kx.at[late], ref.fo_ry.at[0, late], pair_id)
    then_pair_done("cq")
    for copy in hop["text"]:
        copy.wait_recv()
    add_blocks(
        ref.text_out.at[0],
        [text_kx.at[spot_s]] + [ref.text_rz.at[k] for k in range(n_sp - 1)],
    )

    chain_step(n_sp - 1)

    @pl.when(spot_s > 0)
    def _():
        ref.dh1_own[...] += dh1_recv[spot_s].astype(F32)

    @pl.when(spot_s < n_sp - 1)
    def _():
        ref.dh1_own[...] += dh1_recv[n_sp].astype(F32)

    d_shift = ref.dh1_own[...]
    values = ref.x[...].astype(F32)
    centre = values - jnp.mean(values, axis=-1, keepdims=True)
    spread = lax.rsqrt(jnp.mean(centre * centre, axis=-1, keepdims=True) + EPS)
    normed = centre * spread
    scale = 1.0 + (ref.time[1:2, :] + par_ref[1:2, :])
    grad = d_shift * scale
    lean = jnp.mean(grad, axis=-1, keepdims=True)
    tilt = jnp.mean(grad * normed, axis=-1, keepdims=True)
    ref.tokens_out[...] = ref.dx1[...] + spread * (grad - lean - normed * tilt)
    small_ref[0, 0:1, :] = jnp.sum(d_shift, 0, keepdims=True)
    small_ref[0, 1:2, :] = jnp.sum(d_shift * normed, 0, keepdims=True)
    partners = [core_id, pair_id] + [dp_id(bit) for bit in bits] + [blk_id]
    bit = 1
    while bit < n_sp:
        partners.append({SP: spot_s + bit - 2 * bit * lax.rem(spot_s // bit, 2)})
        bit *= 2

    def small_send(k):
        hop["small"] = send(small_ref.at[k], ref.small_recv.at[k], partners[k])

    def small_done(k):
        hop["small"].wait_recv()
        small_ref[k + 1] = small_ref[k] + ref.small_recv[k]
        if k + 1 < len(partners):
            small_send(k + 1)
        else:
            ref.small_out[...] = small_ref[k + 1]

    small_send(0)
    blk_done("ckv")
    line_send("ckv")
    hop["s"].wait_recv()
    own_blk = ref.s_kc.at[pl.ds(spot_b * n_sp, n_sp)]
    add_blocks(ref.s_kx, [own_blk, ref.s_rx])
    small_done(0)
    s_line = []
    s_keep = []
    for j in range(3):
        place = lanes_at(j * width + spot_s * cols, cols)
        part = pl.ds(j * cols, cols)
        copy = pltpu.make_async_copy(
            ref.s_kx.at[spot_s, :, part], ref.s_z.at[:, place], sem_local.at[2 + j]
        )
        copy.start()
        s_keep.append(copy)
        for step in range(1, n_sp):
            s_line.append(
                send(
                    ref.s_kx.at[lax.rem(spot_s + step, n_sp), :, part],
                    ref.s_z.at[:, place],
                    line[step - 1],
                )
            )
    def line_done(name):
        if name == "o":
            hop[name].wait_recv()
        else:
            for copy in hop[name]:
                copy.wait_recv()
        kx = getattr(ref, name + "_kx")
        out = getattr(ref, name + "_out").at[core]
        kz = getattr(ref, name + "_kz")
        if name == "o":
            add_blocks(kz.at[0], [kx.at[pair], ref.o_ry])
        else:
            rz = getattr(ref, name + "_rz")
            add_blocks(kz.at[0], [kx.at[spot_s]] + [rz.at[k] for k in range(n_sp - 1)])
        for k, bit in enumerate(bits):
            got = getattr(ref, name + "_rw").at[k]
            send(kz.at[k], got, dp_id(bit)).wait_recv()
            add_blocks(kz.at[k + 1], [kz.at[k], got])
        last = kz.at[len(bits)]
        own_copy = pltpu.make_async_copy(last, out.at[pair], sem_local.at[1])
        own_copy.start()
        hop[name] = send(last, out.at[pair], pair_id)
        own_copy.wait()

    def pair_back(name):
        hop[name].wait_recv()
        out = getattr(ref, name + "_out").at[core]
        hop[name] = send(out, out, core_id)

    small_done(1)
    line_done("o")
    line_done("co")
    for k in range(2, len(partners) - 2):
        small_done(k)
    line_done("cq")
    for copy in s_keep:
        copy.wait()
    for copy in s_line:
        copy.wait_recv()
    hop["s"] = send(ref.s_z, ref.s_ry.at[0], pair_id)
    small_done(len(partners) - 2)
    pair_back("o")
    pair_back("co")
    line_done("ckv")
    fo_early.wait_recv()
    ff_last("fo")
    small_done(len(partners) - 1)
    pair_back("cq")
    hop["s"].wait_recv()
    s_ry, s_out = ref.s_ry, ref.s_out
    for k in range(len(bits) + 1):
        source = ref.s_z if k == 0 else ref.s_kw.at[k - 1]
        goal = s_out.at[core] if k == len(bits) else ref.s_kw.at[k]
        add_blocks(goal, [source, s_ry.at[k]])
        if k < len(bits):
            send(goal, s_ry.at[k + 1], dp_id(bits[k])).wait_recv()
    hop["s"] = send(s_out.at[core], s_out.at[core], core_id)
    pair_back("ckv")
    for name in ("ckv", "co", "cq", "o", "fi", "fo", "s"):
        hop[name].wait_recv()
    for copy in sent:
        copy.wait_send()
    for block in range(n_sp):

        @pl.when(block > spot_s)
        def _():
            chain_copy(0, block).wait_send()

        @pl.when(block < spot_s)
        def _():
            chain_copy(1, block).wait_send()


def back(**values):
    arrays = types.SimpleNamespace(**values)
    n_sp = lax.axis_size(SP)
    n_dp = lax.axis_size(DP)
    shape = jax.ShapeDtypeStruct
    rows, width = arrays.d_att.shape
    total = n_sp * rows
    cols = arrays.q.shape[1]
    g8 = 2 * n_sp
    more = max(n_dp.bit_length() - 3, 0)
    any_names = ["ckv", "cq", "co", "o", "fi", "fo", "fi_rx", "fo_rx1", "fo_far", "d_att", "text", "q", "kv", "lse", "w", "h1"]
    vmem_names = ["lin", "rho", "trig", "par", "x", "dx1", "time", "small_in", "gate2", "hidden_rows"]
    outs = {}
    for name in ("ckv", "cq", "co", "o"):
        quarter, lanes = getattr(arrays, name).shape[3:]
        outs[name + "_rc"] = shape((g8, 2, quarter, lanes), BF)
        outs[name + "_kc"] = shape((g8, 2, quarter, lanes), BF)
        if name == "o":
            outs[name + "_rz"] = shape((n_sp - 1, 2, 2, quarter, lanes), BF)
            outs[name + "_kl"] = shape((2, 2, quarter, lanes), BF)
            outs[name + "_rx"] = shape((2, quarter, lanes), BF)
            outs[name + "_ry"] = shape((quarter, lanes), BF)
        elif name == "ckv":
            outs[name + "_ry"] = shape((g8, quarter, lanes), BF)
            outs[name + "_ky"] = shape((g8, quarter, lanes), BF)
            outs[name + "_rx"] = shape((n_sp, quarter, lanes), BF)
        else:
            outs[name + "_rx"] = shape((n_sp, 2, quarter, lanes), BF)
            outs[name + "_ky"] = shape((n_sp, 2, quarter, lanes), BF)
            outs[name + "_ry"] = shape((n_sp, quarter, lanes), BF)
        outs[name + "_kx"] = shape((2 if name == "o" else n_sp, quarter, lanes), BF)
        if name != "o":
            outs[name + "_rz"] = shape((n_sp - 1, quarter, lanes), BF)
        outs[name + "_kz"] = shape((more + 1, quarter, lanes), BF)
        outs[name + "_rw"] = shape((more + 1, quarter, lanes), BF)
        outs[name + "_out"] = shape((2, 2, quarter, lanes), BF)
    for name in ("fi", "fo"):
        half = getattr(arrays, name).shape
        outs[name + "_kx"] = shape(half, BF)
        outs[name + "_ry"] = shape((more + 1,) + half, BF)
        outs[name + "_ky"] = shape((more + 1,) + half, BF)
        outs[name + "_out"] = shape((2,) + half, BF)
    outs.update(fo_rx=shape((3,) + arrays.fo.shape[1:], BF))
    text_rows = arrays.text.shape[2]
    outs.update(text_rx=shape((n_sp, text_rows, width), BF))
    outs.update(text_kx=shape((n_sp, text_rows, width), BF))
    outs.update(text_rz=shape((n_sp - 1, text_rows, width), BF))
    outs.update(text_out=shape((1, text_rows, width), F32))
    half_rows = width // g8 // 2
    outs.update(sw=shape((g8, 2, half_rows, 3 * cols), BF))
    outs.update(s_rc=shape((g8, half_rows, 3 * cols), BF))
    outs.update(s_kc=shape((g8, half_rows, 3 * cols), BF))
    outs.update(s_rx=shape((n_sp, half_rows, 3 * cols), BF))
    outs.update(s_kx=shape((n_sp, half_rows, 3 * cols), BF))
    outs.update(s_z=shape((half_rows, 3 * width), BF))
    outs.update(s_ry=shape((more + 1, half_rows, 3 * width), BF))
    outs.update(s_kw=shape((more + 1, half_rows, 3 * width), BF))
    outs.update(s_out=shape((2, half_rows, 3 * width), BF))
    in_any = len(outs)
    outs.update(tokens_out=shape((rows, width), F32))
    outs.update(small_out=shape(arrays.small_in.shape, F32))
    steps = 3 + more + n_sp.bit_length() - 1
    vmem = pltpu.VMEM
    scratch = dict(
        do=vmem((total, cols), BF),
        dq=vmem((total, cols), F32),
        dkv=vmem((2, 2 * total, cols), F32),
        kv_recv=vmem((2, total, cols), BF),
        sums=vmem((n_sp + 1, 8, total), F32),
        proj=vmem((total, 3 * cols), BF),
        dh1=vmem((n_sp, rows, width), BF),
        dh1_own=vmem((rows, width), F32),
        dh1_recv=vmem((n_sp + 1, rows, width), BF),
        chain_send=pltpu.SemaphoreType.DMA((2 * n_sp,)),
        chain_recv=pltpu.SemaphoreType.DMA((n_sp + 1,)),
        small=vmem((steps + 1,) + arrays.small_in.shape, F32),
        small_recv=vmem((steps,) + arrays.small_in.shape, F32),
        send=pltpu.SemaphoreType.DMA((128,)),
        recv=pltpu.SemaphoreType.DMA((128,)),
        local=pltpu.SemaphoreType.DMA((5,)),
    )
    any_place = pl.BlockSpec(memory_space=pl.ANY)
    in_vmem = pl.BlockSpec(memory_space=pltpu.VMEM)
    names = any_names + vmem_names + list(outs) + list(scratch)
    results = pl.pallas_call(
        functools.partial(back_kernel, n_sp, n_dp, names),
        out_shape=tuple(outs.values()),
        in_specs=[any_place] * len(any_names) + [in_vmem] * len(vmem_names),
        out_specs=(any_place,) * in_any + (in_vmem,) * (len(outs) - in_any),
        scratch_shapes=list(scratch.values()),
        compiler_params=pltpu.CompilerParams(
            collective_id=2, has_side_effects=True, vmem_limit_bytes=60 * 2**20
        ),
    )(*[getattr(arrays, name) for name in any_names + vmem_names])
    return types.SimpleNamespace(**dict(zip(outs, results)))


def swap_blk(value):
    return lax.ppermute(value, BLK, [(0, 1), (1, 0)])


def local(
    clip_tokens,
    text_tokens,
    text_lengths,
    positions,
    time_embed,
    modulation,
    gains,
    biases,
    self_qkv,
    self_out,
    cross_qkv,
    cross_out,
    ffn_in,
    ffn_out,
    ffn_bias,
    cotangent,
):
    n_sp = lax.axis_size(SP)
    n_dp = lax.axis_size(DP)
    spot_dp = lax.axis_index(DP)
    spot_b = lax.axis_index(BLK)
    spot_s = lax.axis_index(SP)
    core = spot_dp % 2
    pair = (spot_dp // 2) % 2
    x_own = clip_tokens[0]
    tok_rows, width = x_own.shape
    heads_here = H // n_sp
    cols_here = heads_here * HD
    shard_rows = self_qkv.shape[0]
    scale = HD ** (-0.5)

    small_rows = jnp.concatenate([modulation, gains, biases], 0)
    lanes_here = small_rows.shape[1]
    small_own = jnp.concatenate(
        [
            jnp.pad(
                positions[0].astype(BF), ((0, 13), (0, SMALL_LANES - positions.shape[2]))
            ),
            jnp.pad(small_rows, ((0, 0), (0, SMALL_LANES - lanes_here))),
            jnp.pad(
                ffn_bias, (0, (PARAM_ROWS - 21) * SMALL_LANES - ffn_bias.shape[0])
            ).reshape(-1, SMALL_LANES),
        ],
        0,
    )
    (
        params,
        h1_all,
        qkv_mine,
        lin_parts,
        rho,
        trig,
        q_flat,
        kv_flat,
        lse_wide,
        att_all,
        att_tok,
        rest_all,
        in_other,
        out_other,
        text_every,
        cot_every,
        small_every,
    ) = front(
        x_own,
        small_own,
        self_qkv,
        jnp.concatenate([self_out, cross_out, cross_qkv], 1),
        ffn_in,
        ffn_out,
        text_tokens[0],
        cotangent[0],
        time_embed[0],
    )
    mods = time_embed[0] + params[:6]
    gain_all = params[6:11]
    bias_all = params[11:21]
    ff_here = ffn_in.shape[0]
    bias_rows = small_every.reshape(2, n_sp, SMALL_ROWS, SMALL_LANES)
    bias_rows = lax.dynamic_index_in_dim(bias_rows, spot_s, 1, keepdims=False)[:, 37:]
    bias_rows = bias_rows.reshape(2, -1)[:, :ff_here].astype(F32)
    bias_ff = jnp.where(
        spot_b == 0,
        jnp.concatenate([bias_rows[0], bias_rows[1]]),
        jnp.concatenate([bias_rows[1], bias_rows[0]]),
    )

    own = own_tokens(
        text_lengths, rest_all, x_own, att_tok, text_every, time_embed[0], params
    )
    ffn_rows = own.h2
    x_two = own.two

    fed = feed(**dict(
            in_own=ffn_in,
            in_other=in_other,
            out_own=ffn_out,
            out_other=out_other,
            h2=ffn_rows,
            cot=cot_every,
            bias=bias_ff[None],
            time=time_embed[0],
            par=params,
        )
    )
    d_rows = fed.d_rows
    du_sums = fed.du_sums[0]
    z_lin = (
        lax.psum_scatter(fed.z_out, SP, scatter_dimension=0, tiled=False).astype(F32)
        + bias_all[9]
    )
    grad_y = cotangent[0].astype(F32)
    result = x_two + mods[5] * z_lin
    block_out = result.astype(BF)[None]
    d_gate2 = jnp.sum(grad_y * z_lin, 0)
    last = own_back(**dict(
            len=text_lengths,
            rest=rest_all,
            x_two=x_two,
            x_one=own.one,
            d_rows=d_rows,
            cot=cotangent[0],
            time=time_embed[0],
            par=params,
            a=own.a,
            cin=own.cin,
            ql=own.ql,
            kl=own.kl,
            q=own.q,
            kv=own.kv,
            lse=own.lse,
            oc=own.oc,
            att=att_tok,
            text_in=text_every,
        )
    )

    ff_total = ff_here * 2 * n_sp
    ff_row = jnp.zeros((-(-ff_total // width) * width,), F32)
    own_at = (spot_b * n_sp + spot_s) * ff_here
    far_at = ((1 - spot_b) * n_sp + spot_s) * ff_here
    ff_row = lax.dynamic_update_slice_in_dim(ff_row, du_sums[:ff_here], own_at, 0)
    ff_row = lax.dynamic_update_slice_in_dim(ff_row, du_sums[ff_here:], far_at, 0)
    def quarters(grad):
        return grad.reshape(2 * n_sp, 2, 2, shard_rows // 4, grad.shape[1])

    def chunks(grad):
        return grad.reshape(5, ff_here // 10, width)

    ended = back(**dict(
            ckv=quarters(last.ckv),
            cq=quarters(last.cq),
            co=quarters(last.co),
            o=quarters(last.o),
            fi=chunks(fed.fi_own),
            fo=chunks(fed.fo_own),
            fi_rx=chunks(swap_blk(fed.fi_far)),
            fo_rx1=swap_blk(fed.fo_far[: ff_here // 5]).reshape(2, -1, width),
            fo_far=chunks(fed.fo_far),
            d_att=last.d_att,
            text=last.text_part.reshape(2, n_sp, -1, width),
            q=q_flat,
            kv=kv_flat,
            lse=lse_wide,
            w=qkv_mine,
            h1=h1_all,
            lin=lin_parts,
            rho=rho,
            trig=trig,
            par=params,
            x=x_own,
            dx1=last.dx,
            time=time_embed[0],
            small_in=last.sums,
            gate2=d_gate2[None],
            hidden_rows=ff_row.reshape(-1, width),
        )
    )
    small = ended.small_out
    spot = spot_b * n_sp + spot_s
    small_own = lax.dynamic_slice_in_dim(small[:21], spot * lanes_here, lanes_here, 1)
    part_bias = lax.dynamic_slice_in_dim(small[21:].reshape(-1), own_at, ff_here, 0)

    def whole(name, rows):
        return getattr(ended, name + "_out").reshape(rows, -1).astype(F32)

    return (
        block_out,
        ended.tokens_out[None],
        ended.text_out,
        small_own[:6],
        small_own[6:11],
        small_own[11:21],
        whole("s", shard_rows),
        whole("o", shard_rows),
        jnp.concatenate(
            [
                whole("cq", shard_rows),
                whole("ckv", shard_rows),
            ],
            1,
        ),
        whole("co", shard_rows),
        whole("fi", ff_here),
        whole("fo", ff_here),
        part_bias,
    )


def solution(mesh):
    return jax.shard_map(
        local,
        mesh=mesh,
        in_specs=(
            P(DP, (BLK, SP), None),
            P(DP, (BLK, SP), None),
            P(DP),
            P(DP, None, (BLK, SP)),
            P(DP, None, None),
            P(None, (BLK, SP)),
            P(None, (BLK, SP)),
            P(None, (BLK, SP)),
            P((BLK, SP), None),
            P((BLK, SP), None),
            P((BLK, SP), None),
            P((BLK, SP), None),
            P((BLK, SP), None),
            P((BLK, SP), None),
            P((BLK, SP)),
            P(DP, (BLK, SP), None),
        ),
        out_specs=(
            P(DP, (BLK, SP), None),
            P(DP, (BLK, SP), None),
            P(DP, (BLK, SP), None),
            P(None, (BLK, SP)),
            P(None, (BLK, SP)),
            P(None, (BLK, SP)),
            P((BLK, SP), None),
            P((BLK, SP), None),
            P((BLK, SP), None),
            P((BLK, SP), None),
            P((BLK, SP), None),
            P((BLK, SP), None),
            P((BLK, SP)),
        ),
        check_vma=False,
    )
```

```python
import functools
import types

import jax
import jax.numpy as jnp
import numpy as np
from jax import lax
from jax.experimental import pallas as pl
from jax.experimental.pallas import tpu as pltpu
from jax.sharding import PartitionSpec as P

H = 12
HD = 128


DP, BLK, SP = "dp", "blk", "sp"
EPS = 1e-06
NEG = -1e30


def rope_tables(head_dim):
    pair_count = head_dim // 2
    side_count = head_dim // 6
    first_count = pair_count - 2 * side_count
    tables = np.zeros((3, pair_count))
    for column in range(pair_count):
        if column < first_count:
            tables[0, column] = 10000.0 ** (-column / first_count)
        elif column < first_count + side_count:
            tables[1, column] = 10000.0 ** (-(column - first_count) / side_count)
        else:
            tables[2, column] = 10000.0 ** (-(column - first_count - side_count) / side_count)
    return tables


BF = jnp.bfloat16
F32 = jnp.float32


MESH = pl.DeviceIdType.MESH
PARAM_ROWS = 32
SMALL_ROWS = 16 + PARAM_ROWS
SMALL_LANES = 256


def remote_copy(src, dst, send, recv, target):
    return pltpu.make_async_remote_copy(
        src_ref=src,
        dst_ref=dst,
        send_sem=send,
        recv_sem=recv,
        device_id=target,
        device_id_type=MESH,
    )


def meet(targets):
    barrier = pltpu.get_barrier_semaphore()
    for target in targets:
        pl.semaphore_signal(barrier, inc=1, device_id=target, device_id_type=MESH)
    pl.semaphore_wait(barrier, len(targets))


def rows_at(start, size):
    return pl.ds(pl.multiple_of(start, 16), size)


def lanes_at(start, size):
    return pl.ds(pl.multiple_of(start, 128), size)


def mm(a, b):
    return lax.dot_general(a, b, (((1,), (0,)), ((), ())), preferred_element_type=F32)


def mm_t(a, b):
    return lax.dot_general(a, b, (((1,), (1,)), ((), ())), preferred_element_type=F32)


def mm_first(a, b):
    return lax.dot_general(a, b, (((0,), (0,)), ((), ())), preferred_element_type=F32)


def exact_first(a, b):
    return lax.dot_general(
        a,
        b,
        (((0,), (0,)), ((), ())),
        precision=lax.Precision.HIGHEST,
        preferred_element_type=F32,
    )


def exact_sums(values):
    ones = jnp.ones((8, values.shape[1]), F32)
    return lax.dot_general(
        ones,
        values,
        (((1,), (1,)), ((), ())),
        precision=lax.Precision.HIGHEST,
        preferred_element_type=F32,
    )


def row_pick(which):
    return (lax.broadcasted_iota(jnp.int32, (8, 128), 0) == which).astype(F32)


def turn_sign():
    lane = lax.broadcasted_iota(jnp.int32, (1, HD), 1)
    return jnp.where(lane < HD // 2, -1.0, 1.0).astype(F32)


def turned(value, cosine, sine):
    return value * cosine + pltpu.roll(value, HD // 2, 1) * (sine * turn_sign())


def front_kernel(
    n_sp,
    x_ref,
    small_ref,
    qkv_ref,
    rest_ref,
    in_ref,
    out_ref,
    text_ref,
    cot_ref,
    time_ref,
    table_ref,
    par_ref,
    h1_out,
    w_out_ref,
    lin_out,
    rho_out,
    trig_out,
    q_out,
    kv_out,
    lse_out,
    att_out,
    tok_out,
    rest_out,
    in_out,
    out_out,
    text_out,
    cot_out,
    small_out,
    xall_ref,
    sall_ref,
    w_ref,
    lin_ref,
    sums_ref,
    rho_ref,
    trig_ref,
    q_ref,
    kv_ref,
    acc_ref,
    stat_ref,
    att_ref,
    h1_ref,
    *sems,
):
    lo, zs, zr, ss, sr, ws, wr, xs, xr, cs, cr, ps, pr, vs, vr, qs, qr, ts, tr, out = sems[:20]
    (ls, lr, lxs, lxr, lys, lyr, lcs, lcr, fs, fr, es, er, exs, exr, os, osr) = sems[20:]
    spot_d = lax.axis_index(DP)
    spot_b = lax.axis_index(BLK)
    spot_s = lax.axis_index(SP)
    core = lax.rem(spot_d, 2)
    pair = lax.rem(spot_d // 2, 2)
    core_id = {DP: spot_d + 1 - 2 * core}
    pair_id = {DP: spot_d + 2 - 4 * pair}
    blk_id = {BLK: 1 - spot_b}
    line = [{SP: lax.rem(spot_s + step, n_sp)} for step in range(1, n_sp)]
    rows = x_ref.shape[0]
    shard = qkv_ref.shape[0]
    half = shard // 2
    cols = w_ref.shape[1] // 3
    wide = qkv_ref.shape[1] // 3
    heads_here = cols // HD
    total_rows = n_sp * rows
    sums_ref[spot_s] = jnp.zeros((8, total_rows), F32)
    meet(line + [core_id, blk_id, pair_id])

    def w_rows(blk, spot, part):
        return rows_at((blk * n_sp + spot) * shard + part * half, half)

    here = spot_b * n_sp + spot_s
    keep = [
        pltpu.make_async_copy(
            qkv_ref.at[:, lanes_at(j * wide + spot_s * cols, cols)],
            w_ref.at[rows_at(here * shard, shard), pl.ds(j * cols, cols)],
            lo.at[j],
        )
        for j in range(3)
    ]
    keep.append(pltpu.make_async_copy(x_ref, xall_ref.at[rows_at(spot_s * rows, rows)], lo.at[3]))
    keep.append(pltpu.make_async_copy(small_ref, sall_ref.at[here], lo.at[4]))
    for copy in keep:
        copy.start()
    small_away = [
        remote_copy(small_ref, sall_ref.at[here], ss.at[k], sr.at[k], line[k])
        for k in range(n_sp - 1)
    ]
    for copy in small_away:
        copy.start()
    w_away = []
    for k in range(n_sp - 1):
        spot = lax.rem(spot_s + k + 1, n_sp)
        for j in range(3):
            copy = remote_copy(
                qkv_ref.at[rows_at(core * half, half), lanes_at(j * wide + spot * cols, cols)],
                w_ref.at[w_rows(spot_b, spot_s, core), pl.ds(j * cols, cols)],
                ws.at[3 * k + j],
                wr.at[3 * k + j],
                line[k],
            )
            copy.start()
            w_away.append(copy)

    def sends(way, k):
        if way == 0:
            return jnp.logical_and(spot_s < n_sp - 1, spot_s >= k)
        return jnp.logical_and(spot_s > 0, spot_s + k < n_sp)

    def gets(way, k):
        return spot_s > k if way == 0 else spot_s + k + 1 < n_sp

    def line_gather(first, place, pieces, send, recv, then=None):
        def copy(way, k, part):
            block = spot_s - k if way == 0 else spot_s + k
            at = place(block, part)
            src = first(part) if k == 0 else at
            target = {SP: spot_s + 1 if way == 0 else spot_s - 1}
            index = (way * (n_sp - 1) + k) * pieces + part
            return remote_copy(src, at, send.at[index], recv.at[index], target)

        def step(k):
            for part in range(pieces):
                for way in range(2):
                    if k > 0:

                        @pl.when(gets(way, k - 1))
                        def _():
                            copy(way, k - 1, part).wait_recv()

                    if k < n_sp - 1:

                        @pl.when(sends(way, k))
                        def _():
                            copy(way, k, part).start()

                    if k > 0 and then is not None:

                        @pl.when(gets(way, k - 1))
                        def _():
                            then(spot_s - k if way == 0 else spot_s + k)

        def sent():
            for k in range(n_sp - 1):
                for part in range(pieces):
                    for way in range(2):

                        @pl.when(sends(way, k))
                        def _():
                            copy(way, k, part).wait_send()

        return step, sent

    pieces = 2
    piece = rows // pieces
    token_step, token_sent = line_gather(
        lambda part: x_ref.at[pl.ds(part * piece, piece)],
        lambda block, part: xall_ref.at[rows_at(block * rows + part * piece, piece)],
        pieces,
        zs,
        zr,
    )

    fourth = shard // 4
    quarter = core * 2 + pair

    def rest_rows(blk, spot, which):
        return rest_out.at[rows_at((blk * n_sp + spot) * shard + which * fourth, fourth)]

    def rest_copy(sems, blk, spot, which, slot, target):
        at = rest_rows(blk, spot, which)
        index = (slot * 2 + blk) * n_sp + spot
        return remote_copy(at, at, sems[0].at[index], sems[1].at[index], target)

    def rest_core(blk, spot, slot):
        which = core * 2 + (pair if slot == 0 else 1 - pair)
        return rest_copy((lcs, lcr), blk, spot, which, slot, core_id)

    def rest_pair(blk, spot):
        return rest_copy((lys, lyr), blk, spot, quarter, 0, pair_id)

    def rest_blk(spot):
        at = rest_rows(spot_b, spot, quarter)
        return remote_copy(at, at, lxs.at[spot], lxr.at[spot], blk_id)

    def rest_arrived(spot):
        rest_blk(spot).start()
        rest_pair(spot_b, spot).start()
        rest_core(spot_b, spot, 0).start()

    rest_step, rest_sent = line_gather(
        lambda part: rest_ref.at[rows_at(quarter * fourth, fourth)],
        lambda block, part: rest_rows(spot_b, block, quarter),
        1,
        ls,
        lr,
        rest_arrived,
    )
    rest_own = remote_copy(
        rest_ref.at[rows_at(quarter * fourth, fourth)],
        rest_rows(spot_b, spot_s, quarter),
        lxs.at[spot_s],
        lxr.at[spot_s],
        blk_id,
    )
    rest_keep = pltpu.make_async_copy(
        rest_ref, rest_out.at[rows_at((spot_b * n_sp + spot_s) * shard, shard)], out.at[9]
    )

    def at_distance(k, call):
        if k == 0:
            call(spot_s)
        else:
            for way in range(2):

                @pl.when(gets(way, k - 1))
                def _():
                    call(spot_s - k if way == 0 else spot_s + k)

    def rest_from_blk(k):
        def one(spot):
            rest_blk(spot).wait_recv()
            rest_pair(1 - spot_b, spot).start()
            rest_core(1 - spot_b, spot, 0).start()

        at_distance(k, one)

    def rest_from_pair(k):
        def one(spot):
            if k > 0:
                rest_pair(spot_b, spot).wait_recv()
                rest_core(spot_b, spot, 1).start()
            rest_pair(1 - spot_b, spot).wait_recv()
            rest_core(1 - spot_b, spot, 1).start()

        at_distance(k, one)

    def rest_last(k):
        def one(spot):
            for slot in range(2):
                if k > 0:
                    rest_core(spot_b, spot, slot).wait_recv()
                rest_core(1 - spot_b, spot, slot).wait_recv()

        at_distance(k, one)

    def rest_done(k):
        def one(spot):
            rest_blk(spot).wait_send()
            for slot in range(2):
                if k > 0:
                    rest_core(spot_b, spot, slot).wait_send()
                rest_core(1 - spot_b, spot, slot).wait_send()
            if k > 0:
                rest_pair(spot_b, spot).wait_send()
            rest_pair(1 - spot_b, spot).wait_send()

        at_distance(k, one)

    hidden = in_ref.shape[0]
    hidden_half = hidden // 2

    def hidden_place(which, half):
        goal = in_out if which == 0 else out_out
        return goal.at[pl.ds(half * hidden_half, hidden_half)]

    def hidden_each(call):
        for which in range(2):
            for half in range(2):

                @pl.when(jnp.logical_and(core == half, pair == which))
                def _():
                    call(which, half)

    def hidden_blk(which, half):
        src = in_ref if which == 0 else out_ref
        return remote_copy(
            src.at[pl.ds(half * hidden_half, hidden_half)],
            hidden_place(which, half),
            fs.at[0],
            fr.at[0],
            blk_id,
        )

    def hidden_pair(which, half):
        at = hidden_place(which, half)
        return remote_copy(at, at, fs.at[1], fr.at[1], pair_id)

    def hidden_core(slot, which, half):
        at = hidden_place(which, half)
        return remote_copy(at, at, fs.at[2 + slot], fr.at[2 + slot], core_id)

    def hidden_next(which, half):
        hidden_blk(which, half).wait_recv()
        hidden_pair(which, half).start()
        hidden_core(0, which, half).start()

    def hidden_last(which, half):
        hidden_pair(which, half).wait_recv()
        hidden_core(1, 1 - which, half).start()

    def hidden_end(which, half):
        for slot in range(2):
            hidden_core(slot, which, half).wait_recv()
            hidden_core(slot, which, half).wait_send()
        hidden_pair(which, half).wait_send()
        hidden_blk(which, half).wait_send()

    text_rows = text_ref.shape[0]

    def text_at(blk, spot):
        return text_out.at[rows_at((blk * n_sp + spot) * text_rows, text_rows)]

    def text_blk(spot, own):
        at = text_at(spot_b, spot)
        src = text_ref if own else at
        return remote_copy(src, at, exs.at[spot], exr.at[spot], blk_id)

    text_step, text_sent = line_gather(
        lambda part: text_ref,
        lambda block, part: text_at(spot_b, block),
        1,
        es,
        er,
        lambda spot: text_blk(spot, False).start(),
    )
    text_keep = pltpu.make_async_copy(text_ref, text_at(spot_b, spot_s), out.at[10])
    cot_step, cot_sent = line_gather(
        lambda part: cot_ref,
        lambda block, part: cot_out.at[rows_at(block * rows, rows)],
        1,
        os,
        osr,
    )
    cot_keep = pltpu.make_async_copy(
        cot_ref, cot_out.at[rows_at(spot_s * rows, rows)], out.at[11]
    )

    token_step(0)
    rest_own.start()
    rest_step(0)
    for copy in (rest_keep, text_keep, cot_keep):
        copy.start()
    for copy in small_away:
        copy.wait_recv()
    keep[4].wait()
    small_pass = []
    for spot in range(n_sp):
        at = sall_ref.at[spot_b * n_sp + spot]
        copy = remote_copy(at, at, ps.at[spot], pr.at[spot], blk_id)
        copy.start()
        small_pass.append(copy)
    for j in range(3):
        keep[j].wait()
    blk_away = []
    core_away = []

    def pass_core(blk, spot, which):
        at = w_ref.at[w_rows(blk, spot, core)]
        copy = remote_copy(at, at, cs.at[which], cr.at[which], core_id)
        copy.start()
        core_away.append(copy)

    def pass_blk(step):
        at = w_ref.at[w_rows(spot_b, lax.rem(spot_s + n_sp - step, n_sp), core)]
        copy = remote_copy(at, at, xs.at[step], xr.at[step], blk_id)
        copy.start()
        blk_away.append(copy)

    pass_blk(0)
    for k in range(n_sp - 1):
        for j in range(3):
            w_away[3 * k + j].wait_recv()
        pass_blk(k + 1)
        pass_core(spot_b, lax.rem(spot_s + n_sp - k - 1, n_sp), k)

    for copy in small_pass:
        copy.wait_recv()
    lanes = wide // (2 * n_sp)
    at_row = lax.broadcasted_iota(jnp.int32, (2 * SMALL_LANES, 2 * lanes), 0)
    at_col = lax.broadcasted_iota(jnp.int32, (2 * SMALL_LANES, 2 * lanes), 1)
    place = jnp.where(at_row < SMALL_LANES, at_row, at_row - SMALL_LANES)
    goal = jnp.where(at_row < SMALL_LANES, place, place + lanes)
    chosen = jnp.logical_and(place < lanes, goal == at_col).astype(F32).astype(BF)
    for two in range(n_sp):
        both = jnp.concatenate(
            [sall_ref[2 * two, 16:, :], sall_ref[2 * two + 1, 16:, :]], axis=1
        )
        par_ref[:, 2 * lanes * two : 2 * lanes * (two + 1)] = mm(both, chosen)

    token_step(1)
    for step in range(n_sp):
        blk_away[step].wait_recv()
        pass_core(1 - spot_b, lax.rem(spot_s + n_sp - step, n_sp), n_sp - 1 + step)
    for copy in core_away:
        copy.wait_recv()
    w_keep = pltpu.make_async_copy(w_ref, w_out_ref, lo.at[5])
    w_keep.start()
    keep[3].wait()
    hidden_each(lambda which, half: hidden_blk(which, half).start())
    rest_from_blk(0)

    shift = time_ref[0:1, :] + par_ref[0:1, :]
    scale = 1.0 + (time_ref[1:2, :] + par_ref[1:2, :])
    own = lanes_at(spot_s * cols, cols)

    def project(block):
        at = rows_at(block * rows, rows)
        values = xall_ref[at, :].astype(F32)
        centre = values - jnp.mean(values, axis=-1, keepdims=True)
        spread = jnp.mean(centre * centre, axis=-1, keepdims=True)
        h1_ref[at, :] = (centre * lax.rsqrt(spread + EPS) * scale + shift).astype(BF)
        for j in range(3):
            lin = mm(h1_ref[at, :], w_ref[:, j * cols : (j + 1) * cols])
            lin = lin + par_ref[11 + j : 12 + j, own]
            if j < 2:
                lin_ref[j, at, :] = lin
                sums = exact_sums(lin * lin)
                sums_ref[spot_s, j : j + 1, lanes_at(block * rows, rows)] = sums[0:1]
            else:
                kv_ref[1, at, :] = lin.astype(BF)
        value_copy(block).start()
        angle = exact_first(
            sall_ref[spot_b * n_sp + block, 0:16, :].astype(F32), table_ref[...]
        )
        trig_ref[0, at, :] = jnp.cos(angle)
        trig_ref[1, at, :] = jnp.sin(angle)

    def kv_copy(which, block):
        return remote_copy(
            kv_ref.at[which, rows_at(block * rows, rows)],
            kv_ref.at[which, rows_at(total_rows + block * rows, rows)],
            vs.at[which * n_sp + block],
            vr.at[which * n_sp + block],
            blk_id,
        )

    def value_copy(block):
        return kv_copy(1, block)

    def arrived(k):
        first = (spot_s >= k).astype(jnp.int32)
        last = (spot_s + k < n_sp).astype(jnp.int32)

        def one(i, carry):
            ahead = jnp.logical_and(first == 1, i == 0)
            project(jnp.where(ahead, spot_s - k, spot_s + k))
            return carry

        lax.fori_loop(0, first + last, one, 0)

    project(spot_s)
    rest_step(1)
    arrived(1)
    token_step(2)
    rest_from_blk(1)
    arrived(2)
    rest_step(2)
    token_step(3)
    arrived(3)

    sums_away = []
    for k in range(n_sp - 1):
        copy = remote_copy(
            sums_ref.at[spot_s], sums_ref.at[spot_s], qs.at[k], qr.at[k], line[k]
        )
        copy.start()
        sums_away.append(copy)
    for copy in sums_away:
        copy.wait_recv()
    squares = sums_ref[0]
    for k in range(1, n_sp):
        squares = squares + sums_ref[k]
    rho_rows = lax.rsqrt(squares / wide + EPS)
    sums_ref[n_sp] = rho_rows

    def turn_block(which, block):
        at = rows_at(block * rows, rows)
        rho = exact_first(sums_ref[n_sp, :, lanes_at(block * rows, rows)], row_pick(which))
        rho_ref[which, at, :] = rho
        cosine = trig_ref[0, at, :]
        sine = trig_ref[1, at, :]
        for h in range(heads_here):
            gain = par_ref[6 + which : 7 + which, lanes_at(spot_s * cols + h * HD, HD)]
            value = lin_ref[which, at, h * HD : (h + 1) * HD] * rho * gain
            value = turned(value, cosine, sine).astype(BF)
            if which == 0:
                q_ref[at, h * HD : (h + 1) * HD] = value
            else:
                kv_ref[0, at, h * HD : (h + 1) * HD] = value

    def turn_key(block, carry):
        turn_block(1, block)
        kv_copy(0, block).start()
        return carry

    def turn_query(block, carry):
        turn_block(0, block)
        return carry

    lax.fori_loop(0, n_sp, turn_key, 0)
    lax.fori_loop(0, n_sp, turn_query, 0)
    text_blk(spot_s, True).start()
    text_step(0)
    rest_from_pair(0)
    rest_step(3)
    rest_from_blk(2)
    cot_step(0)
    saves = [
        pltpu.make_async_copy(sall_ref, small_out, out.at[12]),
        pltpu.make_async_copy(h1_ref, h1_out, out.at[0]),
        pltpu.make_async_copy(lin_ref, lin_out, out.at[1]),
        pltpu.make_async_copy(rho_ref, rho_out, out.at[2]),
        pltpu.make_async_copy(trig_ref, trig_out, out.at[3]),
        pltpu.make_async_copy(q_ref, q_out, out.at[4]),
    ]
    for copy in saves:
        copy.start()
    score_scale = HD ** (-0.5)

    def attend(block, h, part):
        at = rows_at(block * rows, rows)
        head = pl.ds(h * HD, HD)
        keys = pl.ds(part * total_rows, total_rows)
        scores = mm_t(q_ref[at, head], kv_ref[0, keys, head]) * score_scale
        top = jnp.max(scores, -1, keepdims=True)
        if part == 1:
            before = stat_ref[0, h, at, 0:1]
            top = jnp.maximum(top, before)
        raised = jnp.exp(scores - top)
        total = jnp.sum(raised, -1, keepdims=True)
        result = mm(raised.astype(BF), kv_ref[1, keys, head])
        if part == 0:
            stat_ref[0, h, at, :] = jnp.broadcast_to(top, (rows, 128))
            stat_ref[1, h, at, :] = jnp.broadcast_to(total, (rows, 128))
            acc_ref[h, at, :] = result
        else:
            fade = jnp.exp(before - top)
            total = total + fade * stat_ref[1, h, at, 0:1]
            result = result + fade * acc_ref[h, at, :]
            att_ref[at, head] = (result / total).astype(BF)
            stat_ref[0, h, at, :] = jnp.broadcast_to(top + jnp.log(total), (rows, 128))

    def first_pass(block, carry):
        for h in range(heads_here):
            attend(block, h, 0)
        return carry

    lax.fori_loop(0, n_sp, first_pass, 0)
    hidden_each(hidden_next)

    def key_wait(block, carry):
        kv_copy(0, block).wait_recv()
        kv_copy(1, block).wait_recv()
        return carry

    lax.fori_loop(0, n_sp, key_wait, 0)
    kv_save = pltpu.make_async_copy(kv_ref, kv_out, out.at[5])
    kv_save.start()
    rest_from_blk(3)
    rest_from_pair(1)

    def att_copy(step):
        block = lax.rem(spot_s + step, n_sp)
        return remote_copy(
            att_ref.at[rows_at(block * rows, rows)],
            tok_out.at[:, lanes_at(spot_s * cols, cols)],
            ts.at[step - 1],
            tr.at[step - 1],
            {SP: block},
        )

    for step in list(range(1, n_sp)) + [0]:
        block = lax.rem(spot_s + step, n_sp)

        def one_head(block=block):
            for h in range(heads_here):
                attend(block, h, 1)

        one_head()
        if step > 0:
            att_copy(step).start()
        if step == 1:
            text_step(1)
            cot_step(1)
        if step == 2:
            rest_from_pair(2)
    own_att = pltpu.make_async_copy(
        att_ref.at[rows_at(spot_s * rows, rows)],
        tok_out.at[:, lanes_at(spot_s * cols, cols)],
        out.at[6],
    )
    own_att.start()
    saves.append(own_att)
    last = [
        pltpu.make_async_copy(stat_ref.at[0], lse_out, out.at[7]),
        pltpu.make_async_copy(att_ref, att_out, out.at[8]),
    ]
    for copy in last:
        copy.start()
    text_step(2)
    cot_step(2)
    hidden_each(hidden_last)
    text_step(3)
    rest_from_pair(3)
    cot_step(3)
    for k in range(n_sp):
        rest_last(k)
        at_distance(k, lambda spot: text_blk(spot, False).wait_recv())
    for step in range(1, n_sp):
        att_copy(step).wait_recv()
    for copy in (rest_keep, text_keep, cot_keep):
        copy.wait()
    for k in range(n_sp):
        rest_done(k)
        at_distance(k, lambda spot: text_blk(spot, False).wait_send())
    hidden_each(hidden_end)
    rest_sent()
    text_sent()
    cot_sent()
    token_sent()
    for copy in saves + last + [kv_save, w_keep]:
        copy.wait()
    for copy in small_away + w_away + blk_away + core_away + small_pass + sums_away:
        copy.wait_send()

    def kv_sent(block, carry):
        kv_copy(0, block).wait_send()
        kv_copy(1, block).wait_send()
        return carry

    lax.fori_loop(0, n_sp, kv_sent, 0)
    for step in range(1, n_sp):
        att_copy(step).wait_send()


def front(x_own, small_own, qkv, rest, shard_in, shard_out, text, cot, time_rows):
    n_sp = lax.axis_size(SP)
    groups = 2 * n_sp
    rows, width = x_own.shape
    total = n_sp * rows
    cols = qkv.shape[1] // 3 // n_sp
    heads_here = cols // HD
    table = np.zeros((16, HD), np.float32)
    pairs = rope_tables(HD)
    table[:3, : HD // 2] = pairs
    table[:3, HD // 2 :] = pairs
    any_place = pl.BlockSpec(memory_space=pl.ANY)
    in_vmem = pl.BlockSpec(memory_space=pltpu.VMEM)
    dma = pltpu.SemaphoreType.DMA
    line = n_sp - 1
    counts = [6, 4 * line, 4 * line, line, line, 3 * line, 3 * line, n_sp, n_sp]
    counts += [2 * n_sp - 1, 2 * n_sp - 1, n_sp, n_sp, 2 * n_sp, 2 * n_sp, line, line]
    counts += [line, line, 13]
    counts += [2 * line, 2 * line, n_sp, n_sp, groups, groups, 2 * groups, 2 * groups, 4, 4]
    counts += [2 * line, 2 * line, n_sp, n_sp, 2 * line, 2 * line]
    shape = jax.ShapeDtypeStruct
    outs = (
        shape((PARAM_ROWS, width), F32),
        shape((total, width), BF),
        shape((width, 3 * cols), BF),
        shape((2, total, cols), F32),
        shape((2, total, HD), F32),
        shape((2, total, HD), F32),
        shape((total, cols), BF),
        shape((2, 2 * total, cols), BF),
        shape((heads_here, total, HD), F32),
        shape((total, cols), BF),
        shape((rows, width), BF),
        shape((groups * rest.shape[0], rest.shape[1]), BF),
        shape(shard_in.shape, BF),
        shape(shard_out.shape, BF),
        shape((groups * text.shape[0], width), BF),
        shape((total, width), BF),
        shape((groups,) + small_own.shape, BF),
    )
    vmem = pltpu.VMEM
    return pl.pallas_call(
        functools.partial(front_kernel, n_sp),
        out_shape=outs,
        in_specs=[any_place] * 8 + [in_vmem] * 2,
        out_specs=(in_vmem,) + (any_place,) * (len(outs) - 1),
        scratch_shapes=[
            vmem((total, width), BF),
            vmem((groups, SMALL_ROWS, SMALL_LANES), BF),
            vmem((width, 3 * cols), BF),
            vmem((2, total, cols), F32),
            vmem((n_sp + 1, 8, total), F32),
            vmem((2, total, HD), F32),
            vmem((2, total, HD), F32),
            vmem((total, cols), BF),
            vmem((2, 2 * total, cols), BF),
            vmem((heads_here, total, HD), F32),
            vmem((2, heads_here, total, HD), F32),
            vmem((total, cols), BF),
            vmem((total, width), BF),
        ]
        + [dma((count,)) for count in counts],
        compiler_params=pltpu.CompilerParams(
            collective_id=1, has_side_effects=True, vmem_limit_bytes=56 * 2**20
        ),
    )(x_own, small_own, qkv, rest, shard_in, shard_out, text, cot, time_rows, jnp.asarray(table))


def normal(values):
    centre = values - jnp.mean(values, axis=-1, keepdims=True)
    spread = lax.rsqrt(jnp.mean(centre * centre, axis=-1, keepdims=True) + EPS)
    return centre * spread, spread


def normal_back(normed, spread, grad):
    lean = jnp.mean(grad, axis=-1, keepdims=True)
    tilt = jnp.mean(grad * normed, axis=-1, keepdims=True)
    return spread * (grad - lean - normed * tilt)


def column_total(values):
    return jnp.sum(values.astype(F32), 0, keepdims=True)


def wide_dot(dst, left, right, call=mm, tile=512, add=None):
    across = dst.shape[-1]
    for start in range(0, across, tile):
        at = pl.ds(start, min(tile, across - start))
        value = call(left, right[:, at])
        if add is not None:
            value = value + add[:, at]
        dst[:, at] = value.astype(dst.dtype)


def wide_dot_t(dst, left, right, tile=512, add=None):
    across = dst.shape[-1]
    for start in range(0, across, tile):
        at = pl.ds(start, min(tile, across - start))
        value = mm_t(left, right[at, :])
        if add is not None:
            value = value + add[:, at]
        dst[:, at] = value.astype(dst.dtype)


def rest_loads(rest_ref, goals, sems, order):
    width = goals[0].shape[1]
    copies = {}
    for slot in order:
        copies[slot] = pltpu.make_async_copy(
            rest_ref.at[:, pl.ds(slot * width, width)], goals[slot], sems.at[slot]
        )
        copies[slot].start()
    return copies


def own_kernel(
    len_ref,
    rest_ref,
    x_ref,
    att_ref,
    text_ref,
    time_ref,
    par_ref,
    a_out,
    one_out,
    cin_out,
    ql_out,
    kl_out,
    q_out,
    kv_out,
    lse_out,
    oc_out,
    two_out,
    h2_out,
    w_o,
    w_co,
    w_cq,
    w_ck,
    w_cv,
    sems,
):
    loads = rest_loads(rest_ref, (w_o, w_co, w_cq, w_ck, w_cv), sems, (0, 2, 3, 4, 1))
    mods = time_ref[...] + par_ref[0:6, :]
    width = x_ref.shape[1]
    loads[0].wait()
    wide_dot(a_out, att_ref[...], w_o, add=par_ref.at[14:15])
    x_one = x_ref[...].astype(F32) + mods[2:3] * a_out[...]
    one_out[...] = x_one
    normed, _ = normal(x_one)
    cin_out[...] = (normed * par_ref[8:9, :] + par_ref[19:20, :]).astype(BF)
    loads[2].wait()
    wide_dot(ql_out, cin_out[...], w_cq, add=par_ref.at[15:16])
    value = ql_out[...]
    rho = lax.rsqrt(jnp.mean(value * value, axis=-1, keepdims=True) + EPS)
    q_out[...] = (value * rho * par_ref[9:10, :]).astype(BF)
    loads[3].wait()
    wide_dot(kl_out, text_ref[...], w_ck, add=par_ref.at[16:17])
    value = kl_out[...]
    rho = lax.rsqrt(jnp.mean(value * value, axis=-1, keepdims=True) + EPS)
    kv_out[0] = (value * rho * par_ref[10:11, :]).astype(BF)
    loads[4].wait()
    wide_dot(kv_out.at[1], text_ref[...], w_cv, add=par_ref.at[17:18])
    texts = text_ref.shape[0]
    rows = x_ref.shape[0]
    valid = lax.broadcasted_iota(jnp.int32, (rows, texts), 1) < len_ref[0]

    def attend(h, carry):
        head = lanes_at(h * HD, HD)
        scores = mm_t(q_out[:, head], kv_out[0, :, head]) * (HD ** (-0.5))
        scores = jnp.where(valid, scores, NEG)
        top = jnp.max(scores, -1, keepdims=True)
        raised = jnp.exp(scores - top)
        total = jnp.sum(raised, -1, keepdims=True)
        result = mm((raised / total).astype(BF), kv_out[1, :, head])
        oc_out[:, head] = result.astype(BF)
        lse_out[h] = jnp.broadcast_to(top + jnp.log(total), (rows, HD))
        return carry

    lax.fori_loop(0, width // HD, attend, 0)
    loads[1].wait()
    wide_dot(two_out, oc_out[...], w_co, add=par_ref.at[18:19])
    x_two = one_out[...] + two_out[...]
    two_out[...] = x_two
    normed, _ = normal(x_two)
    h2_out[...] = (normed * (1.0 + mods[4:5]) + mods[3:4]).astype(BF)


def own_tokens(lengths, rest, x_own, att_tok, text, time_rows, params):
    rows, width = x_own.shape
    texts = text.shape[0]
    shape = jax.ShapeDtypeStruct
    in_vmem = pl.BlockSpec(memory_space=pltpu.VMEM)
    weight = pltpu.VMEM((width, width), BF)
    names = ("a", "one", "cin", "ql", "kl", "q", "kv", "lse", "oc", "two", "h2")
    outs = (
        shape((rows, width), F32),
        shape((rows, width), F32),
        shape((rows, width), BF),
        shape((rows, width), F32),
        shape((texts, width), F32),
        shape((rows, width), BF),
        shape((2, texts, width), BF),
        shape((width // HD, rows, HD), F32),
        shape((rows, width), BF),
        shape((rows, width), F32),
        shape((rows, width), BF),
    )
    results = pl.pallas_call(
        own_kernel,
        out_shape=outs,
        in_specs=[
            pl.BlockSpec(memory_space=pltpu.SMEM),
            pl.BlockSpec(memory_space=pl.ANY),
        ]
        + [in_vmem] * 5,
        out_specs=(in_vmem,) * len(outs),
        scratch_shapes=[weight] * 5 + [pltpu.SemaphoreType.DMA((5,))],
        compiler_params=pltpu.CompilerParams(vmem_limit_bytes=58 * 2**20),
    )(lengths, rest, x_own, att_tok, text, time_rows, params)
    return types.SimpleNamespace(**dict(zip(names, results)))


def own_back_kernel(names, *refs):
    ref = types.SimpleNamespace(**dict(zip(names, refs)))
    sems, out_sem = ref.sems, ref.out_sem
    w_a, w_b, w_c = (getattr(ref, name) for name in ("w_a", "w_b", "w_c"))
    loads = rest_loads(ref.rest, (w_a, w_a, w_b, w_c, w_b), sems, (1, 2, 3))
    par_ref, sums = ref.par, ref.sums
    mods = ref.time[...] + par_ref[0:6, :]
    rows, width = ref.x_two.shape
    texts = ref.text_in.shape[0]
    sums[...] = jnp.zeros(sums.shape, F32)
    grad_y = ref.cot[...].astype(F32)
    sums[20:21, :] = column_total((grad_y * mods[5:6]).astype(BF))
    d_rows = ref.d_rows[...]
    normed, spread = normal(ref.x_two[...])
    sums[3:4, :] = column_total(d_rows)
    sums[4:5, :] = column_total(d_rows * normed)
    dx_ref = ref.dx
    dx_ref[...] = grad_y + normal_back(normed, spread, d_rows * (1.0 + mods[4:5]))
    low_ref = ref.low
    low_ref[...] = dx_ref[...].astype(BF)
    sums[18:19, :] = column_total(low_ref[...])

    saves = []

    def weight_grad(name, left, right, column=0):
        stage = ref.stage
        tile = 384
        for k, start in enumerate(range(0, width, tile)):
            slot = len(saves) % 2
            if len(saves) >= 2:
                saves[-2].wait()
            stage[slot] = mm_first(left[:, start : start + tile], right[...]).astype(BF)
            copy = pltpu.make_async_copy(
                stage.at[slot],
                getattr(ref, name).at[pl.ds(start, tile), pl.ds(column, width)],
                out_sem.at[slot],
            )
            copy.start()
            saves.append(copy)

    weight_grad("co", ref.oc, low_ref)
    loads[1].wait()
    doc_ref = ref.doc
    wide_dot_t(doc_ref, low_ref[...], w_a)
    loads.update(rest_loads(ref.rest, (w_a,), sems, (0,)))
    dq_ref, dkv_ref = ref.dq, ref.dkv
    q_ref, kv_ref = ref.q, ref.kv
    scale = HD ** (-0.5)
    valid = lax.broadcasted_iota(jnp.int32, (rows, texts), 1) < ref.len[0]

    def attend(h, carry):
        head = lanes_at(h * HD, HD)
        query, keys, grad = q_ref[:, head], kv_ref[0, :, head], doc_ref[:, head]
        scores = mm_t(query, keys) * scale
        scores = jnp.where(valid, scores, NEG)
        probs = jnp.exp(scores - ref.lse[h, :, 0:1])
        dkv_ref[1, :, head] = mm_first(probs.astype(BF), grad)
        d_probs = mm_t(grad, kv_ref[1, :, head])
        lean = jnp.sum(probs * d_probs, -1, keepdims=True)
        d_scores = (probs * (d_probs - lean)).astype(BF)
        dq_ref[:, head] = mm(d_scores, keys) * scale
        dkv_ref[0, :, head] = mm_first(d_scores, query) * scale
        return carry

    lax.fori_loop(0, width // HD, attend, 0)

    def rms_back(value, gain, grad):
        rho = lax.rsqrt(jnp.mean(value * value, axis=-1, keepdims=True) + EPS)
        lean = jnp.mean(value * gain * grad, axis=-1, keepdims=True)
        return (
            rho * gain * grad - value * (rho * rho * rho * lean),
            jnp.sum(grad * value * rho, 0, keepdims=True),
        )

    back_q, gain_q = rms_back(ref.ql[...], par_ref[9:10, :], dq_ref[...])
    low_ref[...] = back_q.astype(BF)
    sums[9:10, :] = gain_q
    sums[15:16, :] = column_total(low_ref[...])
    loads[2].wait()
    wide_dot_t(dq_ref, low_ref[...], w_b)
    loads.update(rest_loads(ref.rest, (w_b,) * 5, sems, (4,)))
    d_cin = dq_ref[...]
    normed, spread = normal(ref.x_one[...])
    sums[8:9, :] = column_total(d_cin * normed)
    sums[19:20, :] = column_total(d_cin)
    dx_ref[...] += normal_back(normed, spread, d_cin * par_ref[8:9, :])
    weight_grad("cq", ref.cin, low_ref)
    sums[2:3, :] = column_total(dx_ref[...] * ref.a[...])
    low_ref[...] = (dx_ref[...] * mods[2:3]).astype(BF)
    sums[14:15, :] = column_total(low_ref[...])
    loads[0].wait()
    wide_dot_t(ref.d_att, low_ref[...], w_a)
    weight_grad("o", ref.att, low_ref)
    back_k, gain_k = rms_back(ref.kl[...], par_ref[10:11, :], dkv_ref[0])
    sums[10:11, :] = gain_k
    klow_ref, vlow_ref = ref.klow, ref.vlow
    klow_ref[...] = back_k.astype(BF)
    vlow_ref[...] = dkv_ref[1].astype(BF)
    sums[16:17, :] = column_total(klow_ref[...])
    sums[17:18, :] = column_total(vlow_ref[...])
    weight_grad("ckv", ref.text_in, klow_ref)
    weight_grad("ckv", ref.text_in, vlow_ref, width)
    loads[3].wait()
    wide_dot_t(dkv_ref.at[0], klow_ref[...], w_c)
    loads[4].wait()
    wide_dot_t(ref.text_part, vlow_ref[...], w_b, add=dkv_ref.at[0])
    for copy in saves[-2:]:
        copy.wait()


def own_back(**values):
    arrays = types.SimpleNamespace(**values)
    shape = jax.ShapeDtypeStruct
    rows, width = arrays.x_two.shape
    texts = arrays.text_in.shape[0]
    in_any = ["rest"]
    ins = ["x_two", "x_one", "d_rows", "cot", "time", "par", "a", "cin", "ql", "kl", "q", "kv"]
    ins += ["lse", "oc", "att", "text_in"]
    any_outs = {name: shape((width, width), BF) for name in ("o", "co", "cq")}
    any_outs.update(ckv=shape((width, 2 * width), BF))
    outs = dict(
        d_att=shape((rows, width), BF),
        dx=shape((rows, width), F32),
        text_part=shape((texts, width), BF),
        sums=shape((32, width), F32),
    )
    vmem = pltpu.VMEM
    weight = vmem((width, width), BF)
    scratch = {name: weight for name in ("w_a", "w_b", "w_c")}
    scratch.update(
        dict(
            low=vmem((rows, width), BF),
            doc=vmem((rows, width), BF),
            dq=vmem((rows, width), F32),
            dkv=vmem((2, texts, width), F32),
            klow=vmem((texts, width), BF),
            vlow=vmem((texts, width), BF),
            stage=vmem((2, 384, width), BF),
            sems=pltpu.SemaphoreType.DMA((5,)),
            out_sem=pltpu.SemaphoreType.DMA((2,)),
        )
    )
    any_place = pl.BlockSpec(memory_space=pl.ANY)
    in_vmem = pl.BlockSpec(memory_space=pltpu.VMEM)
    names = ["len"] + in_any + ins + list(any_outs) + list(outs) + list(scratch)
    results = pl.pallas_call(
        functools.partial(own_back_kernel, names),
        out_shape=tuple(any_outs.values()) + tuple(outs.values()),
        in_specs=[pl.BlockSpec(memory_space=pltpu.SMEM), any_place] + [in_vmem] * len(ins),
        out_specs=(any_place,) * len(any_outs) + (in_vmem,) * len(outs),
        scratch_shapes=list(scratch.values()),
        compiler_params=pltpu.CompilerParams(vmem_limit_bytes=60 * 2**20),
    )(*[getattr(arrays, name) for name in ["len"] + in_any + ins])
    return types.SimpleNamespace(**dict(zip(list(any_outs) + list(outs), results)))


def feed_kernel(n_sp, names, *refs):
    ref = types.SimpleNamespace(**dict(zip(names, refs)))
    zs, zr, ds, dr, local, cs, cr, saves_sem = (
        getattr(ref, name) for name in ("zs", "zr", "ds", "dr", "local", "cs", "cr", "saves")
    )
    spot_d = lax.axis_index(DP)
    spot_s = lax.axis_index(SP)
    core = lax.rem(spot_d, 2)
    core_id = {DP: spot_d + 1 - 2 * core}
    line = [{SP: lax.rem(spot_s + step, n_sp)} for step in range(1, n_sp)]
    h2_ref, all_ref = ref.h2, ref.h2_all
    rows, width = h2_ref.shape
    hidden = ref.in_own.shape[0]
    win, wout = ref.win, ref.wout
    meet(line + [core_id])

    pieces = 2
    piece = rows // pieces

    def token_copy(way, k, part):
        block = spot_s - k if way == 0 else spot_s + k
        at = all_ref.at[rows_at(block * rows + part * piece, piece)]
        src = h2_ref.at[pl.ds(part * piece, piece)] if k == 0 else at
        target = {SP: spot_s + 1 if way == 0 else spot_s - 1}
        index = (way * (n_sp - 1) + k) * pieces + part
        return remote_copy(src, at, zs.at[index], zr.at[index], target)

    def sends(way, k):
        if way == 0:
            return jnp.logical_and(spot_s < n_sp - 1, spot_s >= k)
        return jnp.logical_and(spot_s > 0, spot_s + k < n_sp)

    def gets(way, k):
        return spot_s > k if way == 0 else spot_s + k + 1 < n_sp

    def token_step(k):
        for part in range(pieces):
            for way in range(2):
                if k > 0:

                    @pl.when(gets(way, k - 1))
                    def _():
                        token_copy(way, k - 1, part).wait_recv()

                if k < n_sp - 1:

                    @pl.when(sends(way, k))
                    def _():
                        token_copy(way, k, part).start()

    token_step(0)
    keep = pltpu.make_async_copy(h2_ref, all_ref.at[rows_at(spot_s * rows, rows)], local.at[0])
    keep.start()
    loads = [
        pltpu.make_async_copy(getattr(ref, src), goal.at[pl.ds(part * hidden, hidden)], local.at[1 + k])
        for k, (src, goal, part) in enumerate(
            (("in_own", win, 0), ("in_other", win, 1), ("out_own", wout, 0), ("out_other", wout, 1))
        )
    ]
    for copy in loads:
        copy.start()
    gate = ref.time[5:6, :] + ref.par[5:6, :]
    ref.du_sums[...] = jnp.zeros(ref.du_sums.shape, F32)
    cot_ref, dz_ref, g_ref, du_ref = ref.cot, ref.dz, ref.g, ref.du
    z_ref, part_ref, recv_ref, own_ref = ref.z, ref.part, ref.recv, ref.own
    tiles = []
    start = 0
    while start < 2 * hidden:
        tiles.append((start, min(768, 2 * hidden - start)))
        start += 768
    bend = (2.0 / np.pi) ** 0.5
    keep.wait()
    for copy in loads:
        copy.wait()

    def near(k):
        first = (spot_s >= k).astype(jnp.int32)
        return first, first + (spot_s + k < n_sp).astype(jnp.int32)

    def grad_copy(block, owner):
        return remote_copy(
            part_ref.at[block],
            recv_ref.at[spot_s],
            ds.at[block],
            dr.at[owner],
            {SP: block},
        )

    def one(i, carry):
        block = spot_s
        before = jnp.int32(1)
        for k in range(1, n_sp):
            first, count = near(k)

            @pl.when(i == before)
            def _(k=k):
                token_step(k)

            here = jnp.logical_and(i >= before, i < before + count)
            ahead = jnp.logical_and(first == 1, i == before)
            block = jnp.where(here, jnp.where(ahead, spot_s - k, spot_s + k), block)
            before = before + count
        at = rows_at(block * rows, rows)
        dz_ref[at, :] = (cot_ref[at, :].astype(F32) * gate).astype(BF)
        for start, size in tiles:
            place = pl.ds(start, size)
            u = mm_t(all_ref[at, :], win[place, :]) + ref.bias[:, place]
            cube = bend * (u + 0.044715 * (u * u * u))
            t = jnp.tanh(cube)
            g_ref[at, place] = (0.5 * u * (1.0 + t)).astype(BF)
            slope = 0.5 * (1.0 + t) + (0.5 * bend) * u * (1.0 - t * t) * (
                1.0 + (3 * 0.044715) * (u * u)
            )
            grad = (mm_t(dz_ref[at, :], wout[place, :]) * slope).astype(BF)
            du_ref[at, place] = grad
            ref.du_sums[:, place] += column_total(grad)
        for start in range(0, width, 512):
            place = pl.ds(start, 512)
            value = mm(du_ref[at, :], win[:, place])
            part_ref[block, :, place] = value.astype(BF)

            @pl.when(i == 0)
            def _():
                own_ref[:, place] = value

        @pl.when(i > 0)
        def _():
            grad_copy(block, spot_s).start()

        for start in range(0, width, 512):
            place = pl.ds(start, 512)
            z_ref[block, :, place] = mm(g_ref[at, :], wout[:, place]).astype(BF)
        return carry

    lax.fori_loop(0, n_sp, one, 0)
    z_save = pltpu.make_async_copy(z_ref, ref.z_out, local.at[5])
    z_save.start()

    def weight_grad(goal, left, right):
        start = 0
        while start < 2 * hidden:
            size = min(256, 2 * hidden - start)
            goal[start : start + size, :] = mm_first(
                left[:, start : start + size], right[...]
            ).astype(BF)
            start += size

    half = hidden // 2
    core_copies = []

    def core_hop(which, goal):
        for part in range(2):
            copy = remote_copy(
                goal.at[rows_at(part * hidden + (1 - core) * half, half)],
                ref.core_recv.at[which, part],
                cs.at[2 * which + part],
                cr.at[2 * which + part],
                core_id,
            )
            copy.start()
            core_copies.append(copy)

    weight_grad(win, du_ref, all_ref)
    core_hop(0, win)
    weight_grad(wout, g_ref, dz_ref)
    core_hop(1, wout)
    low_ref = ref.core_recv
    out_copies = []
    chunk = half // 5
    for which, goal in enumerate((win, wout)):
        for part in range(2):
            core_copies[2 * which + part].wait_recv()
            for k in range(5):
                at = rows_at(part * hidden + core * half + k * chunk, chunk)
                value = goal[at, :].astype(F32) + low_ref[
                    which, part, k * chunk : (k + 1) * chunk
                ].astype(F32)
                low_ref[which, part, k * chunk : (k + 1) * chunk] = value.astype(BF)
            copy = pltpu.make_async_copy(
                low_ref.at[which, part],
                (ref.fi_own, ref.fi_far, ref.fo_own, ref.fo_far)[2 * which + part],
                saves_sem.at[2 * which + part],
            )
            copy.start()
            out_copies.append(copy)
    for step in range(1, n_sp):
        other = lax.rem(spot_s + step, n_sp)
        grad_copy(other, other).wait_recv()
    total = own_ref[...]
    for step in range(1, n_sp):
        total = total + recv_ref[lax.rem(spot_s + step, n_sp)].astype(F32)
    ref.d_rows[...] = total
    for copy in out_copies + [z_save]:
        copy.wait()
    for copy in core_copies:
        copy.wait_send()
    for step in range(1, n_sp):
        other = lax.rem(spot_s + step, n_sp)
        grad_copy(other, other).wait_send()
    for k in range(n_sp - 1):
        for part in range(pieces):
            for way in range(2):

                @pl.when(sends(way, k))
                def _():
                    token_copy(way, k, part).wait_send()


def feed(**values):
    arrays = types.SimpleNamespace(**values)
    n_sp = lax.axis_size(SP)
    shape = jax.ShapeDtypeStruct
    rows, width = arrays.h2.shape
    hidden = arrays.in_own.shape[0]
    total = n_sp * rows
    ins_any = ["in_own", "in_other", "out_own", "out_other", "h2"]
    ins = ["cot", "bias", "time", "par"]
    any_outs = dict(
        z_out=shape((n_sp, rows, width), BF),
        fi_own=shape((hidden // 2, width), BF),
        fi_far=shape((hidden // 2, width), BF),
        fo_own=shape((hidden // 2, width), BF),
        fo_far=shape((hidden // 2, width), BF),
    )
    outs = {"d_rows": shape((rows, width), F32), "du_sums": shape((1, 2 * hidden), F32)}
    vmem = pltpu.VMEM
    dma = pltpu.SemaphoreType.DMA
    scratch = dict(
        h2_all=vmem((total, width), BF),
        win=vmem((2 * hidden, width), BF),
        wout=vmem((2 * hidden, width), BF),
        dz=vmem((total, width), BF),
        g=vmem((total, 2 * hidden), BF),
        du=vmem((total, 2 * hidden), BF),
        z=vmem((n_sp, rows, width), BF),
        part=vmem((n_sp, rows, width), BF),
        recv=vmem((n_sp, rows, width), BF),
        own=vmem((rows, width), F32),
        core_recv=vmem((2, 2, hidden // 2, width), BF),
        zs=dma((4 * (n_sp - 1),)),
        zr=dma((4 * (n_sp - 1),)),
        ds=dma((n_sp,)),
        dr=dma((n_sp,)),
        local=dma((6,)),
        cs=dma((4,)),
        cr=dma((4,)),
        saves=dma((4,)),
    )
    any_place = pl.BlockSpec(memory_space=pl.ANY)
    in_vmem = pl.BlockSpec(memory_space=pltpu.VMEM)
    names = ins_any + ins + list(any_outs) + list(outs) + list(scratch)
    results = pl.pallas_call(
        functools.partial(feed_kernel, n_sp, names),
        out_shape=tuple(any_outs.values()) + tuple(outs.values()),
        in_specs=[any_place] * len(ins_any) + [in_vmem] * len(ins),
        out_specs=(any_place,) * len(any_outs) + (in_vmem,) * len(outs),
        scratch_shapes=list(scratch.values()),
        compiler_params=pltpu.CompilerParams(
            collective_id=3, has_side_effects=True, vmem_limit_bytes=60 * 2**20
        ),
    )(*[getattr(arrays, name) for name in ins_any + ins])
    return types.SimpleNamespace(**dict(zip(list(any_outs) + list(outs), results)))


class Later:
    def __init__(self, make):
        self.make = make

    def wait_recv(self):
        self.make().wait_recv()

    def wait_send(self):
        self.make().wait_send()


def back_kernel(n_sp, n_dp, names, *refs):
    ref = types.SimpleNamespace(**dict(zip(names, refs)))
    sem_send, sem_recv, sem_local = ref.send, ref.recv, ref.local
    spot_d = lax.axis_index(DP)
    spot_b = lax.axis_index(BLK)
    spot_s = lax.axis_index(SP)
    core = lax.rem(spot_d, 2)
    pair = lax.rem(spot_d // 2, 2)

    def dp_id(bit):
        return {DP: spot_d + bit - 2 * bit * lax.rem(spot_d // bit, 2)}

    bits = []
    bit = 4
    while bit < n_dp:
        bits.append(bit)
        bit *= 2
    core_id, pair_id, blk_id = dp_id(1), dp_id(2), {BLK: 1 - spot_b}
    line = [{SP: lax.rem(spot_s + step, n_sp)} for step in range(1, n_sp)]
    used = [0]
    sent = []

    def send(src, dst, target, view=None):
        index = used[0]
        used[0] += 1
        copy = remote_copy(src, dst, sem_send.at[index], sem_recv.at[index], target)
        copy.start()
        if view is not None:
            copy = Later(
                lambda: remote_copy(
                    view(), view(), sem_send.at[index], sem_recv.at[index], target
                )
            )
        sent.append(copy)
        return copy

    def add_blocks(dst, sources):
        lead = len(dst.shape) - 2

        def body(*blocks):
            total = blocks[0][...].astype(F32)
            for block in blocks[1:-1]:
                total = total + block[...].astype(F32)
            blocks[-1][...] = total.astype(blocks[-1].dtype)

        if lead == 0:
            grid = (dst.shape[0] // 16,)
            spec = pl.BlockSpec((16, dst.shape[1]), lambda place: (place, 0))
        else:
            group = 1
            each = 2 * int(np.prod(dst.shape[1:]))
            while dst.shape[0] % (2 * group) == 0 and 2 * group * each <= 700_000:
                group *= 2
            grid = (dst.shape[0] // group,)
            spec = pl.BlockSpec(
                (group,) + tuple(dst.shape[1:]), lambda place: (place,) + (0,) * (lead + 1)
            )
        pltpu.emit_pipeline(
            body,
            grid=grid,
            in_specs=[spec] * len(sources),
            out_specs=[spec],
        )(*sources, dst)

    meet(line + [core_id, pair_id, blk_id] + [dp_id(bit) for bit in bits])
    d_att, do_ref = ref.d_att, ref.do
    rows = d_att.shape[0]
    total_rows = n_sp * rows
    cols = do_ref.shape[1]
    heads_here = cols // HD
    width = d_att.shape[1]

    def tok(block):
        return rows_at(block * rows, rows)

    do_own = pltpu.make_async_copy(
        d_att.at[:, lanes_at(spot_s * cols, cols)], do_ref.at[tok(spot_s)], sem_local.at[0]
    )
    do_own.start()
    do_away = [
        send(
            d_att.at[:, lanes_at(lax.rem(spot_s + step, n_sp) * cols, cols)],
            do_ref.at[tok(spot_s)],
            line[step - 1],
        )
        for step in range(1, n_sp)
    ]
    groups = ("co", "ckv")
    hop = {}
    for name in groups:
        hop[name] = send(getattr(ref, name).at[:, 1 - core], getattr(ref, name + "_rc"), core_id)
    hop["text"] = send(ref.text.at[1 - spot_b], ref.text_rx, blk_id)

    blocks8 = 2 * n_sp

    def core_done(name):
        hop[name].wait_recv()
        add_blocks(getattr(ref, name + "_kc"), [getattr(ref, name).at[:, core], getattr(ref, name + "_rc")])

    score_scale = HD ** (-0.5)
    dq_ref, dkv_ref = ref.dq, ref.dkv

    def ff_last(name):
        at = getattr(ref, name + "_out").at[core]
        ry = getattr(ref, name + "_ry")
        kx = getattr(ref, name + "_kx")
        hop[name].wait_recv()
        for k in range(len(bits) + 1):
            goal = at if k == len(bits) else getattr(ref, name + "_ky").at[k]
            source = kx if k == 0 else getattr(ref, name + "_ky").at[k - 1]
            add_blocks(goal, [source, ry.at[k]])
            if k < len(bits):
                send(goal, ry.at[k + 1], dp_id(bits[k])).wait_recv()
        hop[name] = send(at, at, core_id)

    def pair_done(name, go=True):
        if name in hop:
            hop[name].wait_recv()
            add_blocks(getattr(ref, name + "_ky"), [getattr(ref, name + "_kc").at[:, pair], getattr(ref, name + "_ry")])
            del hop[name]
        if not go:
            return
        hop[name] = send(
            getattr(ref, name + "_ky").at[pl.ds((1 - spot_b) * n_sp, n_sp)], getattr(ref, name + "_rx"), blk_id
        )

    def blk_done(name):
        hop[name].wait_recv()
        own_blk = getattr(ref, name + "_ky").at[pl.ds(spot_b * n_sp, n_sp)]
        add_blocks(getattr(ref, name + "_kx"), [own_blk, getattr(ref, name + "_rx")])

    def line_send(name):
        hop[name] = [
            send(
                getattr(ref, name + "_kx").at[lax.rem(spot_s + step, n_sp)],
                getattr(ref, name + "_rz").at[step - 1],
                line[step - 1],
            )
            for step in range(1, n_sp)
        ]

    def first_blk_done(name):
        hop[name].wait_recv()
        own_blk = getattr(ref, name + "_kc").at[pl.ds(spot_b * n_sp, n_sp)]
        add_blocks(getattr(ref, name + "_ky"), [own_blk, getattr(ref, name + "_rx")])
        hop[name] = send(getattr(ref, name + "_ky").at[:, 1 - pair], getattr(ref, name + "_ry"), pair_id)

    def then_pair_done(name):
        hop[name].wait_recv()
        add_blocks(getattr(ref, name + "_kx"), [getattr(ref, name + "_ky").at[:, pair], getattr(ref, name + "_ry")])
        line_send(name)

    def attention(q_here, kv_here, lse_here):
        ref.q_here, ref.kv_here, ref.lse_here = q_here, kv_here, lse_here
        loads = [
            pltpu.make_async_copy(getattr(ref, name), getattr(ref, name + "_here"), sem_local.at[2 + k])
            for k, name in enumerate(("q", "kv", "lse"))
        ]
        for copy in loads:
            copy.start()
        q_ref, kv_ref, lse_ref = ref.q_here, ref.kv_here, ref.lse_here
        dkv_ref[...] = jnp.zeros(dkv_ref.shape, F32)

        def attend(block, carry):
            at = tok(block)
            for h in range(heads_here):
                head = pl.ds(h * HD, HD)
                query = q_ref[at, head]
                grad = do_ref[at, head]
                keys = kv_ref[0, :, head]
                scores = mm_t(query, keys) * score_scale
                probs = jnp.exp(scores - lse_ref[h, at, 0:1])
                dkv_ref[1, :, head] += mm_first(probs.astype(BF), grad)
                d_probs = mm_t(grad, kv_ref[1, :, head])
                lean = jnp.sum(probs * d_probs, -1, keepdims=True)
                d_scores = (probs * (d_probs - lean)).astype(BF)
                dq_ref[at, head] = mm(d_scores, keys) * score_scale
                dkv_ref[0, :, head] += mm_first(d_scores, query) * score_scale
            return carry

        add_blocks(ref.fi_kx, [ref.fi, ref.fi_rx])
        goal = lambda: ref.fi_ry.at[0]
        hop["fi"] = send(ref.fi_kx, goal(), pair_id, goal)
        for copy in loads:
            copy.wait()
        do_own.wait()
        for copy in do_away:
            copy.wait_recv()
        lax.fori_loop(0, 1, attend, 0)
        core_done("co")
        goal = lambda: ref.co_rx
        hop["co"] = send(
            ref.co_kc.at[pl.ds((1 - spot_b) * n_sp, n_sp)], goal(), blk_id, goal
        )
        core_done("ckv")
        goal = lambda: ref.ckv_ry
        hop["ckv"] = send(ref.ckv_kc.at[:, 1 - pair], goal(), pair_id, goal)
        for name in ("cq", "o"):
            goal = lambda name=name: getattr(ref, name + "_rc")
            hop[name] = send(getattr(ref, name).at[:, 1 - core], goal(), core_id, goal)
        lax.fori_loop(1, 2, attend, 0)
        core_done("o")
        hop["o"] = []
        for step in range(1, n_sp):
            for half in range(2):
                goal = lambda step=step, half=half: ref.o_rz.at[step - 1, half]
                src = ref.o_kc.at[half * n_sp + lax.rem(spot_s + step, n_sp)]
                hop["o"].append(send(src, goal(), line[step - 1], goal))
        core_done("cq")
        lax.fori_loop(2, n_sp, attend, 0)

    pl.run_scoped(
        attention,
        pltpu.VMEM(ref.q.shape, BF),
        pltpu.VMEM(ref.kv.shape, BF),
        pltpu.VMEM(ref.lse.shape, F32),
    )

    kv_recv, proj_ref = ref.kv_recv, ref.proj
    kv_away = []
    for which in range(2):
        place = pl.ds(which * cols, cols)
        proj_ref[:, place] = dkv_ref[which, total_rows:, :].astype(BF)
        kv_away.append(send(proj_ref.at[:, place], kv_recv.at[which], blk_id))
    hop["text"].wait_recv()
    text_kx = ref.text_kx
    add_blocks(text_kx, [ref.text.at[spot_b], ref.text_rx])
    hop["text"] = [
        send(
            text_kx.at[lax.rem(spot_s + step, n_sp)],
            ref.text_rz.at[step - 1],
            line[step - 1],
        )
        for step in range(1, n_sp)
    ]

    lin_ref, rho_ref, trig_ref = ref.lin, ref.rho, ref.trig
    par_ref, sums_ref = ref.par, ref.sums
    sums_ref[spot_s] = jnp.zeros((8, total_rows), F32)

    def gain_of(which, h):
        return par_ref[6 + which : 7 + which, lanes_at(spot_s * cols + h * HD, HD)]

    def unturn(which, block, carry):
        at = tok(block)
        cosine = trig_ref[0, at, :]
        sine = trig_ref[1, at, :]
        lean = jnp.zeros((rows, HD), F32)
        for h in range(heads_here):
            head = pl.ds(h * HD, HD)
            if which == 0:
                grad = dq_ref[at, head]
            else:
                grad = dkv_ref[0, at, head] + kv_recv[0, at, head].astype(F32)
            grad = turned(grad, cosine, -sine)
            if which == 0:
                dq_ref[at, head] = grad
            else:
                dkv_ref[0, at, head] = grad
            lean = lean + lin_ref[which, at, head] * gain_of(which, h) * grad
        total = exact_sums(lean)
        sums_ref[spot_s, which : which + 1, lanes_at(block * rows, rows)] = total[0:1]
        return carry

    lax.fori_loop(0, n_sp, functools.partial(unturn, 0), 0)
    first_blk_done("co")
    ff_last("fi")
    for copy in kv_away:
        copy.wait()
    sent[:] = [copy for copy in sent if all(copy is not other for other in kv_away)]
    def first_blk_send(name):
        hop[name] = send(
            getattr(ref, name + "_kc").at[pl.ds((1 - spot_b) * n_sp, n_sp)], getattr(ref, name + "_rx"), blk_id
        )

    first_blk_send("cq")
    early, late = pl.ds(0, 2), pl.ds(2, 3)
    hop["fo"] = send(ref.fo_far.at[late], ref.fo_rx, blk_id)
    add_blocks(ref.fo_kx.at[early], [ref.fo.at[early], ref.fo_rx1])
    fo_early = send(ref.fo_kx.at[early], ref.fo_ry.at[0, early], pair_id)
    lax.fori_loop(0, n_sp, functools.partial(unturn, 1), 0)
    sums_away = [
        send(sums_ref.at[spot_s], sums_ref.at[spot_s], line[k]) for k in range(n_sp - 1)
    ]
    then_pair_done("co")
    for copy in hop["o"]:
        copy.wait_recv()
    for half in range(2):
        add_blocks(
            ref.o_kl.at[half],
            [ref.o_kc.at[half * n_sp + spot_s]]
            + [ref.o_rz.at[k, half] for k in range(n_sp - 1)],
        )
    hop["o"] = send(ref.o_kl.at[1 - spot_b], ref.o_rx, blk_id)
    for copy in sums_away:
        copy.wait_recv()
    means = sums_ref[0]
    for k in range(1, n_sp):
        means = means + sums_ref[k]
    sums_ref[n_sp] = means / width
    small_ref = ref.small
    own = lanes_at(spot_s * cols, cols)
    small_ref[0] = ref.small_in[...]
    small_ref[0, 5:6, :] = ref.gate2[...]
    small_ref[0, 21 : 21 + ref.hidden_rows.shape[0], :] = ref.hidden_rows[...]
    for row in (6, 7, 11, 12, 13):
        small_ref[0, row : row + 1, :] = jnp.zeros((1, width), F32)

    def project(block, carry):
        at = tok(block)
        for which in range(2):
            mean = exact_first(sums_ref[n_sp, :, lanes_at(block * rows, rows)], row_pick(which))
            rho = rho_ref[which, at, :]
            cube = rho * rho * rho * mean
            for h in range(heads_here):
                head = pl.ds(h * HD, HD)
                grad = dq_ref[at, head] if which == 0 else dkv_ref[0, at, head]
                value = lin_ref[which, at, head]
                low = (rho * gain_of(which, h) * grad - value * cube).astype(BF)
                place = pl.ds(which * cols + h * HD, HD)
                proj_ref[at, place] = low
                here = lanes_at(spot_s * cols + h * HD, HD)
                small_ref[0, 6 + which : 7 + which, here] += jnp.sum(
                    grad * value * rho, 0, keepdims=True
                )
                small_ref[0, 11 + which : 12 + which, here] += jnp.sum(
                    low.astype(F32), 0, keepdims=True
                )
        low = (dkv_ref[1, at, :] + kv_recv[1, at, :].astype(F32)).astype(BF)
        proj_ref[at, 2 * cols :] = low
        small_ref[0, 13:14, own] += jnp.sum(low.astype(F32), 0, keepdims=True)
        return carry

    lax.fori_loop(0, n_sp, project, 0)
    dh1_ref, dh1_recv, sw_ref = ref.dh1, ref.dh1_recv, ref.sw
    chain_send, chain_recv = ref.chain_send, ref.chain_recv

    def chain_copy(way, block):
        if way == 0:
            slot, target = block, {SP: spot_s + 1}
        else:
            slot = jnp.where(block == spot_s - 1, n_sp, block)
            target = {SP: spot_s - 1}
        return remote_copy(
            dh1_ref.at[block],
            dh1_recv.at[slot],
            chain_send.at[way * n_sp + block],
            chain_recv.at[slot],
            target,
        )

    def chain_wait(slot):
        at = dh1_recv.at[slot]
        remote_copy(at, at, chain_send.at[0], chain_recv.at[slot], blk_id).wait_recv()

    def chain_pass(way, block, slot):
        total = dh1_ref[block].astype(F32) + dh1_recv[slot].astype(F32)
        dh1_ref[block] = total.astype(BF)
        chain_copy(way, block).start()

    def chain_step(time):
        right = n_sp - 1 + spot_s - time
        inside = jnp.logical_and(right >= spot_s, right < n_sp)

        @pl.when(jnp.logical_and(spot_s > 0, inside))
        def _():
            chain_wait(right)

            @pl.when(right > spot_s)
            def _():
                chain_pass(0, right, right)

        left = time - (n_sp - 1 - spot_s)
        inside = jnp.logical_and(left >= 0, left <= spot_s)

        @pl.when(jnp.logical_and(spot_s < n_sp - 1, inside))
        def _():
            slot = jnp.where(left == spot_s, n_sp, left)
            chain_wait(slot)

            @pl.when(left < spot_s)
            def _():
                chain_pass(1, left, slot)

    def products(w_ref, h1_ref, stage):
        sw_copies = []
        w_load = pltpu.make_async_copy(ref.w, w_ref, sem_local.at[0])
        h1_load = pltpu.make_async_copy(ref.h1, h1_ref, sem_local.at[1])
        w_load.start()
        h1_load.start()
        w_load.wait()
        def away(step, carry):
            turn = jnp.where(spot_s < n_sp // 2, n_sp - step, step)
            block = lax.rem(spot_s + turn, n_sp)
            for part in range(width // cols):
                place = pl.ds(part * cols, cols)
                value = mm_t(proj_ref[tok(block), :], w_ref[place, :])
                dh1_ref[block, :, place] = value.astype(BF)

            @pl.when(spot_s == 0)
            def _():
                chain_copy(0, block).start()

            @pl.when(spot_s == n_sp - 1)
            def _():
                chain_copy(1, block).start()

            return carry

        lax.fori_loop(1, n_sp, away, 0)
        for part in range(width // cols):
            place = pl.ds(part * cols, cols)
            ref.dh1_own[:, place] = mm_t(proj_ref[tok(spot_s), :], w_ref[place, :])
        h1_load.wait()
        for part in range(n_sp):
            value = mm_first(h1_ref[:, part * cols : (part + 1) * cols], proj_ref[...])
            value = value.astype(BF)
            slot = part % 2
            if part > 1:
                sw_copies[part - 2].wait()
            for k in range(4):
                half = cols // 4
                stage[slot, k // 2, k % 2] = value[k * half : (k + 1) * half]
            copy = pltpu.make_async_copy(
                stage.at[slot], sw_ref.at[pl.ds(2 * part, 2)], sem_local.at[2 + slot]
            )
            copy.start()
            sw_copies.append(copy)
        for copy in sw_copies[-2:]:
            copy.wait()
        hop["s"] = send(
            sw_ref.at[:, 1 - core], ref.s_rc, core_id, lambda: ref.s_rc
        )

    pl.run_scoped(
        products,
        pltpu.VMEM(ref.w.shape, BF),
        pltpu.VMEM(ref.h1.shape, BF),
        pltpu.VMEM((2, 2, 2, cols // 4, 3 * cols), BF),
    )

    pair_done("ckv")
    chain_step(1)
    hop["s"].wait_recv()
    add_blocks(ref.s_kc, [ref.sw.at[:, core], ref.s_rc])
    hop["s"] = send(ref.s_kc.at[pl.ds((1 - spot_b) * n_sp, n_sp)], ref.s_rx, blk_id)
    hop["o"].wait_recv()
    add_blocks(ref.o_kx, [ref.o_kl.at[spot_b], ref.o_rx])
    hop["o"] = send(ref.o_kx.at[1 - pair], ref.o_ry, pair_id)
    first_blk_done("cq")
    for k in range(2, n_sp - 1):
        chain_step(k)
    hop["fo"].wait_recv()
    add_blocks(ref.fo_kx.at[late], [ref.fo.at[late], ref.fo_rx])
    hop["fo"] = send(ref.fo_kx.at[late], ref.fo_ry.at[0, late], pair_id)
    then_pair_done("cq")
    hop["s"].wait_recv()
    own_blk = ref.s_kc.at[pl.ds(spot_b * n_sp, n_sp)]
    add_blocks(ref.s_kx, [own_blk, ref.s_rx])
    s_line = []
    s_keep = []
    for j in range(3):
        place = lanes_at(j * width + spot_s * cols, cols)
        part = pl.ds(j * cols, cols)
        copy = pltpu.make_async_copy(
            ref.s_kx.at[spot_s, :, part], ref.s_z.at[:, place], sem_local.at[2 + j]
        )
        copy.start()
        s_keep.append(copy)
        for step in range(1, n_sp):
            s_line.append(
                send(
                    ref.s_kx.at[lax.rem(spot_s + step, n_sp), :, part],
                    ref.s_z.at[:, place],
                    line[step - 1],
                )
            )

    def line_done(name):
        if name == "o":
            hop[name].wait_recv()
        else:
            for copy in hop[name]:
                copy.wait_recv()
        kx = getattr(ref, name + "_kx")
        out = getattr(ref, name + "_out").at[core]
        kz = getattr(ref, name + "_kz")
        if name == "o":
            add_blocks(kz.at[0], [kx.at[pair], ref.o_ry])
        else:
            rz = getattr(ref, name + "_rz")
            add_blocks(kz.at[0], [kx.at[spot_s]] + [rz.at[k] for k in range(n_sp - 1)])
        for k, bit in enumerate(bits):
            got = getattr(ref, name + "_rw").at[k]
            send(kz.at[k], got, dp_id(bit)).wait_recv()
            add_blocks(kz.at[k + 1], [kz.at[k], got])
        last = kz.at[len(bits)]
        own_copy = pltpu.make_async_copy(last, out.at[pair], sem_local.at[1])
        own_copy.start()
        hop[name] = send(last, out.at[pair], pair_id)
        own_copy.wait()

    def pair_back(name):
        hop[name].wait_recv()
        out = getattr(ref, name + "_out").at[core]
        hop[name] = send(out, out, core_id)

    line_done("co")
    line_done("o")
    for copy in hop["text"]:
        copy.wait_recv()
    add_blocks(
        ref.text_out.at[0],
        [text_kx.at[spot_s]] + [ref.text_rz.at[k] for k in range(n_sp - 1)],
    )

    chain_step(n_sp - 1)

    @pl.when(spot_s > 0)
    def _():
        ref.dh1_own[...] += dh1_recv[spot_s].astype(F32)

    @pl.when(spot_s < n_sp - 1)
    def _():
        ref.dh1_own[...] += dh1_recv[n_sp].astype(F32)

    d_shift = ref.dh1_own[...]
    values = ref.x[...].astype(F32)
    centre = values - jnp.mean(values, axis=-1, keepdims=True)
    spread = lax.rsqrt(jnp.mean(centre * centre, axis=-1, keepdims=True) + EPS)
    normed = centre * spread
    scale = 1.0 + (ref.time[1:2, :] + par_ref[1:2, :])
    grad = d_shift * scale
    lean = jnp.mean(grad, axis=-1, keepdims=True)
    tilt = jnp.mean(grad * normed, axis=-1, keepdims=True)
    ref.tokens_out[...] = ref.dx1[...] + spread * (grad - lean - normed * tilt)
    small_ref[0, 0:1, :] = jnp.sum(d_shift, 0, keepdims=True)
    small_ref[0, 1:2, :] = jnp.sum(d_shift * normed, 0, keepdims=True)
    partners = [core_id, pair_id] + [dp_id(bit) for bit in bits] + [blk_id]
    bit = 1
    while bit < n_sp:
        partners.append({SP: spot_s + bit - 2 * bit * lax.rem(spot_s // bit, 2)})
        bit *= 2

    def small_send(k):
        hop["small"] = send(small_ref.at[k], ref.small_recv.at[k], partners[k])

    def small_done(k):
        hop["small"].wait_recv()
        small_ref[k + 1] = small_ref[k] + ref.small_recv[k]
        if k + 1 < len(partners):
            small_send(k + 1)
        else:
            ref.small_out[...] = small_ref[k + 1]

    small_send(0)
    blk_done("ckv")
    line_send("ckv")
    small_done(0)

    small_done(1)
    pair_back("o")
    pair_back("co")
    for k in range(2, len(partners) - 2):
        small_done(k)
    line_done("cq")
    for copy in s_keep:
        copy.wait()
    for copy in s_line:
        copy.wait_recv()
    hop["s"] = send(ref.s_z, ref.s_ry.at[0], pair_id)
    small_done(len(partners) - 2)
    line_done("ckv")
    fo_early.wait_recv()
    ff_last("fo")
    small_done(len(partners) - 1)
    pair_back("cq")
    hop["s"].wait_recv()
    s_ry, s_out = ref.s_ry, ref.s_out
    for k in range(len(bits) + 1):
        source = ref.s_z if k == 0 else ref.s_kw.at[k - 1]
        goal = s_out.at[core] if k == len(bits) else ref.s_kw.at[k]
        add_blocks(goal, [source, s_ry.at[k]])
        if k < len(bits):
            send(goal, s_ry.at[k + 1], dp_id(bits[k])).wait_recv()
    hop["s"] = send(s_out.at[core], s_out.at[core], core_id)
    pair_back("ckv")
    for name in ("ckv", "co", "cq", "o", "fi", "fo", "s"):
        hop[name].wait_recv()
    for copy in sent:
        copy.wait_send()
    for block in range(n_sp):

        @pl.when(block > spot_s)
        def _():
            chain_copy(0, block).wait_send()

        @pl.when(block < spot_s)
        def _():
            chain_copy(1, block).wait_send()


def back(**values):
    arrays = types.SimpleNamespace(**values)
    n_sp = lax.axis_size(SP)
    n_dp = lax.axis_size(DP)
    shape = jax.ShapeDtypeStruct
    rows, width = arrays.d_att.shape
    total = n_sp * rows
    cols = arrays.q.shape[1]
    g8 = 2 * n_sp
    more = max(n_dp.bit_length() - 3, 0)
    any_names = ["ckv", "cq", "co", "o", "fi", "fo", "fi_rx", "fo_rx1", "fo_far", "d_att", "text", "q", "kv", "lse", "w", "h1"]
    vmem_names = ["lin", "rho", "trig", "par", "x", "dx1", "time", "small_in", "gate2", "hidden_rows"]
    outs = {}
    for name in ("ckv", "cq", "co", "o"):
        quarter, lanes = getattr(arrays, name).shape[3:]
        outs[name + "_rc"] = shape((g8, 2, quarter, lanes), BF)
        outs[name + "_kc"] = shape((g8, 2, quarter, lanes), BF)
        if name == "o":
            outs[name + "_rz"] = shape((n_sp - 1, 2, 2, quarter, lanes), BF)
            outs[name + "_kl"] = shape((2, 2, quarter, lanes), BF)
            outs[name + "_rx"] = shape((2, quarter, lanes), BF)
            outs[name + "_ry"] = shape((quarter, lanes), BF)
        elif name == "ckv":
            outs[name + "_ry"] = shape((g8, quarter, lanes), BF)
            outs[name + "_ky"] = shape((g8, quarter, lanes), BF)
            outs[name + "_rx"] = shape((n_sp, quarter, lanes), BF)
        else:
            outs[name + "_rx"] = shape((n_sp, 2, quarter, lanes), BF)
            outs[name + "_ky"] = shape((n_sp, 2, quarter, lanes), BF)
            outs[name + "_ry"] = shape((n_sp, quarter, lanes), BF)
        outs[name + "_kx"] = shape((2 if name == "o" else n_sp, quarter, lanes), BF)
        if name != "o":
            outs[name + "_rz"] = shape((n_sp - 1, quarter, lanes), BF)
        outs[name + "_kz"] = shape((more + 1, quarter, lanes), BF)
        outs[name + "_rw"] = shape((more + 1, quarter, lanes), BF)
        outs[name + "_out"] = shape((2, 2, quarter, lanes), BF)
    for name in ("fi", "fo"):
        half = getattr(arrays, name).shape
        outs[name + "_kx"] = shape(half, BF)
        outs[name + "_ry"] = shape((more + 1,) + half, BF)
        outs[name + "_ky"] = shape((more + 1,) + half, BF)
        outs[name + "_out"] = shape((2,) + half, BF)
    outs.update(fo_rx=shape((3,) + arrays.fo.shape[1:], BF))
    text_rows = arrays.text.shape[2]
    outs.update(text_rx=shape((n_sp, text_rows, width), BF))
    outs.update(text_kx=shape((n_sp, text_rows, width), BF))
    outs.update(text_rz=shape((n_sp - 1, text_rows, width), BF))
    outs.update(text_out=shape((1, text_rows, width), F32))
    half_rows = width // g8 // 2
    outs.update(sw=shape((g8, 2, half_rows, 3 * cols), BF))
    outs.update(s_rc=shape((g8, half_rows, 3 * cols), BF))
    outs.update(s_kc=shape((g8, half_rows, 3 * cols), BF))
    outs.update(s_rx=shape((n_sp, half_rows, 3 * cols), BF))
    outs.update(s_kx=shape((n_sp, half_rows, 3 * cols), BF))
    outs.update(s_z=shape((half_rows, 3 * width), BF))
    outs.update(s_ry=shape((more + 1, half_rows, 3 * width), BF))
    outs.update(s_kw=shape((more + 1, half_rows, 3 * width), BF))
    outs.update(s_out=shape((2, half_rows, 3 * width), BF))
    in_any = len(outs)
    outs.update(tokens_out=shape((rows, width), F32))
    outs.update(small_out=shape(arrays.small_in.shape, F32))
    steps = 3 + more + n_sp.bit_length() - 1
    vmem = pltpu.VMEM
    scratch = dict(
        do=vmem((total, cols), BF),
        dq=vmem((total, cols), F32),
        dkv=vmem((2, 2 * total, cols), F32),
        kv_recv=vmem((2, total, cols), BF),
        sums=vmem((n_sp + 1, 8, total), F32),
        proj=vmem((total, 3 * cols), BF),
        dh1=vmem((n_sp, rows, width), BF),
        dh1_own=vmem((rows, width), F32),
        dh1_recv=vmem((n_sp + 1, rows, width), BF),
        chain_send=pltpu.SemaphoreType.DMA((2 * n_sp,)),
        chain_recv=pltpu.SemaphoreType.DMA((n_sp + 1,)),
        small=vmem((steps + 1,) + arrays.small_in.shape, F32),
        small_recv=vmem((steps,) + arrays.small_in.shape, F32),
        send=pltpu.SemaphoreType.DMA((128,)),
        recv=pltpu.SemaphoreType.DMA((128,)),
        local=pltpu.SemaphoreType.DMA((5,)),
    )
    any_place = pl.BlockSpec(memory_space=pl.ANY)
    in_vmem = pl.BlockSpec(memory_space=pltpu.VMEM)
    names = any_names + vmem_names + list(outs) + list(scratch)
    results = pl.pallas_call(
        functools.partial(back_kernel, n_sp, n_dp, names),
        out_shape=tuple(outs.values()),
        in_specs=[any_place] * len(any_names) + [in_vmem] * len(vmem_names),
        out_specs=(any_place,) * in_any + (in_vmem,) * (len(outs) - in_any),
        scratch_shapes=list(scratch.values()),
        compiler_params=pltpu.CompilerParams(
            collective_id=2, has_side_effects=True, vmem_limit_bytes=60 * 2**20
        ),
    )(*[getattr(arrays, name) for name in any_names + vmem_names])
    return types.SimpleNamespace(**dict(zip(outs, results)))


def swap_blk(value):
    return lax.ppermute(value, BLK, [(0, 1), (1, 0)])


def local(
    clip_tokens,
    text_tokens,
    text_lengths,
    positions,
    time_embed,
    modulation,
    gains,
    biases,
    self_qkv,
    self_out,
    cross_qkv,
    cross_out,
    ffn_in,
    ffn_out,
    ffn_bias,
    cotangent,
):
    n_sp = lax.axis_size(SP)
    n_dp = lax.axis_size(DP)
    spot_dp = lax.axis_index(DP)
    spot_b = lax.axis_index(BLK)
    spot_s = lax.axis_index(SP)
    core = spot_dp % 2
    pair = (spot_dp // 2) % 2
    x_own = clip_tokens[0]
    tok_rows, width = x_own.shape
    heads_here = H // n_sp
    cols_here = heads_here * HD
    shard_rows = self_qkv.shape[0]
    scale = HD ** (-0.5)

    small_rows = jnp.concatenate([modulation, gains, biases], 0)
    lanes_here = small_rows.shape[1]
    small_own = jnp.concatenate(
        [
            jnp.pad(
                positions[0].astype(BF), ((0, 13), (0, SMALL_LANES - positions.shape[2]))
            ),
            jnp.pad(small_rows, ((0, 0), (0, SMALL_LANES - lanes_here))),
            jnp.pad(
                ffn_bias, (0, (PARAM_ROWS - 21) * SMALL_LANES - ffn_bias.shape[0])
            ).reshape(-1, SMALL_LANES),
        ],
        0,
    )
    (
        params,
        h1_all,
        qkv_mine,
        lin_parts,
        rho,
        trig,
        q_flat,
        kv_flat,
        lse_wide,
        att_all,
        att_tok,
        rest_all,
        in_other,
        out_other,
        text_every,
        cot_every,
        small_every,
    ) = front(
        x_own,
        small_own,
        self_qkv,
        jnp.concatenate([self_out, cross_out, cross_qkv], 1),
        ffn_in,
        ffn_out,
        text_tokens[0],
        cotangent[0],
        time_embed[0],
    )
    mods = time_embed[0] + params[:6]
    gain_all = params[6:11]
    bias_all = params[11:21]
    ff_here = ffn_in.shape[0]
    bias_rows = small_every.reshape(2, n_sp, SMALL_ROWS, SMALL_LANES)
    bias_rows = lax.dynamic_index_in_dim(bias_rows, spot_s, 1, keepdims=False)[:, 37:]
    bias_rows = bias_rows.reshape(2, -1)[:, :ff_here].astype(F32)
    bias_ff = jnp.where(
        spot_b == 0,
        jnp.concatenate([bias_rows[0], bias_rows[1]]),
        jnp.concatenate([bias_rows[1], bias_rows[0]]),
    )

    own = own_tokens(
        text_lengths, rest_all, x_own, att_tok, text_every, time_embed[0], params
    )
    ffn_rows = own.h2
    x_two = own.two

    fed = feed(**dict(
            in_own=ffn_in,
            in_other=in_other,
            out_own=ffn_out,
            out_other=out_other,
            h2=ffn_rows,
            cot=cot_every,
            bias=bias_ff[None],
            time=time_embed[0],
            par=params,
        )
    )
    d_rows = fed.d_rows
    du_sums = fed.du_sums[0]
    z_lin = (
        lax.psum_scatter(fed.z_out, SP, scatter_dimension=0, tiled=False).astype(F32)
        + bias_all[9]
    )
    grad_y = cotangent[0].astype(F32)
    result = x_two + mods[5] * z_lin
    block_out = result.astype(BF)[None]
    d_gate2 = jnp.sum(grad_y * z_lin, 0)
    last = own_back(**dict(
            len=text_lengths,
            rest=rest_all,
            x_two=x_two,
            x_one=own.one,
            d_rows=d_rows,
            cot=cotangent[0],
            time=time_embed[0],
            par=params,
            a=own.a,
            cin=own.cin,
            ql=own.ql,
            kl=own.kl,
            q=own.q,
            kv=own.kv,
            lse=own.lse,
            oc=own.oc,
            att=att_tok,
            text_in=text_every,
        )
    )

    ff_total = ff_here * 2 * n_sp
    ff_row = jnp.zeros((-(-ff_total // width) * width,), F32)
    own_at = (spot_b * n_sp + spot_s) * ff_here
    far_at = ((1 - spot_b) * n_sp + spot_s) * ff_here
    ff_row = lax.dynamic_update_slice_in_dim(ff_row, du_sums[:ff_here], own_at, 0)
    ff_row = lax.dynamic_update_slice_in_dim(ff_row, du_sums[ff_here:], far_at, 0)
    def quarters(grad):
        return grad.reshape(2 * n_sp, 2, 2, shard_rows // 4, grad.shape[1])

    def chunks(grad):
        return grad.reshape(5, ff_here // 10, width)

    ended = back(**dict(
            ckv=quarters(last.ckv),
            cq=quarters(last.cq),
            co=quarters(last.co),
            o=quarters(last.o),
            fi=chunks(fed.fi_own),
            fo=chunks(fed.fo_own),
            fi_rx=chunks(swap_blk(fed.fi_far)),
            fo_rx1=swap_blk(fed.fo_far[: ff_here // 5]).reshape(2, -1, width),
            fo_far=chunks(fed.fo_far),
            d_att=last.d_att,
            text=last.text_part.reshape(2, n_sp, -1, width),
            q=q_flat,
            kv=kv_flat,
            lse=lse_wide,
            w=qkv_mine,
            h1=h1_all,
            lin=lin_parts,
            rho=rho,
            trig=trig,
            par=params,
            x=x_own,
            dx1=last.dx,
            time=time_embed[0],
            small_in=last.sums,
            gate2=d_gate2[None],
            hidden_rows=ff_row.reshape(-1, width),
        )
    )
    small = ended.small_out
    spot = spot_b * n_sp + spot_s
    small_own = lax.dynamic_slice_in_dim(small[:21], spot * lanes_here, lanes_here, 1)
    part_bias = lax.dynamic_slice_in_dim(small[21:].reshape(-1), own_at, ff_here, 0)

    def whole(name, rows):
        return getattr(ended, name + "_out").reshape(rows, -1).astype(F32)

    return (
        block_out,
        ended.tokens_out[None],
        ended.text_out,
        small_own[:6],
        small_own[6:11],
        small_own[11:21],
        whole("s", shard_rows),
        whole("o", shard_rows),
        jnp.concatenate(
            [
                whole("cq", shard_rows),
                whole("ckv", shard_rows),
            ],
            1,
        ),
        whole("co", shard_rows),
        whole("fi", ff_here),
        whole("fo", ff_here),
        part_bias,
    )


def solution(mesh):
    return jax.shard_map(
        local,
        mesh=mesh,
        in_specs=(
            P(DP, (BLK, SP), None),
            P(DP, (BLK, SP), None),
            P(DP),
            P(DP, None, (BLK, SP)),
            P(DP, None, None),
            P(None, (BLK, SP)),
            P(None, (BLK, SP)),
            P(None, (BLK, SP)),
            P((BLK, SP), None),
            P((BLK, SP), None),
            P((BLK, SP), None),
            P((BLK, SP), None),
            P((BLK, SP), None),
            P((BLK, SP), None),
            P((BLK, SP)),
            P(DP, (BLK, SP), None),
        ),
        out_specs=(
            P(DP, (BLK, SP), None),
            P(DP, (BLK, SP), None),
            P(DP, (BLK, SP), None),
            P(None, (BLK, SP)),
            P(None, (BLK, SP)),
            P(None, (BLK, SP)),
            P((BLK, SP), None),
            P((BLK, SP), None),
            P((BLK, SP), None),
            P((BLK, SP), None),
            P((BLK, SP), None),
            P((BLK, SP), None),
            P((BLK, SP)),
        ),
        check_vma=False,
    )
```
